512 devices in a mesh: dp: 4 (over x), tm: 32 (over z, y_hi), tensor: 4 (over y_lo, core).
Axes of the slice: x: 4, y: 8 (y_hi: 4, y_lo: 2; y = y_hi * 2 + y_lo), z: 8, core: 2. Of those that a mesh axis runs over, the one named last changes fastest.
Arguments:
- acts: bfloat16 [4, 32, 512, 1024], P('dp', 'tm', None, 'tensor'), may hold values from -6 to 6
- grad_in: bfloat16 [4, 32, 512, 1024], P('dp', 'tm', None, 'tensor'), may hold values from -6 to 6
- gain: float32 [1024], replicated, may hold values from 0.1 to 1.9
- w_qkv: bfloat16 [1024, 3, 1024], P(None, None, 'tensor'), may hold values from -0.1875 to 0.1875
- w_out: bfloat16 [1024, 1024], P('tensor'), may hold values from -0.1875 to 0.1875
Outputs:
- grad_acts: bfloat16 [4, 32, 512, 1024], P('dp', 'tm', None, 'tensor')
- grad_w_qkv: float32 [1024, 3, 1024], P(('dp', 'tm'), None, 'tensor')
- grad_w_out_t: float32 [1024, 1024], P(('dp', 'tm'), 'tensor')
- grad_gain: float32 [1024], P('tensor')
The draws below stay inside these ranges and needn't reach their ends.
All inputs are finite; a program needn't handle non-finite values.
Results may differ from the reference program's by a relative error of at most 0.018.
Values may be sent and summed in bfloat16 or wider, within the bound.
No kernel may reach another device: no remote copies, remote signals or barrier semaphores. Data moves between devices by JAX's collectives and lax.ppermute only.
A program may use at most 64 MiB of HBM per device.

```python
import jax
import jax.numpy as jnp
from jax import lax

D = 1024
HD = 64
HEADS_DEV = 4
HC = 1024
PATCH = 512
FRAMES = 32
CLIPS = 4
TOKENS = 65536


def steps_of(key, shape, split, low, high):
    def one(position, blocks):
        steps = jax.random.uniform(jax.random.fold_in(jax.random.fold_in(key, 6), position), (blocks,), jnp.float32, low / len(split), high / len(split))
        return jnp.repeat(jnp.exp(steps), shape[position] // blocks).reshape((-1,) + (1,) * (len(shape) - position - 1))

    factor_of = one(*split[0])
    for cut in split[1:]:
        factor_of = factor_of * one(*cut)
    return factor_of


def bell_draw(key, extent, deviation, reach, cuts=(), kind=jnp.bfloat16):
    values = jax.random.normal(key, extent, jnp.float32) * deviation
    if len(cuts) > 0:
        values = steps_of(key, extent, cuts, -0.22, 0.18) * values
    return jnp.clip(values, min=-reach, max=reach).astype(kind)


def setup_inputs(seed: int = 0) -> dict:
    arg_keys = jax.random.split(jax.random.key(seed), 6)
    return {
        "acts": bell_draw(arg_keys[0], (CLIPS, FRAMES, PATCH, D), 1.0, 6.0, ((0, 4), (1, 32), (3, 4))),
        "grad_in": bell_draw(arg_keys[1], (CLIPS, FRAMES, PATCH, D), 1.0, 6.0, ((0, 4), (1, 32), (3, 4))),
        "gain": jnp.clip(1.0 + 0.18 * jax.random.normal(arg_keys[2], (D,), jnp.float32), 0.1, 1.9),
        "w_qkv": bell_draw(arg_keys[3], (D, 3, HC), D ** -0.5, 0.1875, ((2, 4),)),
        "w_out": bell_draw(arg_keys[4], (HC, D), HC ** -0.5, 0.1875, ((0, 4),)),
    }


EPS = 1e-05

def clip_grads(x, dy, gain, w_qkv, w_out):
    frames, patches, width = x.shape
    rows = frames * patches
    cols = w_qkv.shape[2]
    heads = cols // HD
    scale = HD ** (-0.5)
    flat_x = x.reshape(rows, width).astype(jnp.float32)
    centered_input = flat_x - lax.optimization_barrier(jnp.mean(flat_x, axis=-1, keepdims=True))
    inverse_deviation = lax.rsqrt(lax.optimization_barrier(jnp.mean(centered_input * centered_input, axis=-1, keepdims=True)) + EPS)
    standardized_input = centered_input * inverse_deviation
    normalized_rows = (standardized_input * gain).astype(jnp.bfloat16)
    qkv = jnp.dot(normalized_rows, w_qkv.reshape(width, 3 * cols), preferred_element_type=jnp.float32).astype(jnp.bfloat16)
    flattened_gradient = dy.reshape(rows, width)
    out_grads = lax.dot_general(flattened_gradient, w_out, (((1,), (1,)), ((), ())), preferred_element_type=jnp.float32).astype(jnp.bfloat16)
    queries = qkv[:, :cols].reshape(frames, patches, heads, HD).astype(jnp.float32)
    key_rows = qkv[:, cols:2 * cols].reshape(frames, patches, heads, HD).astype(jnp.float32)
    value_rows = qkv[:, 2 * cols:].reshape(frames, patches, heads, HD).astype(jnp.float32)
    grads_f = out_grads.reshape(frames, patches, heads, HD).astype(jnp.float32)
    scores = jnp.einsum('ipnd,jpnd->pnij', queries, key_rows) * scale
    expd = jnp.exp(scores)
    prob = expd / lax.optimization_barrier(jnp.sum(expd, axis=-1, keepdims=True))
    prob_low = prob.astype(jnp.bfloat16).astype(jnp.float32)
    attn_exact = jnp.einsum('pnij,jpnd->ipnd', prob_low, value_rows)
    attn = attn_exact.astype(jnp.bfloat16)
    delta = jnp.einsum('ipnd,ipnd->pni', grads_f, attn_exact)
    dprob = jnp.einsum('ipnd,jpnd->pnij', grads_f, value_rows)
    dscore = (prob * (dprob - delta[..., None]) * scale).astype(jnp.bfloat16).astype(jnp.float32)
    grad_q = jnp.einsum('pnij,jpnd->ipnd', dscore, key_rows).astype(jnp.bfloat16).reshape(rows, cols)
    grad_k = jnp.einsum('pnij,ipnd->jpnd', dscore, queries).astype(jnp.bfloat16).reshape(rows, cols)
    grad_v = jnp.einsum('pnij,ipnd->jpnd', prob_low, grads_f).astype(jnp.bfloat16).reshape(rows, cols)
    grad_qkv = jnp.stack([grad_q, grad_k, grad_v], axis=1)
    out_term = lax.dot_general(flattened_gradient, attn.reshape(rows, cols), (((0,), (0,)), ((), ())), preferred_element_type=jnp.float32)
    qkv_term = lax.dot_general(normalized_rows, grad_qkv.reshape(rows, 3 * cols), (((0,), (0,)), ((), ())), preferred_element_type=jnp.float32).reshape(width, 3, cols)
    group = HEADS_DEV * HD
    normalized_gradient = jnp.zeros((rows, width), jnp.float32)
    for index in range(cols // group):
        piece = grad_qkv[:, :, index * group:(index + 1) * group].reshape(rows, 3 * group)
        weight = w_qkv[:, :, index * group:(index + 1) * group].reshape(width, 3 * group)
        term = lax.dot_general(piece, weight, (((1,), (1,)), ((), ())), preferred_element_type=jnp.float32)
        normalized_gradient = normalized_gradient + lax.optimization_barrier(term.astype(jnp.bfloat16)).astype(jnp.float32)
    gain_product = lax.optimization_barrier(jnp.sum(normalized_gradient * standardized_input, axis=0))
    scaled_gradient = normalized_gradient * gain
    first_moment = lax.optimization_barrier(jnp.mean(scaled_gradient, axis=-1, keepdims=True))
    second_moment = lax.optimization_barrier(jnp.mean(scaled_gradient * standardized_input, axis=-1, keepdims=True))
    input_gradient = flattened_gradient.astype(jnp.float32) + inverse_deviation * (scaled_gradient - first_moment - standardized_input * second_moment)
    return (input_gradient.astype(jnp.bfloat16).reshape(frames, patches, width), qkv_term, out_term, gain_product)

def reference(acts, grad_in, gain, w_qkv, w_out):

    def one_clip(pair):
        return clip_grads(pair[0], pair[1], gain, w_qkv, w_out)
    grad_acts, qkv_terms, out_terms, gain_terms = lax.map(one_clip, (acts, grad_in))
    layer_norm_fn = TOKENS ** (-0.5)
    return (grad_acts, lax.optimization_barrier(jnp.sum(qkv_terms, axis=0)) * layer_norm_fn, lax.optimization_barrier(jnp.sum(out_terms, axis=0)) * layer_norm_fn, lax.optimization_barrier(jnp.sum(gain_terms, axis=0)) * layer_norm_fn)
```

```python
import jax
import jax.numpy as jnp
from jax import lax
from jax.sharding import PartitionSpec as P

HD = 64
EPS = 1e-05
CORE = [(0, 1), (1, 0), (2, 3), (3, 2)]
CHIP = [(0, 2), (2, 0), (1, 3), (3, 1)]


def gather_pieces(own):
    far = lax.ppermute(own, "tensor", CHIP)
    near = lax.ppermute(own, "tensor", CORE)
    cross = lax.ppermute(far, "tensor", CORE)
    return [own, near, far, cross]


def per_device(acts, grad_in, gain, w_qkv, w_out):
    t = lax.axis_index("tensor")
    dp, tm = lax.axis_size("dp"), lax.axis_size("tm")
    part = acts.shape[3]
    rows = acts.shape[2]
    few = rows // tm
    width = w_qkv.shape[0]
    cols = w_qkv.shape[2]
    heads = cols // HD
    scale = HD ** (-0.5)
    bf = jnp.bfloat16

    def to_patches(a):
        a = a.reshape(tm, few, part)
        return lax.all_to_all(a, "tm", split_axis=0, concat_axis=0, tiled=True).reshape(rows, part)

    def chunk(a, k, axis):
        return lax.dynamic_slice_in_dim(a, (t ^ k) * part, part, axis)

    def relative(a, axis):
        return jnp.concatenate([chunk(a, k, axis) for k in range(4)], axis=axis)

    x_pieces = gather_pieces(to_patches(acts))
    dy_pieces = gather_pieces(to_patches(grad_in))
    gain_rel = relative(gain, 0)
    w_rel = relative(w_qkv.reshape(width, 3 * cols), 0)
    w_out_rel = relative(w_out, 1)

    x = jnp.concatenate(x_pieces, axis=1).astype(jnp.float32)
    dy = jnp.concatenate(dy_pieces, axis=1)
    centered = x - jnp.mean(x, axis=-1, keepdims=True)
    inv = lax.rsqrt(jnp.mean(centered * centered, axis=-1, keepdims=True) + EPS)
    xhat = centered * inv
    normed = (xhat * gain_rel).astype(bf)
    qkv = jnp.dot(normed, w_rel, preferred_element_type=jnp.float32).astype(bf)
    out_grads = lax.dot_general(
        dy, w_out_rel, (((1,), (1,)), ((), ())), preferred_element_type=jnp.float32
    ).astype(bf)

    def heads_of(a):
        return a.reshape(tm, few, heads, HD)

    q, k, v = [heads_of(qkv[:, i * cols : (i + 1) * cols]) for i in range(3)]
    g = heads_of(out_grads)
    scores = jnp.einsum("ipnd,jpnd->pnij", q, k, preferred_element_type=jnp.float32) * scale
    expd = jnp.exp(scores)
    prob = expd / jnp.sum(expd, axis=-1, keepdims=True)
    low = prob.astype(bf)
    exact = jnp.einsum("pnij,jpnd->ipnd", low, v, preferred_element_type=jnp.float32)
    attn = exact.astype(bf).reshape(rows, cols)
    delta = jnp.einsum("ipnd,ipnd->pni", g.astype(jnp.float32), exact)
    dprob = jnp.einsum("ipnd,jpnd->pnij", g, v, preferred_element_type=jnp.float32)
    dscore = (prob * (dprob - delta[..., None]) * scale).astype(bf)
    gq = jnp.einsum("pnij,jpnd->ipnd", dscore, k, preferred_element_type=jnp.float32)
    gk = jnp.einsum("pnij,ipnd->jpnd", dscore, q, preferred_element_type=jnp.float32)
    gv = jnp.einsum("pnij,ipnd->jpnd", low, g, preferred_element_type=jnp.float32)
    gqkv = jnp.concatenate([a.astype(bf).reshape(rows, cols) for a in (gq, gk, gv)], axis=1)

    norm = (rows * dp * tm) ** (-0.5)
    tok = (((0,), (0,)), ((), ()))
    dw_rel = [
        jnp.concatenate(
            [
                lax.dot_general(
                    normed[:, i * part : (i + 1) * part],
                    gqkv,
                    tok,
                    preferred_element_type=jnp.float32,
                ),
                lax.dot_general(dy_pieces[i], attn, tok, preferred_element_type=jnp.float32),
            ],
            axis=1,
        )
        for i in range(4)
    ]
    dw = jnp.zeros((width, 4 * cols), bf)
    for i in range(4):
        dw = lax.dynamic_update_slice_in_dim(dw, (dw_rel[i] * norm).astype(bf), (t ^ i) * part, 0)
    dw = dw.reshape(dp, width // dp, 4 * cols)
    dw = lax.all_to_all(dw, "dp", split_axis=0, concat_axis=0, tiled=True)
    dw = jnp.sum(dw.astype(jnp.float32), axis=0).astype(bf)

    term = lax.dot_general(
        gqkv, w_rel, (((1,), (1,)), ((), ())), preferred_element_type=jnp.float32
    ).astype(bf)
    wide = term.astype(jnp.float32)
    scaled = wide * gain_rel
    moments = jnp.stack([jnp.mean(scaled, axis=-1), jnp.mean(scaled * xhat, axis=-1)])
    gain_part = jnp.sum(wide * xhat, axis=0) * norm
    moments = moments.reshape(-1, part)
    high = moments.astype(bf)
    side = jnp.concatenate([high, (moments - high.astype(jnp.float32)).astype(bf)])
    packs = []
    for i in range(4):
        mine = gain_part[i * part : (i + 1) * part].reshape(1, part)
        high = mine.astype(bf)
        rest = jnp.zeros((16 - side.shape[0] - 2, part), bf)
        packs.append(
            jnp.concatenate(
                [
                    term[:, i * part : (i + 1) * part],
                    side,
                    high,
                    (mine - high.astype(jnp.float32)).astype(bf),
                    rest,
                ]
            )
        )
    got = lax.ppermute(jnp.stack([packs[1], packs[3]]), "tensor", CORE)
    near = packs[0].astype(jnp.float32) + got[0].astype(jnp.float32)
    far = (packs[2].astype(jnp.float32) + got[1].astype(jnp.float32)).astype(bf)
    total = near + lax.ppermute(far, "tensor", CHIP).astype(jnp.float32)
    gn = total[:rows]
    n = side.shape[0] // 2
    moments = (total[rows : rows + n] + total[rows + n : rows + 2 * n]).reshape(2, rows, 1)
    gain_sum = total[rows + 2 * n] + total[rows + 2 * n + 1]
    out = dy_pieces[0].astype(jnp.float32) + inv * (
        gn * gain_rel[:part] - moments[0] - xhat[:, :part] * moments[1]
    )
    out = lax.all_to_all(
        out.astype(bf).reshape(tm, few, part), "tm", split_axis=0, concat_axis=0, tiled=True
    )

    gain_sum = lax.psum(gain_sum, "dp")
    high = gain_sum.astype(bf)
    low = (gain_sum - high.astype(jnp.float32)).astype(bf)
    ride = jnp.concatenate([high, low] * 2).reshape(1, 1, 4 * cols)
    dw = jnp.concatenate(
        [dw.reshape(tm, width // (dp * tm), 4 * cols), jnp.broadcast_to(ride, (tm, 1, 4 * cols))],
        axis=1,
    )
    dw = lax.all_to_all(dw, "tm", split_axis=0, concat_axis=0, tiled=True)
    dw = jnp.sum(dw.astype(jnp.float32), axis=0)
    share = width // (dp * tm)
    grad_gain = dw[share, :part] + dw[share, part : 2 * part]
    return (
        out.reshape(grad_in.shape),
        dw[:share, : 3 * cols].reshape(share, 3, cols),
        dw[:share, 3 * cols :],
        grad_gain,
    )


def solution(mesh):
    placed = (
        P("dp", "tm", None, "tensor"),
        P("dp", "tm", None, "tensor"),
        P(),
        P(None, None, "tensor"),
        P("tensor", None),
    )
    return jax.shard_map(
        per_device,
        mesh=mesh,
        in_specs=placed,
        out_specs=(
            P("dp", "tm", None, "tensor"),
            P(("dp", "tm"), None, "tensor"),
            P(("dp", "tm"), "tensor"),
            P("tensor"),
        ),
        check_vma=False,
    )
```

```python
import functools

import jax
import jax.numpy as jnp
from jax import lax
from jax.experimental import pallas as pl
from jax.experimental.pallas import tpu as pltpu
from jax.sharding import PartitionSpec as P

HD = 64
EPS = 1e-05
CORE = [(0, 1), (1, 0), (2, 3), (3, 2)]
CHIP = [(0, 2), (2, 0), (1, 3), (3, 1)]
EVEN = [(0, 1), (1, 0), (2, 3), (3, 2)]
ODD = [(0, 3), (3, 0), (1, 2), (2, 1)]
F32, BF = jnp.float32, jnp.bfloat16
SIDE = 32


def dot(a, b, contract):
    return lax.dot_general(a, b, (contract, ((), ())), preferred_element_type=F32)


def grouped(a):
    frames, few, part = a.shape
    a = a.astype(F32).reshape(frames, few // 8, 8, part)
    return jnp.concatenate([a[:, i].reshape(frames * 8, part) for i in range(few // 8)])


def attention(q, k, v, g, heads, scale):
    rows, cols = q.shape
    same = (
        lax.broadcasted_iota(jnp.int32, (rows, rows), 0) % 8
        == lax.broadcasted_iota(jnp.int32, (rows, rows), 1) % 8
    )
    lane = lax.broadcasted_iota(jnp.int32, (rows, cols), 1) // HD
    zero = jnp.zeros((rows, cols), BF)
    sums = [jnp.zeros((rows, cols), F32) for _ in range(4)]
    for h in range(heads):
        qh, kh, vh, gh = [jnp.where(lane == h, a, zero) for a in (q, k, v, g)]
        scores = dot(q, kh, ((1,), (1,))) * scale
        expd = jnp.exp(jnp.where(same, scores, -1e30))
        prob = expd / jnp.sum(expd, axis=-1, keepdims=True)
        low = prob.astype(BF)
        dprob = dot(g, vh, ((1,), (1,)))
        delta = jnp.sum(low.astype(F32) * dprob, axis=-1, keepdims=True)
        ds = (prob * (dprob - delta) * scale).astype(BF)
        sums[0] += dot(low, vh, ((1,), (0,)))
        sums[1] += dot(ds, kh, ((1,), (0,)))
        sums[2] += dot(ds, qh, ((0,), (0,)))
        sums[3] += dot(low, gh, ((0,), (0,)))
    return [a.astype(BF) for a in sums]


def split(a):
    high = a.astype(BF).astype(F32)
    return high, a - high


def main_kernel(
    heads, norm, idx, own, near, far, cross, gain, w, w_out,
    a_send, a_keep, b_send, b_keep, send, keep, gains, xhat_out, inv_out,
    gqkv, xhat, normed, dy, attn,
):
    t, d = idx[0], idx[1]
    rows, part = normed.shape[1:]
    width = 4 * part
    pieces = (own, near, far, cross)
    x = [grouped(a[:, 0]) for a in pieces]
    mean = sum(jnp.sum(a, axis=-1, keepdims=True) for a in x) / width
    x = [a - mean for a in x]
    inv = lax.rsqrt(sum(jnp.sum(a * a, axis=-1, keepdims=True) for a in x) / width + EPS)
    inv_out[...] = jnp.broadcast_to(inv, inv_out.shape)
    xhat_out[...] = x[0] * inv
    for i in range(4):
        xhat[i] = x[i] * inv
        normed[i] = (xhat[i] * gain[t ^ i]).astype(BF)
        dy[i] = grouped(pieces[i][:, 1]).astype(BF)
    qkv = [
        sum(dot(normed[i], w[s, t ^ i], ((1,), (0,))) for i in range(4)).astype(BF)
        for s in range(3)
    ]
    g = sum(
        dot(dy[i], w_out[:, pl.ds(pl.multiple_of((t ^ i) * part, part), part)], ((1,), (1,)))
        for i in range(4)
    ).astype(BF)
    half = rows // 2
    for i in range(2):
        span = slice(i * half, (i + 1) * half)
        parts = attention(*(a[span] for a in qkv), g[span], heads, HD ** (-0.5))
        attn[span] = parts[0]
        for s in range(3):
            gqkv[s, span] = parts[1 + s]
    cols = w.shape[3]
    a_at = (a_keep.at[0], a_send.at[0], a_send.at[1], a_keep.at[1])
    b_at = (b_keep.at[0], b_keep.at[1], b_send.at[1], b_send.at[0])
    for r in range(4):
        left = normed[d ^ r ^ t]
        for s, (ref, at) in enumerate(((a_at[r], 0), (a_at[r], cols), (b_at[r], 0))):
            block = dot(left, gqkv[s], ((0,), (0,))) * norm
            ref[:, at : at + cols] = block.astype(BF)
        block = dot(dy[d ^ r ^ t], attn[...], ((0,), (0,))) * norm
        b_at[r][:, cols:] = block.astype(BF)
    first = jnp.zeros((rows, 1), F32)
    second = jnp.zeros((rows, 1), F32)
    outs = (keep.at[0], send.at[0], keep.at[1], send.at[1])
    line = lax.broadcasted_iota(jnp.int32, (8, 128), 0)
    for i in range(4):
        term = sum(dot(gqkv[s], w[s, t ^ i], ((1,), (1,))) for s in range(3)).astype(BF)
        outs[i][:rows] = term
        wide = term.astype(F32)
        product = wide * xhat[i]
        partial = jnp.sum(product, axis=0, keepdims=True) * norm
        partial = jnp.where(line == 0, partial[:, :128], partial[:, 128:])
        for j in range(gains.shape[0]):
            gains[j, t ^ i] = partial
        first += jnp.sum(wide * gain[t ^ i], axis=-1, keepdims=True)
        second += jnp.sum(product * gain[t ^ i], axis=-1, keepdims=True)
    lane = lax.broadcasted_iota(jnp.int32, (rows, 128), 1)
    moments = jnp.where(lane == 0, first, jnp.where(lane == 1, second, 0.0)) / width
    moments = moments.T[:8]
    high, low = split(moments)
    side = [high[:, :part], high[:, part:], low[:, :part], low[:, part:]]
    side = jnp.concatenate(side).astype(BF)
    for ref in outs:
        ref[rows:] = side


def pack_kernel(
    idx, keep, got, last, xhat, inv, own, gain, ride,
    a_keep, a_got, a_last, b_keep, b_got, b_last, out,
):
    t = idx[0]
    rows, part = xhat.shape
    frames = own.shape[0]
    at = 0
    for kept, came, end in ((a_keep, a_got, a_last), (b_keep, b_got, b_last)):
        block = kept[0].astype(F32) + came[0].astype(F32) + end[...].astype(F32)
        cols = block.shape[1]
        out[:, :, at : at + cols] = block.reshape(frames, 8, cols).astype(BF)
        at += cols
    total = keep[0].astype(F32) + got[0].astype(F32) + last[...].astype(F32)
    side = total[rows:]
    moments = jnp.concatenate([side[:8] + side[16:24], side[8:16] + side[24:]], axis=1)
    moments = jnp.concatenate([moments, jnp.zeros((120, rows), F32)]).T
    grad = grouped(own[:, 1]) + inv[:, :1] * (
        total[:rows] * gain[t] - moments[:, :1] - xhat[...] * moments[:, 1:2]
    )
    for i in range(0, rows, frames * 8):
        block = grad[i : i + frames * 8].reshape(frames, 8, part)
        out[:, :, at : at + part] = block.astype(BF)
        at += part
    out[:, :, at:] = jnp.broadcast_to(ride[...][None], (frames, 8, 128)).astype(BF)


def last_kernel(came, out, dw, dw_out, gain):
    frames = came.shape[0]
    part = out.shape[1]
    for s in range(3):
        dw[s] = jnp.sum(came[:, :, s * part : (s + 1) * part].astype(F32), axis=0)
    dw_out[...] = jnp.sum(came[:, :, 3 * part : 4 * part].astype(F32), axis=0)
    grad = [came[:, :, i * part : (i + 1) * part].astype(F32) for i in (4, 5)]
    out[...] = jnp.concatenate(grad, axis=1).reshape(out.shape).astype(BF)
    ride = jnp.sum(came[:, :, 6 * part :].astype(F32), axis=0)
    gain[...] = jnp.concatenate([ride[0:1] + ride[2:3], ride[1:2] + ride[3:4]], axis=1)


def call(kernel, args, outs, scratch=(), flops=0):
    vmem = pl.BlockSpec(memory_space=pltpu.VMEM)
    first = [pl.BlockSpec(memory_space=pltpu.SMEM)] if args[0].dtype == jnp.int32 else [vmem]
    shapes = [jax.ShapeDtypeStruct(s, d) for s, d in outs]
    moved = sum(a.size * a.dtype.itemsize for a in list(args) + shapes)
    return pl.pallas_call(
        kernel,
        out_shape=shapes,
        in_specs=first + [vmem] * (len(args) - 1),
        out_specs=[vmem] * len(shapes),
        scratch_shapes=list(scratch),
        compiler_params=pltpu.CompilerParams(vmem_limit_bytes=48 * 2**20),
        cost_estimate=pl.CostEstimate(flops=flops, bytes_accessed=moved, transcendentals=0),
    )(*args)


def mid_kernel(keep, got, a_keep, a_got, b_keep, b_got, gains, mid, a_mid, b_mid, ride):
    for kept, came, out in ((keep, got, mid), (a_keep, a_got, a_mid), (b_keep, b_got, b_mid)):
        out[...] = (kept[...].astype(F32) + came[...].astype(F32)).astype(BF)
    high, low = split(jnp.sum(gains[...], axis=0))
    line = lax.broadcasted_iota(jnp.int32, (8, 128), 0)
    low = jnp.concatenate([low[0:2], low[0:6]])
    ride[...] = jnp.where(line < 2, high, low)


def middle(pairs, gains):
    args = [a for pair in pairs for a in pair]
    shapes = [jax.ShapeDtypeStruct(pair[0].shape[1:], BF) for pair in pairs]
    shapes.append(jax.ShapeDtypeStruct(gains.shape[1:], F32))

    def second(a):
        return pl.BlockSpec((None,) + a.shape[1:], lambda i: (1, 0, 0))

    return pl.pallas_call(
        mid_kernel,
        grid=(1,),
        out_shape=shapes,
        in_specs=[second(a) for a in args] + [pl.BlockSpec(gains.shape, lambda i: (0, 0, 0))],
        out_specs=[pl.BlockSpec(a.shape, lambda i: (0, 0)) for a in shapes],
        compiler_params=pltpu.CompilerParams(vmem_limit_bytes=32 * 2**20),
        cost_estimate=pl.CostEstimate(flops=1000, bytes_accessed=1000, transcendentals=0),
    )(*args, gains)


def per_device(acts, grad_in, gain, w_qkv, w_out):
    t = lax.axis_index("tensor")
    dp, tm = lax.axis_size("dp"), lax.axis_size("tm")
    part = acts.shape[3]
    rows = acts.shape[2]
    few = rows // tm
    width = w_qkv.shape[0]
    cols = w_qkv.shape[2]
    heads = cols // HD
    norm = (rows * dp * tm) ** (-0.5)
    idx = jnp.stack([t, lax.axis_index("dp")]).astype(jnp.int32)

    own = jnp.stack([acts.reshape(tm, few, part), grad_in.reshape(tm, few, part)], axis=1)
    own = lax.all_to_all(own, "tm", split_axis=0, concat_axis=0, tiled=True)
    far = lax.ppermute(own, "tensor", CHIP)
    near = lax.ppermute(own, "tensor", CORE)
    cross = lax.ppermute(far, "tensor", CORE)

    gain_rows = gain.reshape(4, 1, part)
    w = jnp.transpose(w_qkv, (1, 0, 2)).reshape(3, 4, part, cols)
    half = ((2, part, 2 * cols), BF)
    message = ((2, rows + SIDE, part), BF)
    a_send, a_keep, b_send, b_keep, send, keep, gains, xhat, inv = call(
        functools.partial(main_kernel, heads, norm),
        (idx, own, near, far, cross, gain_rows, w, w_out),
        (
            half,
            half,
            half,
            half,
            message,
            message,
            ((dp, 4, 8, 128), F32),
            ((rows, part), F32),
            ((rows, 128), F32),
        ),
        (
            pltpu.VMEM((3, rows, cols), BF),
            pltpu.VMEM((4, rows, part), F32),
            pltpu.VMEM((4, rows, part), BF),
            pltpu.VMEM((4, rows, part), BF),
            pltpu.VMEM((rows, cols), BF),
        ),
        flops=7 * 10**9,
    )

    a_got = lax.ppermute(a_send, "dp", EVEN)
    b_got = lax.ppermute(b_send, "dp", ODD)

    gains = lax.all_to_all(
        gains.reshape(dp * 4, 8, 128), ("dp", "tensor"), split_axis=0, concat_axis=0, tiled=True
    )
    got = lax.ppermute(send, "tensor", CORE)
    mid, a_mid, b_mid, ride = middle(((keep, got), (a_keep, a_got), (b_keep, b_got)), gains)
    last = lax.ppermute(mid, "tensor", CHIP)
    a_last = lax.ppermute(a_mid, "dp", ODD)
    b_last = lax.ppermute(b_mid, "dp", EVEN)

    share = width // (dp * tm)
    (pack,) = call(
        pack_kernel,
        (
            idx, keep, got, last, xhat, inv, own, gain_rows, ride,
            a_keep, a_got, a_last, b_keep, b_got, b_last,
        ),
        (((tm, share, 4 * cols + 2 * part + 128), BF),),
        flops=10**7,
    )
    pack = lax.all_to_all(pack, "tm", split_axis=0, concat_axis=0, tiled=True)
    out, dw, dw_out, gain_sum = call(
        last_kernel,
        (pack,),
        (((rows, part), BF), ((3, share, cols), F32), ((share, cols), F32), ((1, part), F32)),
        flops=10**7,
    )
    return (
        out.reshape(grad_in.shape),
        jnp.transpose(dw, (1, 0, 2)),
        dw_out,
        gain_sum.reshape(part),
    )


def solution(mesh):
    placed = (
        P("dp", "tm", None, "tensor"),
        P("dp", "tm", None, "tensor"),
        P(),
        P(None, None, "tensor"),
        P("tensor", None),
    )
    return jax.shard_map(
        per_device,
        mesh=mesh,
        in_specs=placed,
        out_specs=(
            P("dp", "tm", None, "tensor"),
            P(("dp", "tm"), None, "tensor"),
            P(("dp", "tm"), "tensor"),
            P("tensor"),
        ),
        check_vma=False,
    )
```

```python
import functools

import jax
import jax.numpy as jnp
from jax import lax
from jax.experimental import pallas as pl
from jax.experimental.pallas import tpu as pltpu
from jax.sharding import PartitionSpec as P

HD = 64
EPS = 1e-05
CORE = [(0, 1), (1, 0), (2, 3), (3, 2)]
CHIP = [(0, 2), (2, 0), (1, 3), (3, 1)]
F32, BF = jnp.float32, jnp.bfloat16
SIDE = 32


def dot(a, b, contract):
    return lax.dot_general(a, b, (contract, ((), ())), preferred_element_type=F32)


def grouped(a):
    frames, few, part = a.shape
    a = a.astype(F32).reshape(frames, few // 8, 8, part)
    return jnp.concatenate([a[:, i].reshape(frames * 8, part) for i in range(few // 8)])


def attention(q, k, v, g, heads, scale):
    rows, cols = q.shape
    same = (
        lax.broadcasted_iota(jnp.int32, (rows, rows), 0) % 8
        == lax.broadcasted_iota(jnp.int32, (rows, rows), 1) % 8
    )
    lane = lax.broadcasted_iota(jnp.int32, (rows, cols), 1) // HD
    zero = jnp.zeros((rows, cols), BF)
    sums = [jnp.zeros((rows, cols), F32) for _ in range(4)]
    for h in range(heads):
        qh, kh, vh, gh = [jnp.where(lane == h, a, zero) for a in (q, k, v, g)]
        scores = dot(q, kh, ((1,), (1,))) * scale
        expd = jnp.exp(jnp.where(same, scores, -1e30))
        prob = expd / jnp.sum(expd, axis=-1, keepdims=True)
        low = prob.astype(BF)
        dprob = dot(g, vh, ((1,), (1,)))
        delta = jnp.sum(low.astype(F32) * dprob, axis=-1, keepdims=True)
        ds = (prob * (dprob - delta) * scale).astype(BF)
        sums[0] += dot(low, vh, ((1,), (0,)))
        sums[1] += dot(ds, kh, ((1,), (0,)))
        sums[2] += dot(ds, qh, ((0,), (0,)))
        sums[3] += dot(low, gh, ((0,), (0,)))
    return [a.astype(BF) for a in sums]


def split(a):
    high = a.astype(BF).astype(F32)
    return high, a - high


def main_kernel(
    heads, norm, idx, own, near, far, cross, gain, w, w_out,
    dw, send, keep, xhat_out, inv_out,
    gqkv, xhat, normed, dy, attn,
):
    t = idx[0]
    rows, part = normed.shape[1:]
    width = 4 * part
    pieces = (own, near, far, cross)
    x = [grouped(a[:, 0]) for a in pieces]
    mean = sum(jnp.sum(a, axis=-1, keepdims=True) for a in x) / width
    x = [a - mean for a in x]
    inv = lax.rsqrt(sum(jnp.sum(a * a, axis=-1, keepdims=True) for a in x) / width + EPS)
    inv_out[...] = jnp.broadcast_to(inv, inv_out.shape)
    xhat_out[...] = x[0] * inv
    for i in range(4):
        xhat[i] = x[i] * inv
        normed[i] = (xhat[i] * gain[t ^ i]).astype(BF)
        dy[i] = grouped(pieces[i][:, 1]).astype(BF)
    qkv = [
        sum(dot(normed[i], w[s, t ^ i], ((1,), (0,))) for i in range(4)).astype(BF)
        for s in range(3)
    ]
    g = sum(
        dot(dy[i], w_out[:, pl.ds(pl.multiple_of((t ^ i) * part, part), part)], ((1,), (1,)))
        for i in range(4)
    ).astype(BF)
    half = rows // 2
    for i in range(2):
        span = slice(i * half, (i + 1) * half)
        parts = attention(*(a[span] for a in qkv), g[span], heads, HD ** (-0.5))
        attn[span] = parts[0]
        for s in range(3):
            gqkv[s, span] = parts[1 + s]
    cols = w.shape[3]
    for i in range(4):
        for s in range(3):
            block = dot(normed[i], gqkv[s], ((0,), (0,))) * norm
            dw[t ^ i, :, s * cols : (s + 1) * cols] = block.astype(BF)
        block = dot(dy[i], attn[...], ((0,), (0,))) * norm
        dw[t ^ i, :, 3 * cols :] = block.astype(BF)
    first = jnp.zeros((rows, 1), F32)
    second = jnp.zeros((rows, 1), F32)
    outs = (keep.at[0], send.at[0], keep.at[1], send.at[1])
    gains = []
    for i in range(4):
        term = sum(dot(gqkv[s], w[s, t ^ i], ((1,), (1,))) for s in range(3)).astype(BF)
        outs[i][:rows] = term
        wide = term.astype(F32)
        product = wide * xhat[i]
        gains.append(jnp.sum(product, axis=0, keepdims=True) * norm)
        first += jnp.sum(wide * gain[t ^ i], axis=-1, keepdims=True)
        second += jnp.sum(product * gain[t ^ i], axis=-1, keepdims=True)
    lane = lax.broadcasted_iota(jnp.int32, (rows, 128), 1)
    moments = jnp.where(lane == 0, first, jnp.where(lane == 1, second, 0.0)) / width
    moments = moments.T[:8]
    high, low = split(moments)
    line = lax.broadcasted_iota(jnp.int32, (8, part), 0)
    for i in range(4):
        gain_high, gain_low = split(gains[i])
        top = jnp.where(line == 2, gain_high, jnp.where(line == 3, gain_low, high[:, :part]))
        side = [top, high[:, part:], low[:, :part], low[:, part:]]
        outs[i][rows:] = jnp.concatenate(side).astype(BF)


def acts_kernel(idx, keep, got, last, xhat, inv, own, gain, out):
    t = idx[0]
    rows, part = xhat.shape
    frames = own.shape[0]
    total = keep[0].astype(F32) + got[0].astype(F32) + last[...].astype(F32)
    side = total[rows:]
    moments = jnp.concatenate([side[:8] + side[16:24], side[8:16] + side[24:]], axis=1)
    moments = jnp.concatenate([moments, jnp.zeros((120, rows), F32)]).T
    grad = grouped(own[:, 1]) + inv[:, :1] * (
        total[:rows] * gain[t] - moments[:, :1] - xhat[...] * moments[:, 1:2]
    )
    half = frames * 8
    for i in range(2):
        block = grad[i * half : (i + 1) * half].reshape(frames, 8, part)
        out[:, :, i * part : (i + 1) * part] = block.astype(BF)


def pack_kernel(dw, grad, gain, out):
    group, share, cols = out.shape[0], out.shape[1], dw.shape[2]
    block = sum(dw[i].astype(F32) for i in range(dw.shape[0]))
    out[:, :, :cols] = block.reshape(group, share, cols).astype(BF)
    end = cols + grad.shape[2]
    out[:, :, cols:end] = grad[...]
    high, low = split(gain[...])
    ride = jnp.concatenate([high, low, high, low])
    out[:, :, end:] = jnp.broadcast_to(ride[None], (group, share, 128)).astype(BF)


def last_kernel(came, out, dw, dw_out, gain):
    frames = came.shape[0]
    part = out.shape[1]
    for s in range(3):
        dw[s] = jnp.sum(came[:, :, s * part : (s + 1) * part].astype(F32), axis=0)
    dw_out[...] = jnp.sum(came[:, :, 3 * part : 4 * part].astype(F32), axis=0)
    grad = [came[:, :, i * part : (i + 1) * part].astype(F32) for i in (4, 5)]
    out[...] = jnp.concatenate(grad, axis=1).reshape(out.shape).astype(BF)
    ride = jnp.sum(came[:, :, 6 * part :].astype(F32), axis=0)
    gain[...] = ride[0:2] + ride[2:4]


def call(kernel, args, outs, scratch=(), flops=0):
    vmem = pl.BlockSpec(memory_space=pltpu.VMEM)
    first = [pl.BlockSpec(memory_space=pltpu.SMEM)] if args[0].dtype == jnp.int32 else [vmem]
    shapes = [jax.ShapeDtypeStruct(s, d) for s, d in outs]
    moved = sum(a.size * a.dtype.itemsize for a in list(args) + shapes)
    return pl.pallas_call(
        kernel,
        out_shape=shapes,
        in_specs=first + [vmem] * (len(args) - 1),
        out_specs=[vmem] * len(shapes),
        scratch_shapes=list(scratch),
        compiler_params=pltpu.CompilerParams(vmem_limit_bytes=48 * 2**20),
        cost_estimate=pl.CostEstimate(flops=flops, bytes_accessed=moved, transcendentals=0),
    )(*args)


def mid_kernel(keep, got, mid, gain):
    rows = mid.shape[0] - SIDE
    total = keep[1].astype(F32) + got[1].astype(F32)
    mid[...] = total.astype(BF)
    near = keep[0, rows:].astype(F32) + got[0, rows:].astype(F32)
    for i, side in enumerate((near, total[rows:])):
        line = side[2:3] + side[3:4]
        gain[2 * i : 2 * i + 1] = line[:, :128]
        gain[2 * i + 1 : 2 * i + 2] = line[:, 128:]


def exchanged(a, axis, bit):
    return lax.ppermute(a, axis, [(i, i ^ bit) for i in range(lax.axis_size(axis))])


def summed(a, axis, bits):
    for bit in bits:
        a = a + exchanged(a, axis, bit)
    return a


def per_device(acts, grad_in, gain, w_qkv, w_out):
    t = lax.axis_index("tensor")
    dp, tm = lax.axis_size("dp"), lax.axis_size("tm")
    part = acts.shape[3]
    rows = acts.shape[2]
    few = rows // tm
    width = w_qkv.shape[0]
    cols = w_qkv.shape[2]
    heads = cols // HD
    norm = (rows * dp * tm) ** (-0.5)
    idx = jnp.reshape(t, (1,)).astype(jnp.int32)

    own = jnp.stack([acts.reshape(tm, few, part), grad_in.reshape(tm, few, part)], axis=1)
    own = lax.all_to_all(own, "tm", split_axis=0, concat_axis=0, tiled=True)
    far = lax.ppermute(own, "tensor", CHIP)
    near = lax.ppermute(own, "tensor", CORE)
    cross = lax.ppermute(far, "tensor", CORE)

    gain_rows = gain.reshape(4, 1, part)
    w = jnp.transpose(w_qkv, (1, 0, 2)).reshape(3, 4, part, cols)
    message = ((2, rows + SIDE, part), BF)
    dw, send, keep, xhat, inv = call(
        functools.partial(main_kernel, heads, norm),
        (idx, own, near, far, cross, gain_rows, w, w_out),
        (
            ((4, part, 4 * cols), BF),
            message,
            message,
            ((rows, part), F32),
            ((rows, 128), F32),
        ),
        (
            pltpu.VMEM((3, rows, cols), BF),
            pltpu.VMEM((4, rows, part), F32),
            pltpu.VMEM((4, rows, part), BF),
            pltpu.VMEM((4, rows, part), BF),
            pltpu.VMEM((rows, cols), BF),
        ),
        flops=7 * 10**9,
    )

    dw = dw.reshape(dp, width // dp, 4 * cols)
    dw = lax.all_to_all(dw, "dp", split_axis=0, concat_axis=0, tiled=True)

    got = lax.ppermute(send, "tensor", CORE)
    mid, gain_sum = call(
        mid_kernel, (keep, got), (((rows + SIDE, part), BF), ((4, 128), F32)), flops=1000
    )
    last = lax.ppermute(mid, "tensor", CHIP)
    gain_sum = summed(gain_sum, "dp", [1, 3])
    gain_sum = gain_sum[:2] + lax.ppermute(gain_sum[2:], "tensor", CHIP)
    (grad,) = call(
        acts_kernel,
        (idx, keep, got, last, xhat, inv, own, gain_rows),
        (((tm, 8, 2 * part), BF),),
        flops=10**6,
    )

    share = width // (dp * tm)
    total = 4 * cols + 2 * part + 128
    group = tm // 4
    pack = pl.pallas_call(
        pack_kernel,
        grid=(tm // group,),
        out_shape=jax.ShapeDtypeStruct((tm, share, total), BF),
        in_specs=[
            pl.BlockSpec((dp, group * share, 4 * cols), lambda i: (0, i, 0)),
            pl.BlockSpec((group, share, 2 * part), lambda i: (i, 0, 0)),
            pl.BlockSpec((2, 128), lambda i: (0, 0)),
        ],
        out_specs=pl.BlockSpec((group, share, total), lambda i: (i, 0, 0)),
        compiler_params=pltpu.CompilerParams(vmem_limit_bytes=32 * 2**20),
        cost_estimate=pl.CostEstimate(flops=10**6, bytes_accessed=10**6, transcendentals=0),
    )(dw, grad, gain_sum)
    pack = lax.all_to_all(pack, "tm", split_axis=0, concat_axis=0, tiled=True)
    out, dw, dw_out, gain_sum = call(
        last_kernel,
        (pack,),
        (((rows, part), BF), ((3, share, cols), F32), ((share, cols), F32), ((2, 128), F32)),
        flops=10**7,
    )
    return (
        out.reshape(grad_in.shape),
        jnp.transpose(dw, (1, 0, 2)),
        dw_out,
        gain_sum.reshape(part),
    )


def solution(mesh):
    placed = (
        P("dp", "tm", None, "tensor"),
        P("dp", "tm", None, "tensor"),
        P(),
        P(None, None, "tensor"),
        P("tensor", None),
    )
    return jax.shard_map(
        per_device,
        mesh=mesh,
        in_specs=placed,
        out_specs=(
            P("dp", "tm", None, "tensor"),
            P(("dp", "tm"), None, "tensor"),
            P(("dp", "tm"), "tensor"),
            P("tensor"),
        ),
        check_vma=False,
    )
```

```python
import functools

import jax
import jax.numpy as jnp
from jax import lax
from jax.experimental import pallas as pl
from jax.experimental.pallas import tpu as pltpu
from jax.sharding import PartitionSpec as P

HD = 64
EPS = 1e-05
CORE = [(0, 1), (1, 0), (2, 3), (3, 2)]
CHIP = [(0, 2), (2, 0), (1, 3), (3, 1)]
F32, BF = jnp.float32, jnp.bfloat16
SIDE = 32


def dot(a, b, contract):
    return lax.dot_general(a, b, (contract, ((), ())), preferred_element_type=F32)


def grouped(a):
    frames, few, part = a.shape
    a = a.astype(F32).reshape(frames, few // 8, 8, part)
    return jnp.concatenate([a[:, i].reshape(frames * 8, part) for i in range(few // 8)])


def attention(q, k, v, g, heads, scale):
    rows, cols = q.shape
    same = (
        lax.broadcasted_iota(jnp.int32, (rows, rows), 0) % 8
        == lax.broadcasted_iota(jnp.int32, (rows, rows), 1) % 8
    )
    lane = lax.broadcasted_iota(jnp.int32, (rows, cols), 1) // HD
    zero = jnp.zeros((rows, cols), BF)
    sums = [jnp.zeros((rows, cols), F32) for _ in range(4)]
    for h in range(heads):
        qh, kh, vh, gh = [jnp.where(lane == h, a, zero) for a in (q, k, v, g)]
        scores = dot(q, kh, ((1,), (1,))) * scale
        expd = jnp.exp(jnp.where(same, scores, -1e30))
        prob = expd / jnp.sum(expd, axis=-1, keepdims=True)
        low = prob.astype(BF)
        dprob = dot(g, vh, ((1,), (1,)))
        delta = jnp.sum(low.astype(F32) * dprob, axis=-1, keepdims=True)
        ds = (prob * (dprob - delta) * scale).astype(BF)
        sums[0] += dot(low, vh, ((1,), (0,)))
        sums[1] += dot(ds, kh, ((1,), (0,)))
        sums[2] += dot(ds, qh, ((0,), (0,)))
        sums[3] += dot(low, gh, ((0,), (0,)))
    return [a.astype(BF) for a in sums]


def split(a):
    high = a.astype(BF).astype(F32)
    return high, a - high


def main_kernel(
    heads, norm, idx, own, near, far, cross, gain, w, w_out,
    dw, send, keep, stats,
    gqkv, xhat, normed, dy, attn,
):
    t = idx[0]
    rows, part = normed.shape[1:]
    width = 4 * part
    pieces = (own, near, far, cross)
    x = [grouped(a[:, 0]) for a in pieces]
    mean = sum(jnp.sum(a, axis=-1, keepdims=True) for a in x) / width
    x = [a - mean for a in x]
    inv = lax.rsqrt(sum(jnp.sum(a * a, axis=-1, keepdims=True) for a in x) / width + EPS)
    for i in range(4):
        xhat[i] = x[i] * inv
        normed[i] = (xhat[i] * gain[t ^ i]).astype(BF)
        dy[i] = grouped(pieces[i][:, 1]).astype(BF)
    qkv = [
        sum(dot(normed[i], w[s, t ^ i], ((1,), (0,))) for i in range(4)).astype(BF)
        for s in range(3)
    ]
    g = sum(
        dot(dy[i], w_out[:, pl.ds(pl.multiple_of((t ^ i) * part, part), part)], ((1,), (1,)))
        for i in range(4)
    ).astype(BF)
    half = rows // 2
    for i in range(2):
        span = slice(i * half, (i + 1) * half)
        parts = attention(*(a[span] for a in qkv), g[span], heads, HD ** (-0.5))
        attn[span] = parts[0]
        for s in range(3):
            gqkv[s, span] = parts[1 + s]
    cols = w.shape[3]
    for i in range(4):
        for s in range(3):
            block = dot(normed[i], gqkv[s], ((0,), (0,))) * norm
            dw[t ^ i, :, s * cols : (s + 1) * cols] = block.astype(BF)
        block = dot(dy[i], attn[...], ((0,), (0,))) * norm
        dw[t ^ i, :, 3 * cols :] = block.astype(BF)
    first = jnp.zeros((rows, 1), F32)
    second = jnp.zeros((rows, 1), F32)
    outs = (keep.at[0], send.at[0], keep.at[1], send.at[1])
    gains = []
    for i in range(4):
        term = sum(dot(gqkv[s], w[s, t ^ i], ((1,), (1,))) for s in range(3)).astype(BF)
        outs[i][:rows] = term
        wide = term.astype(F32)
        product = wide * xhat[i]
        gains.append(jnp.sum(product, axis=0, keepdims=True) * norm)
        first += jnp.sum(wide * gain[t ^ i], axis=-1, keepdims=True)
        second += jnp.sum(product * gain[t ^ i], axis=-1, keepdims=True)
    lane = lax.broadcasted_iota(jnp.int32, (rows, 128), 1)
    moments = jnp.where(lane == 0, first / width, jnp.where(lane == 1, second / width, 0.0))
    moments = jnp.where(lane == 8, mean, jnp.where(lane == 9, inv, moments)).T
    stats[...] = moments[8:16]
    high, low = split(moments[:8])
    line = lax.broadcasted_iota(jnp.int32, (8, part), 0)
    for i in range(4):
        gain_high, gain_low = split(gains[i])
        top = jnp.where(line == 2, gain_high, jnp.where(line == 3, gain_low, high[:, :part]))
        side = [top, high[:, part:], low[:, :part], low[:, part:]]
        outs[i][rows:] = jnp.concatenate(side).astype(BF)


def acts_kernel(idx, keep, got, last, stats, own, gain, out):
    t = idx[0]
    frames, part = own.shape[0], own.shape[3]
    rows = stats.shape[1]
    total = keep[0].astype(F32) + got[0].astype(F32) + last[...].astype(F32)
    side = total[rows:]
    moments = jnp.concatenate([side[:8] + side[16:24], side[8:16] + side[24:]], axis=1)
    moments = jnp.concatenate([moments, stats[...], jnp.zeros((112, rows), F32)]).T
    first, second, mean, inv = [moments[:, i : i + 1] for i in (0, 1, 8, 9)]
    xhat = (grouped(own[:, 0]) - mean) * inv
    grad = grouped(own[:, 1]) + inv * (total[:rows] * gain[t] - first - xhat * second)
    half = frames * 8
    for i in range(2):
        block = grad[i * half : (i + 1) * half].reshape(frames, 8, part)
        out[:, :, i * part : (i + 1) * part] = block.astype(BF)


def pack_kernel(dw, grad, gain, out):
    group, share, cols = out.shape[0], out.shape[1], dw.shape[1]
    out[:, :, :cols] = dw[...].astype(F32).reshape(group, share, cols).astype(BF)
    end = cols + grad.shape[2]
    out[:, :, cols:end] = grad[...]
    high, low = split(gain[...])
    ride = jnp.concatenate([high, low, high, low])
    out[:, :, end:] = jnp.broadcast_to(ride[None], (group, share, 128)).astype(BF)


def last_kernel(came, out, dw, dw_out, gain):
    frames = came.shape[0]
    part = out.shape[1]
    for s in range(3):
        dw[s] = jnp.sum(came[:, :, s * part : (s + 1) * part].astype(F32), axis=0)
    dw_out[...] = jnp.sum(came[:, :, 3 * part : 4 * part].astype(F32), axis=0)
    grad = [came[:, :, i * part : (i + 1) * part].astype(F32) for i in (4, 5)]
    out[...] = jnp.concatenate(grad, axis=1).reshape(out.shape).astype(BF)
    ride = jnp.sum(came[:, :, 6 * part :].astype(F32), axis=0)
    gain[...] = ride[0:2] + ride[2:4]


def call(kernel, args, outs, scratch=(), flops=0, mib=8):
    vmem = pl.BlockSpec(memory_space=pltpu.VMEM)
    first = [pl.BlockSpec(memory_space=pltpu.SMEM)] if args[0].dtype == jnp.int32 else [vmem]
    shapes = [jax.ShapeDtypeStruct(s, d) for s, d in outs]
    moved = sum(a.size * a.dtype.itemsize for a in list(args) + shapes)
    return pl.pallas_call(
        kernel,
        out_shape=shapes,
        in_specs=first + [vmem] * (len(args) - 1),
        out_specs=[vmem] * len(shapes),
        scratch_shapes=list(scratch),
        compiler_params=pltpu.CompilerParams(vmem_limit_bytes=mib * 2**20),
        cost_estimate=pl.CostEstimate(flops=flops, bytes_accessed=moved, transcendentals=0),
    )(*args)


def mid_kernel(keep, got, mid, gain):
    rows = mid.shape[0] - SIDE
    total = keep[1].astype(F32) + got[1].astype(F32)
    mid[...] = total.astype(BF)
    near = keep[0, rows:].astype(F32) + got[0, rows:].astype(F32)
    for i, side in enumerate((near, total[rows:])):
        line = side[2:3] + side[3:4]
        gain[2 * i : 2 * i + 1] = line[:, :128]
        gain[2 * i + 1 : 2 * i + 2] = line[:, 128:]


def exchanged(a, axis, bit):
    return lax.ppermute(a, axis, [(i, i ^ bit) for i in range(lax.axis_size(axis))])


def summed(a, axis, bits):
    for bit in bits:
        a = a + exchanged(a, axis, bit)
    return a


def per_device(acts, grad_in, gain, w_qkv, w_out):
    t = lax.axis_index("tensor")
    dp, tm = lax.axis_size("dp"), lax.axis_size("tm")
    part = acts.shape[3]
    rows = acts.shape[2]
    few = rows // tm
    width = w_qkv.shape[0]
    cols = w_qkv.shape[2]
    heads = cols // HD
    norm = (rows * dp * tm) ** (-0.5)
    idx = jnp.reshape(t, (1,)).astype(jnp.int32)

    own = jnp.stack([acts.reshape(tm, few, part), grad_in.reshape(tm, few, part)], axis=1)
    own = lax.all_to_all(own, "tm", split_axis=0, concat_axis=0, tiled=True)
    far = lax.ppermute(own, "tensor", CHIP)
    near = lax.ppermute(own, "tensor", CORE)
    cross = lax.ppermute(far, "tensor", CORE)

    gain_rows = gain.reshape(4, 1, part)
    w = jnp.transpose(w_qkv, (1, 0, 2)).reshape(3, 4, part, cols)
    message = ((2, rows + SIDE, part), BF)
    dw, send, keep, stats = call(
        functools.partial(main_kernel, heads, norm),
        (idx, own, near, far, cross, gain_rows, w, w_out),
        (
            ((4, part, 4 * cols), BF),
            message,
            message,
            ((8, rows), F32),
        ),
        (
            pltpu.VMEM((3, rows, cols), BF),
            pltpu.VMEM((4, rows, part), F32),
            pltpu.VMEM((4, rows, part), BF),
            pltpu.VMEM((4, rows, part), BF),
            pltpu.VMEM((rows, cols), BF),
        ),
        flops=7 * 10**9,
        mib=24,
    )

    dw = lax.psum_scatter(dw.reshape(width, 4 * cols), "dp", scatter_dimension=0, tiled=True)

    got = lax.ppermute(send, "tensor", CORE)
    mid, gain_sum = call(
        mid_kernel, (keep, got), (((rows + SIDE, part), BF), ((4, 128), F32)), flops=1000
    )
    last = lax.ppermute(mid, "tensor", CHIP)
    gain_sum = summed(gain_sum, "dp", [1, 3])
    gain_sum = gain_sum[:2] + lax.ppermute(gain_sum[2:], "tensor", CHIP)
    (grad,) = call(
        acts_kernel,
        (idx, keep, got, last, stats, own, gain_rows),
        (((tm, 8, 2 * part), BF),),
        flops=10**6,
    )

    share = width // (dp * tm)
    total = 4 * cols + 2 * part + 128
    group = tm // 4
    pack = pl.pallas_call(
        pack_kernel,
        grid=(tm // group,),
        out_shape=jax.ShapeDtypeStruct((tm, share, total), BF),
        in_specs=[
            pl.BlockSpec((group * share, 4 * cols), lambda i: (i, 0)),
            pl.BlockSpec((group, share, 2 * part), lambda i: (i, 0, 0)),
            pl.BlockSpec((2, 128), lambda i: (0, 0)),
        ],
        out_specs=pl.BlockSpec((group, share, total), lambda i: (i, 0, 0)),
        compiler_params=pltpu.CompilerParams(vmem_limit_bytes=8 * 2**20),
        cost_estimate=pl.CostEstimate(flops=10**6, bytes_accessed=10**6, transcendentals=0),
    )(dw, grad, gain_sum)
    pack = lax.all_to_all(pack, "tm", split_axis=0, concat_axis=0, tiled=True)
    out, dw, dw_out, gain_sum = call(
        last_kernel,
        (pack,),
        (((rows, part), BF), ((3, share, cols), F32), ((share, cols), F32), ((2, 128), F32)),
        flops=10**7,
    )
    return (
        out.reshape(grad_in.shape),
        jnp.transpose(dw, (1, 0, 2)),
        dw_out,
        gain_sum.reshape(part),
    )


def solution(mesh):
    placed = (
        P("dp", "tm", None, "tensor"),
        P("dp", "tm", None, "tensor"),
        P(),
        P(None, None, "tensor"),
        P("tensor", None),
    )
    return jax.shard_map(
        per_device,
        mesh=mesh,
        in_specs=placed,
        out_specs=(
            P("dp", "tm", None, "tensor"),
            P(("dp", "tm"), None, "tensor"),
            P(("dp", "tm"), "tensor"),
            P("tensor"),
        ),
        check_vma=False,
    )
```

```python
import functools

import jax
import jax.numpy as jnp
from jax import lax
from jax.experimental import pallas as pl
from jax.experimental.pallas import tpu as pltpu
from jax.sharding import PartitionSpec as P

HD = 64
EPS = 1e-05
CORE = [(0, 1), (1, 0), (2, 3), (3, 2)]
CHIP = [(0, 2), (2, 0), (1, 3), (3, 1)]
F32, BF = jnp.float32, jnp.bfloat16
SIDE = 32


def dot(a, b, contract):
    return lax.dot_general(a, b, (contract, ((), ())), preferred_element_type=F32)


def grouped(a):
    frames, few, part = a.shape
    a = a.astype(F32).reshape(frames, few // 8, 8, part)
    return jnp.concatenate([a[:, i].reshape(frames * 8, part) for i in range(few // 8)])


def attention(q, k, v, g, heads, scale):
    rows, cols = q.shape
    same = (
        lax.broadcasted_iota(jnp.int32, (rows, rows), 0) % 8
        == lax.broadcasted_iota(jnp.int32, (rows, rows), 1) % 8
    )
    lane = lax.broadcasted_iota(jnp.int32, (rows, cols), 1) // HD
    zero = jnp.zeros((rows, cols), BF)
    sums = [jnp.zeros((rows, cols), F32) for _ in range(4)]
    for h in range(heads):
        qh, kh, vh, gh = [jnp.where(lane == h, a, zero) for a in (q, k, v, g)]
        scores = dot(q, kh, ((1,), (1,))) * scale
        expd = jnp.exp(jnp.where(same, scores, -1e30))
        prob = expd / jnp.sum(expd, axis=-1, keepdims=True)
        low = prob.astype(BF)
        dprob = dot(g, vh, ((1,), (1,)))
        delta = jnp.sum(low.astype(F32) * dprob, axis=-1, keepdims=True)
        ds = (prob * (dprob - delta) * scale).astype(BF)
        sums[0] += dot(low, vh, ((1,), (0,)))
        sums[1] += dot(ds, kh, ((1,), (0,)))
        sums[2] += dot(ds, qh, ((0,), (0,)))
        sums[3] += dot(low, gh, ((0,), (0,)))
    return [a.astype(BF) for a in sums]


def split(a):
    high = a.astype(BF).astype(F32)
    return high, a - high


def main_kernel(
    heads, norm, idx, gain, own, near, far, cross, w_at, w_out_at,
    dw_at, send, keep, stats,
    pieces, w, w_out, dw, gqkv, xhat, normed, dy, attn, arrived, left,
):
    t = idx[0]
    rows, part = normed.shape[1:]
    width = 4 * part
    sources = (own, near, far, cross, w_at, w_out_at)
    places = [pieces.at[i] for i in range(4)] + [w, w_out]
    copies = [
        pltpu.make_async_copy(a, b, arrived.at[i]) for i, (a, b) in enumerate(zip(sources, places))
    ]
    for copy in copies:
        copy.start()
    for copy in copies[:4]:
        copy.wait()
    x = [grouped(pieces[i, :, 0]) for i in range(4)]
    mean = sum(jnp.sum(a, axis=-1, keepdims=True) for a in x) / width
    x = [a - mean for a in x]
    inv = lax.rsqrt(sum(jnp.sum(a * a, axis=-1, keepdims=True) for a in x) / width + EPS)
    for i in range(4):
        xhat[i] = x[i] * inv
        normed[i] = (xhat[i] * gain[t ^ i]).astype(BF)
        dy[i] = grouped(pieces[i, :, 1]).astype(BF)
    for copy in copies[4:]:
        copy.wait()
    qkv = [
        sum(dot(normed[i], w[s, t ^ i], ((1,), (0,))) for i in range(4)).astype(BF)
        for s in range(3)
    ]
    g = sum(
        dot(dy[i], w_out[:, pl.ds(pl.multiple_of((t ^ i) * part, part), part)], ((1,), (1,)))
        for i in range(4)
    ).astype(BF)
    half = rows // 2
    for i in range(2):
        span = slice(i * half, (i + 1) * half)
        parts = attention(*(a[span] for a in qkv), g[span], heads, HD ** (-0.5))
        attn[span] = parts[0]
        for s in range(3):
            gqkv[s, span] = parts[1 + s]
    cols = w.shape[3]
    copies = []
    for i in range(4):
        for s in range(3):
            block = dot(normed[i], gqkv[s], ((0,), (0,))) * norm
            dw[i, :, s * cols : (s + 1) * cols] = block.astype(BF)
        block = dot(dy[i], attn[...], ((0,), (0,))) * norm
        dw[i, :, 3 * cols :] = block.astype(BF)
        copies.append(pltpu.make_async_copy(dw.at[i], dw_at.at[t ^ i], left.at[i]))
        copies[i].start()
    first = jnp.zeros((rows, 1), F32)
    second = jnp.zeros((rows, 1), F32)
    outs = (keep.at[0], send.at[0], keep.at[1], send.at[1])
    gains = []
    for i in range(4):
        term = sum(dot(gqkv[s], w[s, t ^ i], ((1,), (1,))) for s in range(3)).astype(BF)
        outs[i][:rows] = term
        wide = term.astype(F32)
        product = wide * xhat[i]
        gains.append(jnp.sum(product, axis=0, keepdims=True) * norm)
        first += jnp.sum(wide * gain[t ^ i], axis=-1, keepdims=True)
        second += jnp.sum(product * gain[t ^ i], axis=-1, keepdims=True)
    lane = lax.broadcasted_iota(jnp.int32, (rows, 128), 1)
    moments = jnp.where(lane == 0, first / width, jnp.where(lane == 1, second / width, 0.0))
    moments = jnp.where(lane == 8, mean, jnp.where(lane == 9, inv, moments)).T
    stats[...] = moments[8:16]
    high, low = split(moments[:8])
    line = lax.broadcasted_iota(jnp.int32, (8, part), 0)
    for i in range(4):
        gain_high, gain_low = split(gains[i])
        top = jnp.where(line == 2, gain_high, jnp.where(line == 3, gain_low, high[:, :part]))
        side = [top, high[:, part:], low[:, :part], low[:, part:]]
        outs[i][rows:] = jnp.concatenate(side).astype(BF)
    for copy in copies:
        copy.wait()


def acts_kernel(idx, keep, got, last, stats, own, gain, out, gain_sum):
    t = idx[0]
    frames, part = own.shape[0], own.shape[3]
    rows = stats.shape[1]
    total = keep[0].astype(F32) + got[0].astype(F32) + last[...].astype(F32)
    side = total[rows:]
    line = side[2:3] + side[3:4]
    gain_sum[0:1] = line[:, :128]
    gain_sum[1:2] = line[:, 128:]
    moments = jnp.concatenate([side[:8] + side[16:24], side[8:16] + side[24:]], axis=1)
    moments = jnp.concatenate([moments, stats[...], jnp.zeros((112, rows), F32)]).T
    first, second, mean, inv = [moments[:, i : i + 1] for i in (0, 1, 8, 9)]
    xhat = (grouped(own[:, 0]) - mean) * inv
    grad = grouped(own[:, 1]) + inv * (total[:rows] * gain[t] - first - xhat * second)
    half = frames * 8
    for i in range(2):
        block = grad[i * half : (i + 1) * half].reshape(frames, 8, part)
        out[:, :, i * part : (i + 1) * part] = block.astype(BF)


def pack_kernel(dw, grad, gain, first, second, third, out):
    group, share, cols = out.shape[0], out.shape[1], dw.shape[2]
    block = sum(dw[i].astype(F32) for i in range(dw.shape[0]))
    out[:, :, :cols] = block.reshape(group, share, cols).astype(BF)
    end = cols + grad.shape[2]
    out[:, :, cols:end] = grad[...]
    high, low = split(gain[...] + first[...] + second[...] + third[...])
    ride = jnp.concatenate([high, low, high, low])
    out[:, :, end:] = jnp.broadcast_to(ride[None], (group, share, 128)).astype(BF)


def last_kernel(came, out, dw, dw_out, gain):
    frames = came.shape[0]
    part = out.shape[1]
    for s in range(3):
        dw[s] = jnp.sum(came[:, :, s * part : (s + 1) * part].astype(F32), axis=0)
    dw_out[...] = jnp.sum(came[:, :, 3 * part : 4 * part].astype(F32), axis=0)
    grad = [came[:, :, i * part : (i + 1) * part].astype(F32) for i in (4, 5)]
    out[...] = jnp.concatenate(grad, axis=1).reshape(out.shape).astype(BF)
    ride = jnp.sum(came[:, :, 6 * part :].astype(F32), axis=0)
    gain[...] = ride[0:2] + ride[2:4]


def call(kernel, args, outs, scratch=(), flops=0, mib=8, anywhere=None):
    vmem = pl.BlockSpec(memory_space=pltpu.VMEM)
    in_specs, out_specs = [vmem] * len(args), [vmem] * len(outs)
    if args[0].dtype == jnp.int32:
        in_specs[0] = pl.BlockSpec(memory_space=pltpu.SMEM)
    if anywhere is not None:
        start, end = anywhere
        in_specs[start:] = [pl.BlockSpec(memory_space=pl.ANY)] * (len(args) - start)
        out_specs[:end] = [pl.BlockSpec(memory_space=pl.ANY)] * end
    shapes = [jax.ShapeDtypeStruct(s, d) for s, d in outs]
    moved = sum(a.size * a.dtype.itemsize for a in list(args) + shapes)
    return pl.pallas_call(
        kernel,
        out_shape=shapes,
        in_specs=in_specs,
        out_specs=out_specs,
        scratch_shapes=list(scratch),
        compiler_params=pltpu.CompilerParams(vmem_limit_bytes=mib * 2**20),
        cost_estimate=pl.CostEstimate(flops=flops, bytes_accessed=moved, transcendentals=0),
    )(*args)


def mid_kernel(keep, got, mid):
    mid[...] = (keep[1].astype(F32) + got[1].astype(F32)).astype(BF)


def per_device(acts, grad_in, gain, w_qkv, w_out):
    t = lax.axis_index("tensor")
    dp, tm = lax.axis_size("dp"), lax.axis_size("tm")
    part = acts.shape[3]
    rows = acts.shape[2]
    few = rows // tm
    width = w_qkv.shape[0]
    cols = w_qkv.shape[2]
    heads = cols // HD
    norm = (rows * dp * tm) ** (-0.5)
    idx = jnp.reshape(t, (1,)).astype(jnp.int32)

    own = jnp.stack([acts.reshape(tm, few, part), grad_in.reshape(tm, few, part)], axis=1)
    own = lax.all_to_all(own, "tm", split_axis=0, concat_axis=0, tiled=True)
    far = lax.ppermute(own, "tensor", CHIP)
    near = lax.ppermute(own, "tensor", CORE)
    cross = lax.ppermute(far, "tensor", CORE)

    gain_rows = gain.reshape(4, 1, part)
    w = jnp.transpose(w_qkv, (1, 0, 2)).reshape(3, 4, part, cols)
    message = ((2, rows + SIDE, part), BF)
    dw, send, keep, stats = call(
        functools.partial(main_kernel, heads, norm),
        (idx, gain_rows, own, near, far, cross, w, w_out),
        (((4, part, 4 * cols), BF), message, message, ((8, rows), F32)),
        (
            pltpu.VMEM((4,) + own.shape, BF),
            pltpu.VMEM(w.shape, BF),
            pltpu.VMEM(w_out.shape, BF),
            pltpu.VMEM((4, part, 4 * cols), BF),
            pltpu.VMEM((3, rows, cols), BF),
            pltpu.VMEM((4, rows, part), F32),
            pltpu.VMEM((4, rows, part), BF),
            pltpu.VMEM((4, rows, part), BF),
            pltpu.VMEM((rows, cols), BF),
            pltpu.SemaphoreType.DMA((6,)),
            pltpu.SemaphoreType.DMA((4,)),
        ),
        flops=7 * 10**9,
        mib=32,
        anywhere=(2, 1),
    )

    dw = dw.reshape(dp, width // dp, 4 * cols)
    dw = lax.all_to_all(dw, "dp", split_axis=0, concat_axis=0, tiled=True)

    got = lax.ppermute(send, "tensor", CORE)
    (mid,) = call(mid_kernel, (keep, got), (((rows + SIDE, part), BF),), flops=1000)
    last = lax.ppermute(mid, "tensor", CHIP)
    grad, gain_sum = call(
        acts_kernel,
        (idx, keep, got, last, stats, own, gain_rows),
        (((tm, 8, 2 * part), BF), ((2, 128), F32)),
        flops=10**6,
    )
    gain_sums = [gain_sum] + [
        lax.ppermute(gain_sum, "dp", [(i, i ^ bit) for i in range(dp)]) for bit in (1, 3, 2)
    ]

    share = width // (dp * tm)
    total = 4 * cols + 2 * part + 128
    group = tm // 4
    pack = pl.pallas_call(
        pack_kernel,
        grid=(tm // group,),
        out_shape=jax.ShapeDtypeStruct((tm, share, total), BF),
        in_specs=[
            pl.BlockSpec((dp, group * share, 4 * cols), lambda i: (0, i, 0)),
            pl.BlockSpec((group, share, 2 * part), lambda i: (i, 0, 0)),
        ]
        + [pl.BlockSpec((2, 128), lambda i: (0, 0))] * 4,
        out_specs=pl.BlockSpec((group, share, total), lambda i: (i, 0, 0)),
        compiler_params=pltpu.CompilerParams(vmem_limit_bytes=8 * 2**20),
        cost_estimate=pl.CostEstimate(flops=10**6, bytes_accessed=10**6, transcendentals=0),
    )(dw, grad, *gain_sums)
    pack = lax.all_to_all(pack, "tm", split_axis=0, concat_axis=0, tiled=True)
    out, dw, dw_out, gain_sum = call(
        last_kernel,
        (pack,),
        (((rows, part), BF), ((3, share, cols), F32), ((share, cols), F32), ((2, 128), F32)),
        flops=10**7,
    )
    return (
        out.reshape(grad_in.shape),
        jnp.transpose(dw, (1, 0, 2)),
        dw_out,
        gain_sum.reshape(part),
    )


def solution(mesh):
    placed = (
        P("dp", "tm", None, "tensor"),
        P("dp", "tm", None, "tensor"),
        P(),
        P(None, None, "tensor"),
        P("tensor", None),
    )
    return jax.shard_map(
        per_device,
        mesh=mesh,
        in_specs=placed,
        out_specs=(
            P("dp", "tm", None, "tensor"),
            P(("dp", "tm"), None, "tensor"),
            P(("dp", "tm"), "tensor"),
            P("tensor"),
        ),
        check_vma=False,
    )
```

```python
import functools

import jax
import jax.numpy as jnp
from jax import lax
from jax.experimental import pallas as pl
from jax.experimental.pallas import tpu as pltpu
from jax.sharding import PartitionSpec as P

HD = 64
EPS = 1e-05
CORE = [(0, 1), (1, 0), (2, 3), (3, 2)]
CHIP = [(0, 2), (2, 0), (1, 3), (3, 1)]
F32, BF = jnp.float32, jnp.bfloat16
SIDE = 32


def dot(a, b, contract):
    return lax.dot_general(a, b, (contract, ((), ())), preferred_element_type=F32)


def grouped(a):
    frames, few, part = a.shape
    a = a.astype(F32).reshape(frames, few // 8, 8, part)
    return jnp.concatenate([a[:, i].reshape(frames * 8, part) for i in range(few // 8)])


def attention(q, k, v, g, heads, scale):
    rows, cols = q.shape
    same = (
        lax.broadcasted_iota(jnp.int32, (rows, rows), 0) % 8
        == lax.broadcasted_iota(jnp.int32, (rows, rows), 1) % 8
    )
    lane = lax.broadcasted_iota(jnp.int32, (rows, cols), 1) // HD
    zero = jnp.zeros((rows, cols), BF)
    sums = [jnp.zeros((rows, cols), F32) for _ in range(4)]
    for h in range(heads):
        qh, kh, vh, gh = [jnp.where(lane == h, a, zero) for a in (q, k, v, g)]
        scores = dot(q, kh, ((1,), (1,))) * scale
        expd = jnp.exp(jnp.where(same, scores, -1e30))
        prob = expd / jnp.sum(expd, axis=-1, keepdims=True)
        low = prob.astype(BF)
        dprob = dot(g, vh, ((1,), (1,)))
        delta = jnp.sum(low.astype(F32) * dprob, axis=-1, keepdims=True)
        ds = (prob * (dprob - delta) * scale).astype(BF)
        sums[0] += dot(low, vh, ((1,), (0,)))
        sums[1] += dot(ds, kh, ((1,), (0,)))
        sums[2] += dot(ds, qh, ((0,), (0,)))
        sums[3] += dot(low, gh, ((0,), (0,)))
    return [a.astype(BF) for a in sums]


def split(a):
    high = a.astype(BF).astype(F32)
    return high, a - high


def main_kernel(
    heads, norm, idx, gain, own, near, far, cross, w_at, w_out_at,
    dw_at, send_at, keep, stats,
    pieces, w, w_out, dw, send, gqkv, xhat, normed, dy, attn, arrived, left,
):
    t = idx[0]
    rows, part = normed.shape[1:]
    width = 4 * part
    sources = (own, near, far, cross, w_at, w_out_at)
    places = [pieces.at[i] for i in range(4)] + [w, w_out]
    copies = [
        pltpu.make_async_copy(a, b, arrived.at[i]) for i, (a, b) in enumerate(zip(sources, places))
    ]
    for copy in copies:
        copy.start()
    for copy in copies[:4]:
        copy.wait()
    x = [grouped(pieces[i, :, 0]) for i in range(4)]
    mean = sum(jnp.sum(a, axis=-1, keepdims=True) for a in x) / width
    x = [a - mean for a in x]
    inv = lax.rsqrt(sum(jnp.sum(a * a, axis=-1, keepdims=True) for a in x) / width + EPS)
    for i in range(4):
        xhat[i] = x[i] * inv
        normed[i] = (xhat[i] * gain[t ^ i]).astype(BF)
        dy[i] = grouped(pieces[i, :, 1]).astype(BF)
    for copy in copies[4:]:
        copy.wait()
    qkv = [
        sum(dot(normed[i], w[s, t ^ i], ((1,), (0,))) for i in range(4)).astype(BF)
        for s in range(3)
    ]
    g = sum(
        dot(dy[i], w_out[:, pl.ds(pl.multiple_of((t ^ i) * part, part), part)], ((1,), (1,)))
        for i in range(4)
    ).astype(BF)
    half = rows // 2
    for i in range(2):
        span = slice(i * half, (i + 1) * half)
        parts = attention(*(a[span] for a in qkv), g[span], heads, HD ** (-0.5))
        attn[span] = parts[0]
        for s in range(3):
            gqkv[s, span] = parts[1 + s]
    cols = w.shape[3]
    copies = []
    for i in range(4):
        for s in range(3):
            block = dot(normed[i], gqkv[s], ((0,), (0,))) * norm
            dw[i, :, s * cols : (s + 1) * cols] = block.astype(BF)
        block = dot(dy[i], attn[...], ((0,), (0,))) * norm
        dw[i, :, 3 * cols :] = block.astype(BF)
        copies.append(pltpu.make_async_copy(dw.at[i], dw_at.at[t ^ i], left.at[i]))
        copies[i].start()
    first = jnp.zeros((rows, 1), F32)
    second = jnp.zeros((rows, 1), F32)
    outs = (keep.at[0], send.at[0], keep.at[1], send.at[1])
    gains = []
    for i in range(4):
        term = sum(dot(gqkv[s], w[s, t ^ i], ((1,), (1,))) for s in range(3)).astype(BF)
        outs[i][:rows] = term
        wide = term.astype(F32)
        product = wide * xhat[i]
        gains.append(jnp.sum(product, axis=0, keepdims=True) * norm)
        first += jnp.sum(wide * gain[t ^ i], axis=-1, keepdims=True)
        second += jnp.sum(product * gain[t ^ i], axis=-1, keepdims=True)
    lane = lax.broadcasted_iota(jnp.int32, (rows, 128), 1)
    moments = jnp.where(lane == 0, first / width, jnp.where(lane == 1, second / width, 0.0))
    moments = jnp.where(lane == 8, mean, jnp.where(lane == 9, inv, moments)).T
    stats[...] = moments[8:16]
    high, low = split(moments[:8])
    line = lax.broadcasted_iota(jnp.int32, (8, part), 0)
    for i in range(4):
        gain_high, gain_low = split(gains[i])
        top = jnp.where(line == 2, gain_high, jnp.where(line == 3, gain_low, high[:, :part]))
        side = [top, high[:, part:], low[:, :part], low[:, part:]]
        outs[i][rows:] = jnp.concatenate(side).astype(BF)
    copies.append(pltpu.make_async_copy(send, send_at, left.at[4]))
    copies[4].start()
    for copy in copies:
        copy.wait()


def acts_kernel(idx, keep, got, last, stats, own, gain, out):
    t = idx[0]
    frames, part = own.shape[0], own.shape[3]
    rows = stats.shape[1]
    total = keep[0].astype(F32) + got[0].astype(F32) + last[...].astype(F32)
    side = total[rows:]
    moments = jnp.concatenate([side[:8] + side[16:24], side[8:16] + side[24:]], axis=1)
    moments = jnp.concatenate([moments, stats[...], jnp.zeros((112, rows), F32)]).T
    first, second, mean, inv = [moments[:, i : i + 1] for i in (0, 1, 8, 9)]
    xhat = (grouped(own[:, 0]) - mean) * inv
    grad = grouped(own[:, 1]) + inv * (total[:rows] * gain[t] - first - xhat * second)
    half = frames * 8
    for i in range(2):
        block = grad[i * half : (i + 1) * half].reshape(frames, 8, part)
        out[:, :, i * part : (i + 1) * part] = block.astype(BF)


def pack_kernel(dw, grad, gain, first, second, third, out):
    group, share, cols = out.shape[0], out.shape[1], dw.shape[2]
    block = sum(dw[i].astype(F32) for i in range(dw.shape[0]))
    out[:, :, :cols] = block.reshape(group, share, cols).astype(BF)
    end = cols + grad.shape[2]
    out[:, :, cols:end] = grad[...]
    high, low = split(gain[...] + first[...] + second[...] + third[...])
    ride = jnp.concatenate([high, low, high, low])
    out[:, :, end:] = jnp.broadcast_to(ride[None], (group, share, 128)).astype(BF)


def last_kernel(came, out, dw, dw_out, gain):
    frames = came.shape[0]
    part = out.shape[1]
    for s in range(3):
        dw[s] = jnp.sum(came[:, :, s * part : (s + 1) * part].astype(F32), axis=0)
    dw_out[...] = jnp.sum(came[:, :, 3 * part : 4 * part].astype(F32), axis=0)
    grad = [came[:, :, i * part : (i + 1) * part].astype(F32) for i in (4, 5)]
    out[...] = jnp.concatenate(grad, axis=1).reshape(out.shape).astype(BF)
    ride = jnp.sum(came[:, :, 6 * part :].astype(F32), axis=0)
    gain[...] = ride[0:2] + ride[2:4]


def call(kernel, args, outs, scratch=(), flops=0, mib=8, hbm=None):
    vmem = pl.BlockSpec(memory_space=pltpu.VMEM)
    in_specs, out_specs = [vmem] * len(args), [vmem] * len(outs)
    if args[0].dtype == jnp.int32:
        in_specs[0] = pl.BlockSpec(memory_space=pltpu.SMEM)
    if hbm is not None:
        start, end = hbm
        in_specs[start:] = [pl.BlockSpec(memory_space=pl.ANY)] * (len(args) - start)
        out_specs[:end] = [pl.BlockSpec(memory_space=pl.ANY)] * end
    shapes = [jax.ShapeDtypeStruct(s, d) for s, d in outs]
    moved = sum(a.size * a.dtype.itemsize for a in list(args) + shapes)
    return pl.pallas_call(
        kernel,
        out_shape=shapes,
        in_specs=in_specs,
        out_specs=out_specs,
        scratch_shapes=list(scratch),
        compiler_params=pltpu.CompilerParams(vmem_limit_bytes=mib * 2**20),
        cost_estimate=pl.CostEstimate(flops=flops, bytes_accessed=moved, transcendentals=0),
    )(*args)


def gain_kernel(keep, got, gain):
    rows = keep.shape[1] - SIDE
    for i in range(2):
        side = keep[i, rows:].astype(F32) + got[i, rows:].astype(F32)
        line = side[2:3] + side[3:4]
        gain[2 * i : 2 * i + 1] = line[:, :128]
        gain[2 * i + 1 : 2 * i + 2] = line[:, 128:]


def mid_kernel(keep, got, near, far, mid, gain):
    mid[...] = (keep[1].astype(F32) + got[1].astype(F32)).astype(BF)
    gain[...] = near[0:2] + far[...]


def per_device(acts, grad_in, gain, w_qkv, w_out):
    t = lax.axis_index("tensor")
    dp, tm = lax.axis_size("dp"), lax.axis_size("tm")
    part = acts.shape[3]
    rows = acts.shape[2]
    few = rows // tm
    width = w_qkv.shape[0]
    cols = w_qkv.shape[2]
    heads = cols // HD
    norm = (rows * dp * tm) ** (-0.5)
    idx = jnp.reshape(t, (1,)).astype(jnp.int32)

    own = jnp.stack([acts.reshape(tm, few, part), grad_in.reshape(tm, few, part)], axis=1)
    own = lax.all_to_all(own, "tm", split_axis=0, concat_axis=0, tiled=True)
    far = lax.ppermute(own, "tensor", CHIP)
    near = lax.ppermute(own, "tensor", CORE)
    cross = lax.ppermute(far, "tensor", CORE)

    gain_rows = gain.reshape(4, 1, part)
    w = jnp.transpose(w_qkv, (1, 0, 2)).reshape(3, 4, part, cols)
    message = ((2, rows + SIDE, part), BF)
    dw, send, keep, stats = call(
        functools.partial(main_kernel, heads, norm),
        (idx, gain_rows, own, near, far, cross, w, w_out),
        (((4, part, 4 * cols), BF), message, message, ((8, rows), F32)),
        (
            pltpu.VMEM((4,) + own.shape, BF),
            pltpu.VMEM(w.shape, BF),
            pltpu.VMEM(w_out.shape, BF),
            pltpu.VMEM((4, part, 4 * cols), BF),
            pltpu.VMEM((2, rows + SIDE, part), BF),
            pltpu.VMEM((3, rows, cols), BF),
            pltpu.VMEM((4, rows, part), F32),
            pltpu.VMEM((4, rows, part), BF),
            pltpu.VMEM((4, rows, part), BF),
            pltpu.VMEM((rows, cols), BF),
            pltpu.SemaphoreType.DMA((6,)),
            pltpu.SemaphoreType.DMA((5,)),
        ),
        flops=7 * 10**9,
        mib=60,
        hbm=(2, 2),
    )

    dw = dw.reshape(dp, width // dp, 4 * cols)
    dw = lax.all_to_all(dw, "dp", split_axis=0, concat_axis=0, tiled=True)

    got = lax.ppermute(send, "tensor", CORE)
    (near_sum,) = call(gain_kernel, (keep, got), (((4, 128), F32),), flops=1000)
    far_sum = lax.ppermute(near_sum[2:], "tensor", CHIP)
    mid, gain_sum = call(
        mid_kernel,
        (keep, got, near_sum, far_sum),
        (((rows + SIDE, part), BF), ((2, 128), F32)),
        flops=1000,
    )
    last = lax.ppermute(mid, "tensor", CHIP)
    gain_sums = [gain_sum] + [
        lax.ppermute(gain_sum, "dp", [(i, i ^ bit) for i in range(dp)]) for bit in (1, 3, 2)
    ]
    (grad,) = call(
        acts_kernel,
        (idx, keep, got, last, stats, own, gain_rows),
        (((tm, 8, 2 * part), BF),),
        flops=10**6,
    )

    share = width // (dp * tm)
    total = 4 * cols + 2 * part + 128
    group = tm // 4
    pack = pl.pallas_call(
        pack_kernel,
        grid=(tm // group,),
        out_shape=jax.ShapeDtypeStruct((tm, share, total), BF),
        in_specs=[
            pl.BlockSpec((dp, group * share, 4 * cols), lambda i: (0, i, 0)),
            pl.BlockSpec((group, share, 2 * part), lambda i: (i, 0, 0)),
        ]
        + [pl.BlockSpec((2, 128), lambda i: (0, 0))] * 4,
        out_specs=pl.BlockSpec((group, share, total), lambda i: (i, 0, 0)),
        compiler_params=pltpu.CompilerParams(vmem_limit_bytes=8 * 2**20),
        cost_estimate=pl.CostEstimate(flops=10**6, bytes_accessed=10**6, transcendentals=0),
    )(dw, grad, *gain_sums)
    pack = lax.all_to_all(pack, "tm", split_axis=0, concat_axis=0, tiled=True)
    out, dw, dw_out, gain_sum = call(
        last_kernel,
        (pack,),
        (((rows, part), BF), ((3, share, cols), F32), ((share, cols), F32), ((2, 128), F32)),
        flops=10**7,
    )
    return (
        out.reshape(grad_in.shape),
        jnp.transpose(dw, (1, 0, 2)),
        dw_out,
        gain_sum.reshape(part),
    )


def solution(mesh):
    placed = (
        P("dp", "tm", None, "tensor"),
        P("dp", "tm", None, "tensor"),
        P(),
        P(None, None, "tensor"),
        P("tensor", None),
    )
    return jax.shard_map(
        per_device,
        mesh=mesh,
        in_specs=placed,
        out_specs=(
            P("dp", "tm", None, "tensor"),
            P(("dp", "tm"), None, "tensor"),
            P(("dp", "tm"), "tensor"),
            P("tensor"),
        ),
        check_vma=False,
    )
```

```python
import functools
import math

import jax
import jax.numpy as jnp
from jax import lax
from jax.experimental import pallas as pl
from jax.experimental.pallas import tpu as pltpu
from jax.sharding import PartitionSpec as P

HD = 64
EPS = 1e-05
CORE = [(0, 1), (1, 0), (2, 3), (3, 2)]
CHIP = [(0, 2), (2, 0), (1, 3), (3, 1)]
F32, BF = jnp.float32, jnp.bfloat16
SIDE = 32


def dot(a, b, contract):
    return lax.dot_general(a, b, (contract, ((), ())), preferred_element_type=F32)


def grouped(a):
    frames, few, part = a.shape
    a = a.astype(F32).reshape(frames, few // 8, 8, part)
    return jnp.concatenate([a[:, i].reshape(frames * 8, part) for i in range(few // 8)])


def attention(q, k, v, g, heads, scale):
    rows, cols = q.shape
    same = (
        lax.broadcasted_iota(jnp.int32, (rows, rows), 0) % 8
        == lax.broadcasted_iota(jnp.int32, (rows, rows), 1) % 8
    )
    lane = lax.broadcasted_iota(jnp.int32, (rows, cols), 1) // HD
    zero = jnp.zeros((rows, cols), BF)
    sums = [jnp.zeros((rows, cols), F32) for _ in range(4)]
    g_scaled = (g.astype(F32) * scale).astype(BF)
    for h in range(heads):
        qh, kh, vh, gh = [jnp.where(lane == h, a, zero) for a in (q, k, v, g)]
        scores = dot(q, kh, ((1,), (1,))) * (scale * math.log2(math.e))
        expd = jnp.exp2(jnp.where(same, scores, -1e30))
        prob = expd * (1.0 / jnp.sum(expd, axis=-1, keepdims=True))
        low = prob.astype(BF)
        dprob = dot(g_scaled, vh, ((1,), (1,)))
        delta = jnp.sum(low.astype(F32) * dprob, axis=-1, keepdims=True)
        ds = (prob * (dprob - delta)).astype(BF)
        sums[0] += dot(low, vh, ((1,), (0,)))
        sums[1] += dot(ds, kh, ((1,), (0,)))
        sums[2] += dot(ds, qh, ((0,), (0,)))
        sums[3] += dot(low, gh, ((0,), (0,)))
    return [a.astype(BF) for a in sums]


def split(a):
    high = a.astype(BF).astype(F32)
    return high, a - high


def main_kernel(
    heads, norm, idx, gain, own, near, far, cross, w_at, w_out_at,
    dw_at, send_at, keep_at, stats,
    pieces, w, w_out, dw, send, keep, gqkv, xhat, normed, dy, attn, arrived, left,
):
    t = idx[0]
    rows, part = normed.shape[1:]
    width = 4 * part
    sources = (own, near, far, cross)
    moves = [(sources[i].at[:, 0], pieces.at[i, :, 0]) for i in range(4)] + [(w_at, w)]
    moves += [(sources[i].at[:, 1], pieces.at[i, :, 1]) for i in range(4)] + [(w_out_at, w_out)]
    copies = [pltpu.make_async_copy(a, b, arrived.at[i]) for i, (a, b) in enumerate(moves)]
    for copy in copies:
        copy.start()
    for copy in copies[:4]:
        copy.wait()
    x = [grouped(pieces[i, :, 0]) for i in range(4)]
    mean = sum(jnp.sum(a, axis=-1, keepdims=True) for a in x) / width
    x = [a - mean for a in x]
    inv = lax.rsqrt(sum(jnp.sum(a * a, axis=-1, keepdims=True) for a in x) / width + EPS)
    for i in range(4):
        xhat[i] = x[i] * inv
        normed[i] = (xhat[i] * gain[t ^ i]).astype(BF)
    copies[4].wait()
    qkv = [
        sum(dot(normed[i], w[s, t ^ i], ((1,), (0,))) for i in range(4)).astype(BF)
        for s in range(3)
    ]
    for copy in copies[5:]:
        copy.wait()
    for i in range(4):
        dy[i] = grouped(pieces[i, :, 1]).astype(BF)
    g = sum(
        dot(dy[i], w_out[:, pl.ds(pl.multiple_of((t ^ i) * part, part), part)], ((1,), (1,)))
        for i in range(4)
    ).astype(BF)
    half = rows // 2
    for i in range(2):
        span = slice(i * half, (i + 1) * half)
        parts = attention(*(a[span] for a in qkv), g[span], heads, HD ** (-0.5))
        attn[span] = parts[0]
        for s in range(3):
            gqkv[s, span] = parts[1 + s]
    first = jnp.zeros((rows, 1), F32)
    second = jnp.zeros((rows, 1), F32)
    outs = (keep.at[0], send.at[0], keep.at[1], send.at[1])
    gains = []
    for i in range(4):
        term = sum(dot(gqkv[s], w[s, t ^ i], ((1,), (1,))) for s in range(3)).astype(BF)
        outs[i][:rows] = term
        wide = term.astype(F32)
        product = wide * xhat[i]
        gains.append(jnp.sum(product, axis=0, keepdims=True) * norm)
        first += jnp.sum(wide * gain[t ^ i], axis=-1, keepdims=True)
        second += jnp.sum(product * gain[t ^ i], axis=-1, keepdims=True)
    lane = lax.broadcasted_iota(jnp.int32, (rows, 128), 1)
    moments = jnp.where(lane == 0, first / width, jnp.where(lane == 1, second / width, 0.0))
    moments = jnp.where(lane == 8, mean, jnp.where(lane == 9, inv, moments)).T
    stats[...] = moments[8:16]
    high, low = split(moments[:8])
    line = lax.broadcasted_iota(jnp.int32, (8, part), 0)
    for i in range(4):
        gain_high, gain_low = split(gains[i])
        top = jnp.where(line == 2, gain_high, jnp.where(line == 3, gain_low, high[:, :part]))
        side = [top, high[:, part:], low[:, :part], low[:, part:]]
        outs[i][rows:] = jnp.concatenate(side).astype(BF)
    copies = [
        pltpu.make_async_copy(send, send_at, left.at[4]),
        pltpu.make_async_copy(keep, keep_at, left.at[5]),
    ]
    for copy in copies:
        copy.start()
    cols = w.shape[3]
    for i in range(4):
        for s in range(3):
            block = dot(normed[i], gqkv[s], ((0,), (0,))) * norm
            dw[i, :, s * cols : (s + 1) * cols] = block.astype(BF)
        block = dot(dy[i], attn[...], ((0,), (0,))) * norm
        dw[i, :, 3 * cols :] = block.astype(BF)
        copies.append(pltpu.make_async_copy(dw.at[i], dw_at.at[t ^ i], left.at[i]))
        copies[-1].start()
    for copy in copies:
        copy.wait()


def acts_kernel(idx, keep, got, last, stats, own, gain, out):
    t = idx[0]
    frames, part = own.shape[0], own.shape[3]
    rows = stats.shape[1]
    total = keep[0].astype(F32) + got[0].astype(F32) + last[...].astype(F32)
    side = total[rows:]
    moments = jnp.concatenate([side[:8] + side[16:24], side[8:16] + side[24:]], axis=1)
    moments = jnp.concatenate([moments, stats[...], jnp.zeros((112, rows), F32)]).T
    first, second, mean, inv = [moments[:, i : i + 1] for i in (0, 1, 8, 9)]
    xhat = (grouped(own[:, 0]) - mean) * inv
    grad = grouped(own[:, 1]) + inv * (total[:rows] * gain[t] - first - xhat * second)
    half = frames * 8
    for i in range(2):
        block = grad[i * half : (i + 1) * half].reshape(frames, 8, part)
        out[:, :, i * part : (i + 1) * part] = block.astype(BF)


def pack_kernel(dw, grad, gain, first, second, third, out):
    group, share, cols = out.shape[0], out.shape[1], dw.shape[2]
    block = sum(dw[i].astype(F32) for i in range(dw.shape[0]))
    out[:, :, :cols] = block.reshape(group, share, cols).astype(BF)
    end = cols + grad.shape[2]
    out[:, :, cols:end] = grad[...]
    high, low = split(gain[...] + first[...] + second[...] + third[...])
    ride = jnp.concatenate([high, low, high, low])
    out[:, :, end:] = jnp.broadcast_to(ride[None], (group, share, 128)).astype(BF)


def last_kernel(came, out, dw, dw_out, gain):
    frames = came.shape[0]
    part = out.shape[1]
    for s in range(3):
        dw[s] = jnp.sum(came[:, :, s * part : (s + 1) * part].astype(F32), axis=0)
    dw_out[...] = jnp.sum(came[:, :, 3 * part : 4 * part].astype(F32), axis=0)
    grad = [came[:, :, i * part : (i + 1) * part].astype(F32) for i in (4, 5)]
    out[...] = jnp.concatenate(grad, axis=1).reshape(out.shape).astype(BF)
    ride = jnp.sum(came[:, :, 6 * part :].astype(F32), axis=0)
    gain[...] = ride[0:2] + ride[2:4]


def call(kernel, args, outs, scratch=(), flops=0, mib=8, hbm=None):
    vmem = pl.BlockSpec(memory_space=pltpu.VMEM)
    in_specs, out_specs = [vmem] * len(args), [vmem] * len(outs)
    if args[0].dtype == jnp.int32:
        in_specs[0] = pl.BlockSpec(memory_space=pltpu.SMEM)
    if hbm is not None:
        start, end = hbm
        in_specs[start:] = [pl.BlockSpec(memory_space=pl.ANY)] * (len(args) - start)
        out_specs[:end] = [pl.BlockSpec(memory_space=pl.ANY)] * end
    shapes = [jax.ShapeDtypeStruct(s, d) for s, d in outs]
    moved = sum(a.size * a.dtype.itemsize for a in list(args) + shapes)
    return pl.pallas_call(
        kernel,
        out_shape=shapes,
        in_specs=in_specs,
        out_specs=out_specs,
        scratch_shapes=list(scratch),
        compiler_params=pltpu.CompilerParams(vmem_limit_bytes=mib * 2**20),
        cost_estimate=pl.CostEstimate(flops=flops, bytes_accessed=moved, transcendentals=0),
    )(*args)


def gain_kernel(keep, got, gain):
    rows = keep.shape[1] - SIDE
    for i in range(2):
        side = keep[i, rows:].astype(F32) + got[i, rows:].astype(F32)
        line = side[2:3] + side[3:4]
        gain[2 * i : 2 * i + 1] = line[:, :128]
        gain[2 * i + 1 : 2 * i + 2] = line[:, 128:]


def mid_kernel(keep, got, near, far, mid, gain):
    mid[...] = (keep[1].astype(F32) + got[1].astype(F32)).astype(BF)
    gain[...] = near[0:2] + far[...]


def per_device(acts, grad_in, gain, w_qkv, w_out):
    t = lax.axis_index("tensor")
    dp, tm = lax.axis_size("dp"), lax.axis_size("tm")
    part = acts.shape[3]
    rows = acts.shape[2]
    few = rows // tm
    width = w_qkv.shape[0]
    cols = w_qkv.shape[2]
    heads = cols // HD
    norm = (rows * dp * tm) ** (-0.5)
    idx = jnp.reshape(t, (1,)).astype(jnp.int32)

    own = jnp.stack([acts.reshape(tm, few, part), grad_in.reshape(tm, few, part)], axis=1)
    own = lax.all_to_all(own, "tm", split_axis=0, concat_axis=0, tiled=True)
    far = lax.ppermute(own, "tensor", CHIP)
    near = lax.ppermute(own, "tensor", CORE)
    cross = lax.ppermute(far, "tensor", CORE)

    gain_rows = gain.reshape(4, 1, part)
    w = jnp.transpose(w_qkv, (1, 0, 2)).reshape(3, 4, part, cols)
    message = ((2, rows + SIDE, part), BF)
    dw, send, keep, stats = call(
        functools.partial(main_kernel, heads, norm),
        (idx, gain_rows, own, near, far, cross, w, w_out),
        (((4, part, 4 * cols), BF), message, message, ((8, rows), F32)),
        (
            pltpu.VMEM((4,) + own.shape, BF),
            pltpu.VMEM(w.shape, BF),
            pltpu.VMEM(w_out.shape, BF),
            pltpu.VMEM((4, part, 4 * cols), BF),
            pltpu.VMEM((2, rows + SIDE, part), BF),
            pltpu.VMEM((2, rows + SIDE, part), BF),
            pltpu.VMEM((3, rows, cols), BF),
            pltpu.VMEM((4, rows, part), F32),
            pltpu.VMEM((4, rows, part), BF),
            pltpu.VMEM((4, rows, part), BF),
            pltpu.VMEM((rows, cols), BF),
            pltpu.SemaphoreType.DMA((10,)),
            pltpu.SemaphoreType.DMA((6,)),
        ),
        flops=7 * 10**9,
        mib=60,
        hbm=(2, 3),
    )

    dw = dw.reshape(dp, width // dp, 4 * cols)
    dw = lax.all_to_all(dw, "dp", split_axis=0, concat_axis=0, tiled=True)

    got = lax.ppermute(send, "tensor", CORE)
    (near_sum,) = call(gain_kernel, (keep, got), (((4, 128), F32),), flops=1000)
    far_sum = lax.ppermute(near_sum[2:], "tensor", CHIP)
    mid, gain_sum = call(
        mid_kernel,
        (keep, got, near_sum, far_sum),
        (((rows + SIDE, part), BF), ((2, 128), F32)),
        flops=1000,
    )
    last = lax.ppermute(mid, "tensor", CHIP)
    gain_sums = [gain_sum] + [
        lax.ppermute(gain_sum, "dp", [(i, i ^ bit) for i in range(dp)]) for bit in (1, 3, 2)
    ]
    (grad,) = call(
        acts_kernel,
        (idx, keep, got, last, stats, own, gain_rows),
        (((tm, 8, 2 * part), BF),),
        flops=10**6,
    )

    share = width // (dp * tm)
    total = 4 * cols + 2 * part + 128
    group = tm // 4
    pack = pl.pallas_call(
        pack_kernel,
        grid=(tm // group,),
        out_shape=jax.ShapeDtypeStruct((tm, share, total), BF),
        in_specs=[
            pl.BlockSpec((dp, group * share, 4 * cols), lambda i: (0, i, 0)),
            pl.BlockSpec((group, share, 2 * part), lambda i: (i, 0, 0)),
        ]
        + [pl.BlockSpec((2, 128), lambda i: (0, 0))] * 4,
        out_specs=pl.BlockSpec((group, share, total), lambda i: (i, 0, 0)),
        compiler_params=pltpu.CompilerParams(vmem_limit_bytes=8 * 2**20),
        cost_estimate=pl.CostEstimate(flops=10**6, bytes_accessed=10**6, transcendentals=0),
    )(dw, grad, *gain_sums)
    pack = lax.all_to_all(pack, "tm", split_axis=0, concat_axis=0, tiled=True)
    out, dw, dw_out, gain_sum = call(
        last_kernel,
        (pack,),
        (((rows, part), BF), ((3, share, cols), F32), ((share, cols), F32), ((2, 128), F32)),
        flops=10**7,
    )
    return (
        out.reshape(grad_in.shape),
        jnp.transpose(dw, (1, 0, 2)),
        dw_out,
        gain_sum.reshape(part),
    )


def solution(mesh):
    placed = (
        P("dp", "tm", None, "tensor"),
        P("dp", "tm", None, "tensor"),
        P(),
        P(None, None, "tensor"),
        P("tensor", None),
    )
    return jax.shard_map(
        per_device,
        mesh=mesh,
        in_specs=placed,
        out_specs=(
            P("dp", "tm", None, "tensor"),
            P(("dp", "tm"), None, "tensor"),
            P(("dp", "tm"), "tensor"),
            P("tensor"),
        ),
        check_vma=False,
    )
```

```python
import functools
import math

import jax
import jax.numpy as jnp
from jax import lax
from jax.experimental import pallas as pl
from jax.experimental.pallas import tpu as pltpu
from jax.sharding import PartitionSpec as P

HD = 64
EPS = 1e-05
CORE = [(0, 1), (1, 0), (2, 3), (3, 2)]
CHIP = [(0, 2), (2, 0), (1, 3), (3, 1)]
F32, BF = jnp.float32, jnp.bfloat16
SIDE = 32


def dot(a, b, contract):
    return lax.dot_general(a, b, (contract, ((), ())), preferred_element_type=F32)


def grouped(a):
    frames, few, part = a.shape
    a = a.astype(F32).reshape(frames, few // 8, 8, part)
    return jnp.concatenate([a[:, i].reshape(frames * 8, part) for i in range(few // 8)])


def attention(q, k, v, g, heads, scale):
    rows, cols = q.shape
    same = (
        lax.broadcasted_iota(jnp.int32, (rows, rows), 0) % 8
        == lax.broadcasted_iota(jnp.int32, (rows, rows), 1) % 8
    )
    lane = lax.broadcasted_iota(jnp.int32, (rows, cols), 1) // HD
    zero = jnp.zeros((rows, cols), BF)
    sums = [jnp.zeros((rows, cols), F32) for _ in range(4)]
    g_scaled = (g.astype(F32) * scale).astype(BF)
    for h in range(heads):
        qh, kh, vh, gh = [jnp.where(lane == h, a, zero) for a in (q, k, v, g)]
        scores = dot(q, kh, ((1,), (1,))) * (scale * math.log2(math.e))
        expd = jnp.exp2(jnp.where(same, scores, -1e30))
        prob = expd * (1.0 / jnp.sum(expd, axis=-1, keepdims=True))
        low = prob.astype(BF)
        dprob = dot(g_scaled, vh, ((1,), (1,)))
        delta = jnp.sum(low.astype(F32) * dprob, axis=-1, keepdims=True)
        ds = (prob * (dprob - delta)).astype(BF)
        sums[0] += dot(low, vh, ((1,), (0,)))
        sums[1] += dot(ds, kh, ((1,), (0,)))
        sums[2] += dot(ds, qh, ((0,), (0,)))
        sums[3] += dot(low, gh, ((0,), (0,)))
    return [a.astype(BF) for a in sums]


def split(a):
    high = a.astype(BF).astype(F32)
    return high, a - high


def main_kernel(
    heads, norm, gain, own, near, far, cross, w, w_out,
    dw_at, send_at, keep_at, stats,
    dw, send, keep, gqkv, xhat, normed, dy, attn, left,
):
    t = lax.axis_index("tensor")
    rows, part = normed.shape[1:]
    width = 4 * part
    pieces = (own, near, far, cross)
    x = [grouped(a[:, 0]) for a in pieces]
    mean = sum(jnp.sum(a, axis=-1, keepdims=True) for a in x) / width
    x = [a - mean for a in x]
    inv = lax.rsqrt(sum(jnp.sum(a * a, axis=-1, keepdims=True) for a in x) / width + EPS)
    for i in range(4):
        xhat[i] = x[i] * inv
        normed[i] = (xhat[i] * gain[t ^ i]).astype(BF)
    qkv = [
        sum(dot(normed[i], w[s, t ^ i], ((1,), (0,))) for i in range(4)).astype(BF)
        for s in range(3)
    ]
    for i in range(4):
        dy[i] = grouped(pieces[i][:, 1]).astype(BF)
    g = sum(
        dot(dy[i], w_out[:, pl.ds(pl.multiple_of((t ^ i) * part, part), part)], ((1,), (1,)))
        for i in range(4)
    ).astype(BF)
    half = rows // 2
    for i in range(2):
        span = slice(i * half, (i + 1) * half)
        parts = attention(*(a[span] for a in qkv), g[span], heads, HD ** (-0.5))
        attn[span] = parts[0]
        for s in range(3):
            gqkv[s, span] = parts[1 + s]
    first = jnp.zeros((rows, 1), F32)
    second = jnp.zeros((rows, 1), F32)
    outs = (keep.at[0], send.at[0], keep.at[1], send.at[1])
    gains = []
    for i in range(4):
        term = sum(dot(gqkv[s], w[s, t ^ i], ((1,), (1,))) for s in range(3)).astype(BF)
        outs[i][:rows] = term
        wide = term.astype(F32)
        product = wide * xhat[i]
        gains.append(jnp.sum(product, axis=0, keepdims=True) * norm)
        first += jnp.sum(wide * gain[t ^ i], axis=-1, keepdims=True)
        second += jnp.sum(product * gain[t ^ i], axis=-1, keepdims=True)
    lane = lax.broadcasted_iota(jnp.int32, (rows, 128), 1)
    moments = jnp.where(lane == 0, first / width, jnp.where(lane == 1, second / width, 0.0))
    moments = jnp.where(lane == 8, mean, jnp.where(lane == 9, inv, moments)).T
    stats[...] = moments[8:16]
    high, low = split(moments[:8])
    line = lax.broadcasted_iota(jnp.int32, (8, part), 0)
    for i in range(4):
        gain_high, gain_low = split(gains[i])
        top = jnp.where(line == 2, gain_high, jnp.where(line == 3, gain_low, high[:, :part]))
        side = [top, high[:, part:], low[:, :part], low[:, part:]]
        outs[i][rows:] = jnp.concatenate(side).astype(BF)
    copies = [
        pltpu.make_async_copy(send, send_at, left.at[4]),
        pltpu.make_async_copy(keep, keep_at, left.at[5]),
    ]
    for copy in copies:
        copy.start()
    cols = w.shape[3]
    for i in range(4):
        for s in range(3):
            block = dot(normed[i], gqkv[s], ((0,), (0,))) * norm
            dw[i, :, s * cols : (s + 1) * cols] = block.astype(BF)
        block = dot(dy[i], attn[...], ((0,), (0,))) * norm
        dw[i, :, 3 * cols :] = block.astype(BF)
        copies.append(pltpu.make_async_copy(dw.at[i], dw_at.at[t ^ i], left.at[i]))
        copies[-1].start()
    for copy in copies:
        copy.wait()


def acts_kernel(keep, got, last, stats, own, gain, out):
    t = lax.axis_index("tensor")
    frames, part = own.shape[0], own.shape[3]
    rows = stats.shape[1]
    total = keep[0].astype(F32) + got[0].astype(F32) + last[...].astype(F32)
    side = total[rows:]
    moments = jnp.concatenate([side[:8] + side[16:24], side[8:16] + side[24:]], axis=1)
    moments = jnp.concatenate([moments, stats[...], jnp.zeros((112, rows), F32)]).T
    first, second, mean, inv = [moments[:, i : i + 1] for i in (0, 1, 8, 9)]
    xhat = (grouped(own[:, 0]) - mean) * inv
    grad = grouped(own[:, 1]) + inv * (total[:rows] * gain[t] - first - xhat * second)
    half = frames * 8
    for i in range(2):
        block = grad[i * half : (i + 1) * half].reshape(frames, 8, part)
        out[:, :, i * part : (i + 1) * part] = block.astype(BF)


def pack_kernel(dw, grad, gain, first, second, third, out):
    group, share, cols = out.shape[0], out.shape[1], dw.shape[2]
    block = sum(dw[i].astype(F32) for i in range(dw.shape[0]))
    out[:, :, :cols] = block.reshape(group, share, cols).astype(BF)
    end = cols + grad.shape[2]
    out[:, :, cols:end] = grad[...]
    high, low = split(gain[...] + first[...] + second[...] + third[...])
    ride = jnp.concatenate([high, low, high, low])
    out[:, :, end:] = jnp.broadcast_to(ride[None], (group, share, 128)).astype(BF)


def last_kernel(came, out, dw, dw_out, gain):
    frames = came.shape[0]
    part = out.shape[1]
    for s in range(3):
        dw[s] = jnp.sum(came[:, :, s * part : (s + 1) * part].astype(F32), axis=0)
    dw_out[...] = jnp.sum(came[:, :, 3 * part : 4 * part].astype(F32), axis=0)
    grad = [came[:, :, i * part : (i + 1) * part].astype(F32) for i in (4, 5)]
    out[...] = jnp.concatenate(grad, axis=1).reshape(out.shape).astype(BF)
    ride = jnp.sum(came[:, :, 6 * part :].astype(F32), axis=0)
    gain[...] = ride[0:2] + ride[2:4]


def call(kernel, args, outs, scratch=(), flops=0, mib=8, copied=0):
    vmem, anywhere = [pl.BlockSpec(memory_space=a) for a in (pltpu.VMEM, pl.ANY)]
    shapes = [jax.ShapeDtypeStruct(s, d) for s, d in outs]
    moved = sum(a.size * a.dtype.itemsize for a in list(args) + shapes)
    return pl.pallas_call(
        kernel,
        out_shape=shapes,
        in_specs=[vmem] * len(args),
        out_specs=[anywhere] * copied + [vmem] * (len(outs) - copied),
        scratch_shapes=list(scratch),
        compiler_params=pltpu.CompilerParams(vmem_limit_bytes=mib * 2**20),
        cost_estimate=pl.CostEstimate(flops=flops, bytes_accessed=moved, transcendentals=0),
    )(*args)


def gain_kernel(keep, got, gain):
    rows = keep.shape[1] - SIDE
    for i in range(2):
        side = keep[i, rows:].astype(F32) + got[i, rows:].astype(F32)
        line = side[2:3] + side[3:4]
        gain[2 * i : 2 * i + 1] = line[:, :128]
        gain[2 * i + 1 : 2 * i + 2] = line[:, 128:]


def mid_kernel(keep, got, near, far, mid, gain):
    mid[...] = (keep[1].astype(F32) + got[1].astype(F32)).astype(BF)
    gain[...] = near[0:2] + far[...]


def per_device(acts, grad_in, gain, w_qkv, w_out):
    dp, tm = lax.axis_size("dp"), lax.axis_size("tm")
    part = acts.shape[3]
    rows = acts.shape[2]
    few = rows // tm
    width = w_qkv.shape[0]
    cols = w_qkv.shape[2]
    heads = cols // HD
    norm = (rows * dp * tm) ** (-0.5)

    own = jnp.stack([acts.reshape(tm, few, part), grad_in.reshape(tm, few, part)], axis=1)
    own = lax.all_to_all(own, "tm", split_axis=0, concat_axis=0, tiled=True)
    far = lax.ppermute(own, "tensor", CHIP)
    near = lax.ppermute(own, "tensor", CORE)
    cross = lax.ppermute(far, "tensor", CORE)

    gain_rows = gain.reshape(4, 1, part)
    w = jnp.transpose(w_qkv, (1, 0, 2)).reshape(3, 4, part, cols)
    message = ((2, rows + SIDE, part), BF)
    dw, send, keep, stats = call(
        functools.partial(main_kernel, heads, norm),
        (gain_rows, own, near, far, cross, w, w_out),
        (((4, part, 4 * cols), BF), message, message, ((8, rows), F32)),
        (
            pltpu.VMEM((4, part, 4 * cols), BF),
            pltpu.VMEM((2, rows + SIDE, part), BF),
            pltpu.VMEM((2, rows + SIDE, part), BF),
            pltpu.VMEM((3, rows, cols), BF),
            pltpu.VMEM((4, rows, part), F32),
            pltpu.VMEM((4, rows, part), BF),
            pltpu.VMEM((4, rows, part), BF),
            pltpu.VMEM((rows, cols), BF),
            pltpu.SemaphoreType.DMA((6,)),
        ),
        flops=7 * 10**9,
        mib=48,
        copied=3,
    )

    dw = dw.reshape(dp, width // dp, 4 * cols)
    dw = lax.all_to_all(dw, "dp", split_axis=0, concat_axis=0, tiled=True)

    got = lax.ppermute(send, "tensor", CORE)
    (near_sum,) = call(gain_kernel, (keep, got), (((4, 128), F32),), flops=1000)
    far_sum = lax.ppermute(near_sum[2:], "tensor", CHIP)
    mid, gain_sum = call(
        mid_kernel,
        (keep, got, near_sum, far_sum),
        (((rows + SIDE, part), BF), ((2, 128), F32)),
        flops=1000,
    )
    last = lax.ppermute(mid, "tensor", CHIP)
    gain_sums = [gain_sum] + [
        lax.ppermute(gain_sum, "dp", [(i, i ^ bit) for i in range(dp)]) for bit in (1, 3, 2)
    ]
    (grad,) = call(
        acts_kernel,
        (keep, got, last, stats, own, gain_rows),
        (((tm, 8, 2 * part), BF),),
        flops=10**6,
    )

    share = width // (dp * tm)
    total = 4 * cols + 2 * part + 128
    group = tm // 4
    pack = pl.pallas_call(
        pack_kernel,
        grid=(tm // group,),
        out_shape=jax.ShapeDtypeStruct((tm, share, total), BF),
        in_specs=[
            pl.BlockSpec((dp, group * share, 4 * cols), lambda i: (0, i, 0)),
            pl.BlockSpec((group, share, 2 * part), lambda i: (i, 0, 0)),
        ]
        + [pl.BlockSpec((2, 128), lambda i: (0, 0))] * 4,
        out_specs=pl.BlockSpec((group, share, total), lambda i: (i, 0, 0)),
        compiler_params=pltpu.CompilerParams(vmem_limit_bytes=8 * 2**20),
        cost_estimate=pl.CostEstimate(flops=10**6, bytes_accessed=10**6, transcendentals=0),
    )(dw, grad, *gain_sums)
    pack = lax.all_to_all(pack, "tm", split_axis=0, concat_axis=0, tiled=True)
    out, dw, dw_out, gain_sum = call(
        last_kernel,
        (pack,),
        (((rows, part), BF), ((3, share, cols), F32), ((share, cols), F32), ((2, 128), F32)),
        flops=10**7,
    )
    return (
        out.reshape(grad_in.shape),
        jnp.transpose(dw, (1, 0, 2)),
        dw_out,
        gain_sum.reshape(part),
    )


def solution(mesh):
    placed = (
        P("dp", "tm", None, "tensor"),
        P("dp", "tm", None, "tensor"),
        P(),
        P(None, None, "tensor"),
        P("tensor", None),
    )
    return jax.shard_map(
        per_device,
        mesh=mesh,
        in_specs=placed,
        out_specs=(
            P("dp", "tm", None, "tensor"),
            P(("dp", "tm"), None, "tensor"),
            P(("dp", "tm"), "tensor"),
            P("tensor"),
        ),
        check_vma=False,
    )
```

```python
import functools
import math

import jax
import jax.numpy as jnp
from jax import lax
from jax.experimental import pallas as pl
from jax.experimental.pallas import tpu as pltpu
from jax.sharding import PartitionSpec as P

HD = 64
EPS = 1e-05
CORE = [(0, 1), (1, 0), (2, 3), (3, 2)]
CHIP = [(0, 2), (2, 0), (1, 3), (3, 1)]
F32, BF = jnp.float32, jnp.bfloat16
SIDE = 32


def dot(a, b, contract):
    return lax.dot_general(a, b, (contract, ((), ())), preferred_element_type=F32)


def turned(a, ref, frames, few):
    columns = []
    for i in range(a.shape[1] // 128):
        ref[i] = a[:, i * 128 : (i + 1) * 128]
        parts = [ref[i, pl.ds(j, frames, stride=few), :] for j in range(few)]
        columns.append(jnp.concatenate(parts))
    return jnp.concatenate(columns, axis=1)


def attention(q, k, v, g, heads, scale, frames):
    rows, cols = q.shape
    lane = lax.broadcasted_iota(jnp.int32, (rows, cols), 1) // HD
    zero = jnp.zeros((rows, cols), BF)

    def stacked(a):
        return jnp.concatenate([jnp.where(lane == h, a, zero) for h in range(heads)])

    def folded(a):
        return sum(
            jnp.where(lane == h, a[h * rows : (h + 1) * rows], 0.0) for h in range(heads)
        )

    score_shape = (rows, heads * rows)
    row = lax.broadcasted_iota(jnp.int32, score_shape, 0)
    col = lax.broadcasted_iota(jnp.int32, score_shape, 1)
    same = row // frames == (col % rows) // frames
    head = col // rows

    def by_head(a, each):
        parts = [each(jnp.sum(jnp.where(head == h, a, 0.0), axis=-1, keepdims=True)) for h in range(heads)]
        out = jnp.broadcast_to(parts[0], score_shape)
        for h in range(1, heads):
            out = jnp.where(head == h, parts[h], out)
        return out

    k_stacked, v_stacked = stacked(k), stacked(v)
    scores = dot(q, k_stacked, ((1,), (1,))) * (scale * math.log2(math.e))
    expd = jnp.exp2(jnp.where(same, scores, -1e30))
    prob = expd * by_head(expd, lambda a: 1.0 / a)
    low = prob.astype(BF)
    g_scaled = (g.astype(F32) * scale).astype(BF)
    dprob = dot(g_scaled, v_stacked, ((1,), (1,)))
    delta = by_head(low.astype(F32) * dprob, lambda a: a)
    ds = (prob * (dprob - delta)).astype(BF)
    return [
        a.astype(BF)
        for a in (
            dot(low, v_stacked, ((1,), (0,))),
            dot(ds, k_stacked, ((1,), (0,))),
            folded(dot(ds, q, ((0,), (0,)))),
            folded(dot(low, g, ((0,), (0,)))),
        )
    ]


def split(a):
    high = a.astype(BF).astype(F32)
    return high, a - high


def main_kernel(
    heads, norm, gain, own, near, far, cross, w, w_out,
    dw_at, send_at, keep_at, stats,
    dw, send, keep, gqkv, xhat, normed, dy, attn, turn, left,
):
    t = lax.axis_index("tensor")
    rows, part = normed.shape[1:]
    width = 4 * part
    pieces = (own, near, far, cross)
    frames, _, few, _ = own.shape
    x = [a[:, 0].astype(F32).reshape(rows, part) for a in pieces]
    mean = sum(jnp.sum(a, axis=-1, keepdims=True) for a in x) / width
    x = [a - mean for a in x]
    inv = lax.rsqrt(sum(jnp.sum(a * a, axis=-1, keepdims=True) for a in x) / width + EPS)
    for i in range(4):
        xhat[i] = turned(x[i] * inv, turn.at[i], frames, few)
        normed[i] = (xhat[i] * gain[t ^ i]).astype(BF)
    qkv = [
        sum(dot(normed[i], w[s, t ^ i], ((1,), (0,))) for i in range(4)).astype(BF)
        for s in range(3)
    ]
    for i in range(4):
        natural = pieces[i][:, 1].astype(F32).reshape(rows, part)
        dy[i] = turned(natural, turn.at[4 + i], frames, few).astype(BF)
    g = sum(
        dot(dy[i], w_out[:, pl.ds(pl.multiple_of((t ^ i) * part, part), part)], ((1,), (1,)))
        for i in range(4)
    ).astype(BF)
    group = 2 * frames
    for i in range(0, rows, group):
        span = slice(i, i + group)
        parts = attention(*(a[span] for a in qkv), g[span], heads, HD ** (-0.5), frames)
        attn[span] = parts[0]
        for s in range(3):
            gqkv[s, span] = parts[1 + s]
    first = jnp.zeros((rows, 1), F32)
    second = jnp.zeros((rows, 1), F32)
    outs = (keep.at[0], send.at[0], keep.at[1], send.at[1])
    gains = []
    for i in range(4):
        term = sum(dot(gqkv[s], w[s, t ^ i], ((1,), (1,))) for s in range(3)).astype(BF)
        outs[i][:rows] = term
        wide = term.astype(F32)
        product = wide * xhat[i]
        gains.append(jnp.sum(product, axis=0, keepdims=True) * norm)
        first += jnp.sum(wide * gain[t ^ i], axis=-1, keepdims=True)
        second += jnp.sum(product * gain[t ^ i], axis=-1, keepdims=True)
    lane = lax.broadcasted_iota(jnp.int32, (rows, 128), 1)
    stats[...] = jnp.where(lane == 0, mean, jnp.where(lane == 1, inv, 0.0)).T[:8]
    moments = jnp.where(lane == 0, first / width, jnp.where(lane == 1, second / width, 0.0)).T
    high, low = split(moments[:8])
    line = lax.broadcasted_iota(jnp.int32, (8, part), 0)
    for i in range(4):
        gain_high, gain_low = split(gains[i])
        top = jnp.where(line == 2, gain_high, jnp.where(line == 3, gain_low, high[:, :part]))
        side = [top, high[:, part:], low[:, :part], low[:, part:]]
        outs[i][rows:] = jnp.concatenate(side).astype(BF)
    copies = [
        pltpu.make_async_copy(send, send_at, left.at[4]),
        pltpu.make_async_copy(keep, keep_at, left.at[5]),
    ]
    for copy in copies:
        copy.start()
    cols = w.shape[3]
    for i in range(4):
        for s in range(3):
            block = dot(normed[i], gqkv[s], ((0,), (0,))) * norm
            dw[i, :, s * cols : (s + 1) * cols] = block.astype(BF)
        block = dot(dy[i], attn[...], ((0,), (0,))) * norm
        dw[i, :, 3 * cols :] = block.astype(BF)
        copies.append(pltpu.make_async_copy(dw.at[i], dw_at.at[t ^ i], left.at[i]))
        copies[-1].start()
    for copy in copies:
        copy.wait()


def acts_kernel(keep, got, last, stats, own, gain, out, turn):
    t = lax.axis_index("tensor")
    frames, _, few, part = own.shape
    rows = frames * few
    total = keep[0].astype(F32) + got[0].astype(F32) + last[...].astype(F32)
    side = total[rows:]
    moments = jnp.concatenate([side[:8] + side[16:24], side[8:16] + side[24:]], axis=1)
    pad = jnp.zeros((120, rows), F32)
    columns = jnp.concatenate([moments, pad]).T
    total = turned(jnp.concatenate([total[:rows], columns], axis=1), turn, few, frames)
    first, second = total[:, part : part + 1], total[:, part + 1 : part + 2]
    columns = jnp.concatenate([stats[...], pad]).T
    mean, inv = columns[:, 0:1], columns[:, 1:2]
    xhat = (own[:, 0].astype(F32).reshape(rows, part) - mean) * inv
    grad = own[:, 1].astype(F32).reshape(rows, part)
    grad = grad + inv * (total[:, :part] * gain[t] - first - xhat * second)
    grad = grad.reshape(frames, few, part)
    for i in range(few // 8):
        out[:, :, i * part : (i + 1) * part] = grad[:, i * 8 : (i + 1) * 8].astype(BF)


def pack_kernel(dw, grad, gain, first, second, third, out):
    group, share, cols = out.shape[0], out.shape[1], dw.shape[2]
    block = sum(dw[i].astype(F32) for i in range(dw.shape[0]))
    out[:, :, :cols] = block.reshape(group, share, cols).astype(BF)
    end = cols + grad.shape[2]
    out[:, :, cols:end] = grad[...]
    high, low = split(gain[...] + first[...] + second[...] + third[...])
    ride = jnp.concatenate([high, low, high, low])
    out[:, :, end:] = jnp.broadcast_to(ride[None], (group, share, 128)).astype(BF)


def last_kernel(came, out, dw, dw_out, gain):
    frames = came.shape[0]
    part = out.shape[1]
    for s in range(3):
        dw[s] = jnp.sum(came[:, :, s * part : (s + 1) * part].astype(F32), axis=0)
    dw_out[...] = jnp.sum(came[:, :, 3 * part : 4 * part].astype(F32), axis=0)
    grad = [came[:, :, i * part : (i + 1) * part].astype(F32) for i in (4, 5)]
    out[...] = jnp.concatenate(grad, axis=1).reshape(out.shape).astype(BF)
    ride = jnp.sum(came[:, :, 6 * part :].astype(F32), axis=0)
    gain[...] = ride[0:2] + ride[2:4]


def call(kernel, args, outs, scratch=(), flops=0, mib=8, copied=0):
    vmem, anywhere = [pl.BlockSpec(memory_space=a) for a in (pltpu.VMEM, pl.ANY)]
    shapes = [jax.ShapeDtypeStruct(s, d) for s, d in outs]
    moved = sum(a.size * a.dtype.itemsize for a in list(args) + shapes)
    return pl.pallas_call(
        kernel,
        out_shape=shapes,
        in_specs=[vmem] * len(args),
        out_specs=[anywhere] * copied + [vmem] * (len(outs) - copied),
        scratch_shapes=list(scratch),
        compiler_params=pltpu.CompilerParams(vmem_limit_bytes=mib * 2**20),
        cost_estimate=pl.CostEstimate(flops=flops, bytes_accessed=moved, transcendentals=0),
    )(*args)


def gain_kernel(keep, got, gain):
    rows = keep.shape[1] - SIDE
    for i in range(2):
        side = keep[i, rows:].astype(F32) + got[i, rows:].astype(F32)
        line = side[2:3] + side[3:4]
        gain[2 * i : 2 * i + 1] = line[:, :128]
        gain[2 * i + 1 : 2 * i + 2] = line[:, 128:]


def mid_kernel(keep, got, near, far, mid, gain):
    mid[...] = (keep[1].astype(F32) + got[1].astype(F32)).astype(BF)
    gain[...] = near[0:2] + far[...]


def per_device(acts, grad_in, gain, w_qkv, w_out):
    dp, tm = lax.axis_size("dp"), lax.axis_size("tm")
    part = acts.shape[3]
    rows = acts.shape[2]
    few = rows // tm
    width = w_qkv.shape[0]
    cols = w_qkv.shape[2]
    heads = cols // HD
    norm = (rows * dp * tm) ** (-0.5)

    own = jnp.stack([acts.reshape(tm, few, part), grad_in.reshape(tm, few, part)], axis=1)
    own = lax.all_to_all(own, "tm", split_axis=0, concat_axis=0, tiled=True)
    far = lax.ppermute(own, "tensor", CHIP)
    near = lax.ppermute(own, "tensor", CORE)
    cross = lax.ppermute(far, "tensor", CORE)

    gain_rows = gain.reshape(4, 1, part)
    w = jnp.transpose(w_qkv, (1, 0, 2)).reshape(3, 4, part, cols)
    message = ((2, rows + SIDE, part), BF)
    dw, send, keep, stats = call(
        functools.partial(main_kernel, heads, norm),
        (gain_rows, own, near, far, cross, w, w_out),
        (((4, part, 4 * cols), BF), message, message, ((8, rows), F32)),
        (
            pltpu.VMEM((4, part, 4 * cols), BF),
            pltpu.VMEM((2, rows + SIDE, part), BF),
            pltpu.VMEM((2, rows + SIDE, part), BF),
            pltpu.VMEM((3, rows, cols), BF),
            pltpu.VMEM((4, rows, part), F32),
            pltpu.VMEM((4, rows, part), BF),
            pltpu.VMEM((4, rows, part), BF),
            pltpu.VMEM((rows, cols), BF),
            pltpu.VMEM((8, part // 128, rows, 128), F32),
            pltpu.SemaphoreType.DMA((6,)),
        ),
        flops=7 * 10**9,
        mib=48,
        copied=3,
    )

    dw = dw.reshape(dp, width // dp, 4 * cols)
    dw = lax.all_to_all(dw, "dp", split_axis=0, concat_axis=0, tiled=True)

    got = lax.ppermute(send, "tensor", CORE)
    (near_sum,) = call(gain_kernel, (keep, got), (((4, 128), F32),), flops=1000)
    far_sum = lax.ppermute(near_sum[2:], "tensor", CHIP)
    mid, gain_sum = call(
        mid_kernel,
        (keep, got, near_sum, far_sum),
        (((rows + SIDE, part), BF), ((2, 128), F32)),
        flops=1000,
    )
    last = lax.ppermute(mid, "tensor", CHIP)
    gain_sums = [gain_sum] + [
        lax.ppermute(gain_sum, "dp", [(i, i ^ bit) for i in range(dp)]) for bit in (1, 3, 2)
    ]
    (grad,) = call(
        acts_kernel,
        (keep, got, last, stats, own, gain_rows),
        (((tm, 8, 2 * part), BF),),
        (pltpu.VMEM((part // 128 + 1, rows, 128), F32),),
        flops=10**6,
    )

    share = width // (dp * tm)
    total = 4 * cols + 2 * part + 128
    group = tm // 4
    pack = pl.pallas_call(
        pack_kernel,
        grid=(tm // group,),
        out_shape=jax.ShapeDtypeStruct((tm, share, total), BF),
        in_specs=[
            pl.BlockSpec((dp, group * share, 4 * cols), lambda i: (0, i, 0)),
            pl.BlockSpec((group, share, 2 * part), lambda i: (i, 0, 0)),
        ]
        + [pl.BlockSpec((2, 128), lambda i: (0, 0))] * 4,
        out_specs=pl.BlockSpec((group, share, total), lambda i: (i, 0, 0)),
        compiler_params=pltpu.CompilerParams(vmem_limit_bytes=8 * 2**20),
        cost_estimate=pl.CostEstimate(flops=10**6, bytes_accessed=10**6, transcendentals=0),
    )(dw, grad, *gain_sums)
    pack = lax.all_to_all(pack, "tm", split_axis=0, concat_axis=0, tiled=True)
    out, dw, dw_out, gain_sum = call(
        last_kernel,
        (pack,),
        (((rows, part), BF), ((3, share, cols), F32), ((share, cols), F32), ((2, 128), F32)),
        flops=10**7,
    )
    return (
        out.reshape(grad_in.shape),
        jnp.transpose(dw, (1, 0, 2)),
        dw_out,
        gain_sum.reshape(part),
    )


def solution(mesh):
    placed = (
        P("dp", "tm", None, "tensor"),
        P("dp", "tm", None, "tensor"),
        P(),
        P(None, None, "tensor"),
        P("tensor", None),
    )
    return jax.shard_map(
        per_device,
        mesh=mesh,
        in_specs=placed,
        out_specs=(
            P("dp", "tm", None, "tensor"),
            P(("dp", "tm"), None, "tensor"),
            P(("dp", "tm"), "tensor"),
            P("tensor"),
        ),
        check_vma=False,
    )
```

```python
import functools
import math

import jax
import jax.numpy as jnp
from jax import lax
from jax.experimental import pallas as pl
from jax.experimental.pallas import tpu as pltpu
from jax.sharding import PartitionSpec as P

HD = 64
EPS = 1e-05
CORE = [(0, 1), (1, 0), (2, 3), (3, 2)]
CHIP = [(0, 2), (2, 0), (1, 3), (3, 1)]
BOTH = [(0, 3), (3, 0), (1, 2), (2, 1)]
F32, BF = jnp.float32, jnp.bfloat16
SIDE = 32


def dot(a, b, contract):
    return lax.dot_general(a, b, (contract, ((), ())), preferred_element_type=F32)


def grouped(a):
    frames, few, part = a.shape
    a = a.astype(F32).reshape(frames, few // 8, 8, part)
    return jnp.concatenate([a[:, i].reshape(frames * 8, part) for i in range(few // 8)])


def attention(q, k, v, g, heads, scale):
    rows, cols = q.shape
    same = (
        lax.broadcasted_iota(jnp.int32, (rows, rows), 0) % 8
        == lax.broadcasted_iota(jnp.int32, (rows, rows), 1) % 8
    )
    lane = lax.broadcasted_iota(jnp.int32, (rows, cols), 1) // HD
    zero = jnp.zeros((rows, cols), BF)
    sums = [jnp.zeros((rows, cols), F32) for _ in range(4)]
    g_scaled = (g.astype(F32) * scale).astype(BF)
    for h in range(heads):
        qh, kh, vh, gh = [jnp.where(lane == h, a, zero) for a in (q, k, v, g)]
        scores = dot(q, kh, ((1,), (1,))) * (scale * math.log2(math.e))
        expd = jnp.exp2(jnp.where(same, scores, -1e30))
        prob = expd * (1.0 / jnp.sum(expd, axis=-1, keepdims=True))
        low = prob.astype(BF)
        dprob = dot(g_scaled, vh, ((1,), (1,)))
        delta = jnp.sum(low.astype(F32) * dprob, axis=-1, keepdims=True)
        ds = (prob * (dprob - delta)).astype(BF)
        sums[0] += dot(low, vh, ((1,), (0,)))
        sums[1] += dot(ds, kh, ((1,), (0,)))
        sums[2] += dot(ds, qh, ((0,), (0,)))
        sums[3] += dot(low, gh, ((0,), (0,)))
    return [a.astype(BF) for a in sums]


def split(a):
    high = a.astype(BF).astype(F32)
    return high, a - high


def main_kernel(
    heads, norm, gain, own, near, far, cross, w, w_out,
    dw_at, send_at, keep, stats, far_gain, cross_gain,
    dw, send, gqkv, xhat, normed, dy, attn, left,
):
    t = lax.axis_index("tensor")
    rows, part = normed.shape[1:]
    width = 4 * part
    pieces = (own, near, far, cross)
    x = [grouped(a[:, 0]) for a in pieces]
    mean = sum(jnp.sum(a, axis=-1, keepdims=True) for a in x) / width
    x = [a - mean for a in x]
    inv = lax.rsqrt(sum(jnp.sum(a * a, axis=-1, keepdims=True) for a in x) / width + EPS)
    for i in range(4):
        xhat[i] = x[i] * inv
        normed[i] = (xhat[i] * gain[t ^ i]).astype(BF)
    qkv = [
        sum(dot(normed[i], w[s, t ^ i], ((1,), (0,))) for i in range(4)).astype(BF)
        for s in range(3)
    ]
    for i in range(4):
        dy[i] = grouped(pieces[i][:, 1]).astype(BF)
    g = sum(
        dot(dy[i], w_out[:, pl.ds(pl.multiple_of((t ^ i) * part, part), part)], ((1,), (1,)))
        for i in range(4)
    ).astype(BF)
    half = rows // 2
    for i in range(2):
        span = slice(i * half, (i + 1) * half)
        parts = attention(*(a[span] for a in qkv), g[span], heads, HD ** (-0.5))
        attn[span] = parts[0]
        for s in range(3):
            gqkv[s, span] = parts[1 + s]
    first = jnp.zeros((rows, 1), F32)
    second = jnp.zeros((rows, 1), F32)
    outs = (keep.at[0], send.at[0], keep.at[1], send.at[1])
    gains = []
    for i in range(4):
        term = sum(dot(gqkv[s], w[s, t ^ i], ((1,), (1,))) for s in range(3)).astype(BF)
        outs[i][:rows] = term
        wide = term.astype(F32)
        product = wide * xhat[i]
        gains.append(jnp.sum(product, axis=0, keepdims=True) * norm)
        first += jnp.sum(wide * gain[t ^ i], axis=-1, keepdims=True)
        second += jnp.sum(product * gain[t ^ i], axis=-1, keepdims=True)
    for ref, line in ((far_gain, gains[2]), (cross_gain, gains[3])):
        ref[0:1] = line[:, :128]
        ref[1:2] = line[:, 128:]
    lane = lax.broadcasted_iota(jnp.int32, (rows, 128), 1)
    moments = jnp.where(lane == 0, first / width, jnp.where(lane == 1, second / width, 0.0))
    moments = jnp.where(lane == 8, mean, jnp.where(lane == 9, inv, moments)).T
    stats[...] = moments[8:16]
    high, low = split(moments[:8])
    line = lax.broadcasted_iota(jnp.int32, (8, part), 0)
    for i in range(4):
        gain_high, gain_low = split(gains[i])
        top = jnp.where(line == 2, gain_high, jnp.where(line == 3, gain_low, high[:, :part]))
        side = [top, high[:, part:], low[:, :part], low[:, part:]]
        outs[i][rows:] = jnp.concatenate(side).astype(BF)
    copies = [pltpu.make_async_copy(send, send_at, left.at[4])]
    copies[0].start()
    cols = w.shape[3]
    for i in range(4):
        for s in range(3):
            block = dot(normed[i], gqkv[s], ((0,), (0,))) * norm
            dw[i, :, s * cols : (s + 1) * cols] = block.astype(BF)
        block = dot(dy[i], attn[...], ((0,), (0,))) * norm
        dw[i, :, 3 * cols :] = block.astype(BF)
        copies.append(pltpu.make_async_copy(dw.at[i], dw_at.at[t ^ i], left.at[i]))
        copies[-1].start()
    for copy in copies:
        copy.wait()


def acts_kernel(keep, got, last, stats, own, gain, out):
    t = lax.axis_index("tensor")
    frames, part = own.shape[0], own.shape[3]
    rows = stats.shape[1]
    total = keep[0].astype(F32) + got[0].astype(F32) + last[...].astype(F32)
    side = total[rows:]
    moments = jnp.concatenate([side[:8] + side[16:24], side[8:16] + side[24:]], axis=1)
    moments = jnp.concatenate([moments, stats[...], jnp.zeros((112, rows), F32)]).T
    first, second, mean, inv = [moments[:, i : i + 1] for i in (0, 1, 8, 9)]
    xhat = (grouped(own[:, 0]) - mean) * inv
    grad = grouped(own[:, 1]) + inv * (total[:rows] * gain[t] - first - xhat * second)
    half = frames * 8
    for i in range(2):
        block = grad[i * half : (i + 1) * half].reshape(frames, 8, part)
        out[:, :, i * part : (i + 1) * part] = block.astype(BF)


def pack_kernel(dw, grad, gain, first, second, third, out):
    group, share, cols = out.shape[0], out.shape[1], dw.shape[2]
    block = sum(dw[i].astype(F32) for i in range(dw.shape[0]))
    out[:, :, :cols] = block.reshape(group, share, cols).astype(BF)
    end = cols + grad.shape[2]
    out[:, :, cols:end] = grad[...]
    high, low = split(gain[...] + first[...] + second[...] + third[...])
    ride = jnp.concatenate([high, low, high, low])
    out[:, :, end:] = jnp.broadcast_to(ride[None], (group, share, 128)).astype(BF)


def last_kernel(came, out, dw, dw_out, gain):
    frames = came.shape[0]
    part = out.shape[1]
    for s in range(3):
        dw[s] = jnp.sum(came[:, :, s * part : (s + 1) * part].astype(F32), axis=0)
    dw_out[...] = jnp.sum(came[:, :, 3 * part : 4 * part].astype(F32), axis=0)
    grad = [came[:, :, i * part : (i + 1) * part].astype(F32) for i in (4, 5)]
    out[...] = jnp.concatenate(grad, axis=1).reshape(out.shape).astype(BF)
    ride = jnp.sum(came[:, :, 6 * part :].astype(F32), axis=0)
    gain[...] = ride[0:2] + ride[2:4]


def call(kernel, args, outs, scratch=(), flops=0, mib=8, copied=0):
    vmem, hbm = [pl.BlockSpec(memory_space=a) for a in (pltpu.VMEM, pltpu.HBM)]
    shapes = [
        pltpu.HBM(s, d) if i < copied else jax.ShapeDtypeStruct(s, d)
        for i, (s, d) in enumerate(outs)
    ]
    moved = sum(math.prod(a.shape) * a.dtype.itemsize for a in list(args) + shapes)
    return pl.pallas_call(
        kernel,
        out_shape=shapes,
        in_specs=[vmem] * len(args),
        out_specs=[hbm] * copied + [vmem] * (len(outs) - copied),
        scratch_shapes=list(scratch),
        compiler_params=pltpu.CompilerParams(vmem_limit_bytes=mib * 2**20),
        cost_estimate=pl.CostEstimate(flops=flops, bytes_accessed=moved, transcendentals=0),
    )(*args)


def mid_kernel(keep, got, far, cross, mid, gain):
    mid[...] = (keep[1].astype(F32) + got[1].astype(F32)).astype(BF)
    rows = keep.shape[1] - SIDE
    side = keep[0, rows:].astype(F32) + got[0, rows:].astype(F32)
    line = side[2:3] + side[3:4]
    gain[0:1] = line[:, :128] + far[0:1] + cross[0:1]
    gain[1:2] = line[:, 128:] + far[1:2] + cross[1:2]


def per_device(acts, grad_in, gain, w_qkv, w_out):
    dp, tm = lax.axis_size("dp"), lax.axis_size("tm")
    part = acts.shape[3]
    rows = acts.shape[2]
    few = rows // tm
    width = w_qkv.shape[0]
    cols = w_qkv.shape[2]
    heads = cols // HD
    norm = (rows * dp * tm) ** (-0.5)

    own = jnp.stack([acts.reshape(tm, few, part), grad_in.reshape(tm, few, part)], axis=1)
    own = lax.all_to_all(own, "tm", split_axis=0, concat_axis=0, tiled=True)
    far = lax.ppermute(own, "tensor", CHIP)
    near = lax.ppermute(own, "tensor", CORE)
    cross = lax.ppermute(far, "tensor", CORE)

    gain_rows = gain.reshape(4, 1, part)
    w = jnp.transpose(w_qkv, (1, 0, 2)).reshape(3, 4, part, cols)
    message = ((2, rows + SIDE, part), BF)
    dw, send, keep, stats, far_gain, cross_gain = call(
        functools.partial(main_kernel, heads, norm),
        (gain_rows, own, near, far, cross, w, w_out),
        (
            ((4, part, 4 * cols), BF),
            message,
            message,
            ((8, rows), F32),
            ((2, 128), F32),
            ((2, 128), F32),
        ),
        (
            pltpu.VMEM((4, part, 4 * cols), BF),
            pltpu.VMEM((2, rows + SIDE, part), BF),
            pltpu.VMEM((3, rows, cols), BF),
            pltpu.VMEM((4, rows, part), F32),
            pltpu.VMEM((4, rows, part), BF),
            pltpu.VMEM((4, rows, part), BF),
            pltpu.VMEM((rows, cols), BF),
            pltpu.SemaphoreType.DMA((5,)),
        ),
        flops=7 * 10**9,
        mib=36,
        copied=2,
    )

    dw = dw.reshape(dp, width // dp, 4 * cols)
    dw = lax.all_to_all(dw, "dp", split_axis=0, concat_axis=0, tiled=True)

    far_gain = lax.ppermute(far_gain, "tensor", CHIP)
    cross_gain = lax.ppermute(cross_gain, "tensor", BOTH)
    got = lax.ppermute(send, "tensor", CORE)
    mid, gain_sum = call(
        mid_kernel,
        (keep, got, far_gain, cross_gain),
        (((rows + SIDE, part), BF), ((2, 128), F32)),
        flops=1000,
    )
    last = lax.ppermute(mid, "tensor", CHIP)
    gain_sums = [gain_sum] + [
        lax.ppermute(gain_sum, "dp", [(i, i ^ bit) for i in range(dp)]) for bit in (1, 3, 2)
    ]
    (grad,) = call(
        acts_kernel,
        (keep, got, last, stats, own, gain_rows),
        (((tm, 8, 2 * part), BF),),
        flops=10**6,
    )

    share = width // (dp * tm)
    total = 4 * cols + 2 * part + 128
    group = tm // 4
    pack = pl.pallas_call(
        pack_kernel,
        grid=(tm // group,),
        out_shape=jax.ShapeDtypeStruct((tm, share, total), BF),
        in_specs=[
            pl.BlockSpec((dp, group * share, 4 * cols), lambda i: (0, i, 0)),
            pl.BlockSpec((group, share, 2 * part), lambda i: (i, 0, 0)),
        ]
        + [pl.BlockSpec((2, 128), lambda i: (0, 0))] * 4,
        out_specs=pl.BlockSpec((group, share, total), lambda i: (i, 0, 0)),
        compiler_params=pltpu.CompilerParams(vmem_limit_bytes=8 * 2**20),
        cost_estimate=pl.CostEstimate(flops=10**6, bytes_accessed=10**6, transcendentals=0),
    )(dw, grad, *gain_sums)
    pack = lax.all_to_all(pack, "tm", split_axis=0, concat_axis=0, tiled=True)
    out, dw, dw_out, gain_sum = call(
        last_kernel,
        (pack,),
        (((rows, part), BF), ((3, share, cols), F32), ((share, cols), F32), ((2, 128), F32)),
        flops=10**7,
    )
    return (
        out.reshape(grad_in.shape),
        jnp.transpose(dw, (1, 0, 2)),
        dw_out,
        gain_sum.reshape(part),
    )


def solution(mesh):
    placed = (
        P("dp", "tm", None, "tensor"),
        P("dp", "tm", None, "tensor"),
        P(),
        P(None, None, "tensor"),
        P("tensor", None),
    )
    return jax.shard_map(
        per_device,
        mesh=mesh,
        in_specs=placed,
        out_specs=(
            P("dp", "tm", None, "tensor"),
            P(("dp", "tm"), None, "tensor"),
            P(("dp", "tm"), "tensor"),
            P("tensor"),
        ),
        check_vma=False,
    )
```

```python
import functools
import math

import jax
import jax.numpy as jnp
from jax import lax
from jax.experimental import pallas as pl
from jax.experimental.pallas import tpu as pltpu
from jax.sharding import PartitionSpec as P

HD = 64
EPS = 1e-05
CORE = [(0, 1), (1, 0), (2, 3), (3, 2)]
CHIP = [(0, 2), (2, 0), (1, 3), (3, 1)]
F32, BF = jnp.float32, jnp.bfloat16
SIDE = 32


def dot(a, b, contract):
    return lax.dot_general(a, b, (contract, ((), ())), preferred_element_type=F32)


def grouped(a):
    frames, few, part = a.shape
    a = a.astype(F32).reshape(frames, few // 8, 8, part)
    return jnp.concatenate([a[:, i].reshape(frames * 8, part) for i in range(few // 8)])


def attention(q, k, v, g, heads, scale):
    rows, cols = q.shape
    same = (
        lax.broadcasted_iota(jnp.int32, (rows, rows), 0) % 8
        == lax.broadcasted_iota(jnp.int32, (rows, rows), 1) % 8
    )
    lane = lax.broadcasted_iota(jnp.int32, (rows, cols), 1) // HD
    zero = jnp.zeros((rows, cols), BF)
    sums = [jnp.zeros((rows, cols), F32) for _ in range(4)]
    g_scaled = (g.astype(F32) * scale).astype(BF)
    for h in range(heads):
        qh, kh, vh, gh = [jnp.where(lane == h, a, zero) for a in (q, k, v, g)]
        scores = dot(q, kh, ((1,), (1,))) * (scale * math.log2(math.e))
        expd = jnp.exp2(jnp.where(same, scores, -1e30))
        prob = expd * (1.0 / jnp.sum(expd, axis=-1, keepdims=True))
        low = prob.astype(BF)
        dprob = dot(g_scaled, vh, ((1,), (1,)))
        delta = jnp.sum(low.astype(F32) * dprob, axis=-1, keepdims=True)
        ds = (prob * (dprob - delta)).astype(BF)
        sums[0] += dot(low, vh, ((1,), (0,)))
        sums[1] += dot(ds, kh, ((1,), (0,)))
        sums[2] += dot(ds, qh, ((0,), (0,)))
        sums[3] += dot(low, gh, ((0,), (0,)))
    return [a.astype(BF) for a in sums]


def split(a):
    high = a.astype(BF).astype(F32)
    return high, a - high


def main_kernel(
    heads, norm, gain, own, near, far, cross, w, w_out,
    dw_at, send_at, keep, stats,
    dw, send, gqkv, xhat, normed, dy, attn, left,
):
    t = lax.axis_index("tensor")
    rows, part = normed.shape[1:]
    width = 4 * part
    pieces = (own, near, far, cross)
    x = [grouped(a[:, 0]) for a in pieces]
    mean = sum(jnp.sum(a, axis=-1, keepdims=True) for a in x) / width
    x = [a - mean for a in x]
    inv = lax.rsqrt(sum(jnp.sum(a * a, axis=-1, keepdims=True) for a in x) / width + EPS)
    for i in range(4):
        xhat[i] = x[i] * inv
        normed[i] = (xhat[i] * gain[t ^ i]).astype(BF)
    qkv = [
        sum(dot(normed[i], w[s, t ^ i], ((1,), (0,))) for i in range(4)).astype(BF)
        for s in range(3)
    ]
    for i in range(4):
        dy[i] = grouped(pieces[i][:, 1]).astype(BF)
    g = sum(
        dot(dy[i], w_out[:, pl.ds(pl.multiple_of((t ^ i) * part, part), part)], ((1,), (1,)))
        for i in range(4)
    ).astype(BF)
    half = rows // 2
    for i in range(2):
        span = slice(i * half, (i + 1) * half)
        parts = attention(*(a[span] for a in qkv), g[span], heads, HD ** (-0.5))
        attn[span] = parts[0]
        for s in range(3):
            gqkv[s, span] = parts[1 + s]
    first = jnp.zeros((rows, 1), F32)
    second = jnp.zeros((rows, 1), F32)
    outs = (keep.at[0], send.at[0], keep.at[1], send.at[1])
    gains = []
    for i in range(4):
        term = sum(dot(gqkv[s], w[s, t ^ i], ((1,), (1,))) for s in range(3)).astype(BF)
        outs[i][:rows] = term
        wide = term.astype(F32)
        product = wide * xhat[i]
        gains.append(jnp.sum(product, axis=0, keepdims=True) * norm)
        first += jnp.sum(wide * gain[t ^ i], axis=-1, keepdims=True)
        second += jnp.sum(product * gain[t ^ i], axis=-1, keepdims=True)
    lane = lax.broadcasted_iota(jnp.int32, (rows, 128), 1)
    moments = jnp.where(lane == 0, first / width, jnp.where(lane == 1, second / width, 0.0))
    moments = jnp.where(lane == 8, mean, jnp.where(lane == 9, inv, moments)).T
    stats[...] = moments[8:16]
    high, low = split(moments[:8])
    line = lax.broadcasted_iota(jnp.int32, (8, part), 0)
    for i in range(4):
        gain_high, gain_low = split(gains[i])
        top = jnp.where(line == 2, gain_high, jnp.where(line == 3, gain_low, high[:, :part]))
        side = [top, high[:, part:], low[:, :part], low[:, part:]]
        outs[i][rows:] = jnp.concatenate(side).astype(BF)
    copies = [pltpu.make_async_copy(send, send_at, left.at[4])]
    copies[0].start()
    cols = w.shape[3]
    for i in range(4):
        for s in range(3):
            block = dot(normed[i], gqkv[s], ((0,), (0,))) * norm
            dw[i, :, s * cols : (s + 1) * cols] = block.astype(BF)
        block = dot(dy[i], attn[...], ((0,), (0,))) * norm
        dw[i, :, 3 * cols :] = block.astype(BF)
        copies.append(pltpu.make_async_copy(dw.at[i], dw_at.at[t ^ i], left.at[i]))
        copies[-1].start()
    for copy in copies:
        copy.wait()


def acts_kernel(keep, got, last, stats, own, gain, out):
    t = lax.axis_index("tensor")
    frames, part = own.shape[0], own.shape[3]
    rows = stats.shape[1]
    total = keep[0].astype(F32) + got[0].astype(F32) + last[...].astype(F32)
    side = total[rows:]
    moments = jnp.concatenate([side[:8] + side[16:24], side[8:16] + side[24:]], axis=1)
    moments = jnp.concatenate([moments, stats[...], jnp.zeros((112, rows), F32)]).T
    first, second, mean, inv = [moments[:, i : i + 1] for i in (0, 1, 8, 9)]
    xhat = (grouped(own[:, 0]) - mean) * inv
    grad = grouped(own[:, 1]) + inv * (total[:rows] * gain[t] - first - xhat * second)
    half = frames * 8
    for i in range(2):
        block = grad[i * half : (i + 1) * half].reshape(frames, 8, part)
        out[:, :, i * part : (i + 1) * part] = block.astype(BF)


def pack_kernel(dw, grad, gain, first, second, third, out):
    group, share, cols = out.shape[0], out.shape[1], dw.shape[2]
    block = sum(dw[i].astype(F32) for i in range(dw.shape[0]))
    out[:, :, :cols] = block.reshape(group, share, cols).astype(BF)
    end = cols + grad.shape[2]
    out[:, :, cols:end] = grad[...]
    high, low = split(gain[...] + first[...] + second[...] + third[...])
    ride = jnp.concatenate([high, low, high, low])
    out[:, :, end:] = jnp.broadcast_to(ride[None], (group, share, 128)).astype(BF)


def last_kernel(came, out, dw, dw_out, gain):
    frames = came.shape[0]
    part = out.shape[1]
    for s in range(3):
        dw[s] = jnp.sum(came[:, :, s * part : (s + 1) * part].astype(F32), axis=0)
    dw_out[...] = jnp.sum(came[:, :, 3 * part : 4 * part].astype(F32), axis=0)
    grad = [came[:, :, i * part : (i + 1) * part].astype(F32) for i in (4, 5)]
    out[...] = jnp.concatenate(grad, axis=1).reshape(out.shape).astype(BF)
    ride = jnp.sum(came[:, :, 6 * part :].astype(F32), axis=0)
    gain[...] = ride[0:2] + ride[2:4]


def call(kernel, args, outs, scratch=(), flops=0, mib=8, copied=0):
    vmem, hbm = [pl.BlockSpec(memory_space=a) for a in (pltpu.VMEM, pltpu.HBM)]
    shapes = [
        pltpu.HBM(s, d) if i < copied else jax.ShapeDtypeStruct(s, d)
        for i, (s, d) in enumerate(outs)
    ]
    moved = sum(math.prod(a.shape) * a.dtype.itemsize for a in list(args) + shapes)
    return pl.pallas_call(
        kernel,
        out_shape=shapes,
        in_specs=[vmem] * len(args),
        out_specs=[hbm] * copied + [vmem] * (len(outs) - copied),
        scratch_shapes=list(scratch),
        compiler_params=pltpu.CompilerParams(vmem_limit_bytes=mib * 2**20),
        cost_estimate=pl.CostEstimate(flops=flops, bytes_accessed=moved, transcendentals=0),
    )(*args)


def mid_kernel(keep, got, mid, near_gain, far_gain):
    rows = keep.shape[1] - SIDE
    near = keep[0, rows:].astype(F32) + got[0, rows:].astype(F32)
    total = keep[1].astype(F32) + got[1].astype(F32)
    mid[...] = total.astype(BF)
    for ref, side in ((near_gain, near), (far_gain, total[rows:])):
        line = side[2:3] + side[3:4]
        ref[0:1] = line[:, :128]
        ref[1:2] = line[:, 128:]


def sum_kernel(near, far, out):
    out[...] = near[...] + far[...]


def per_device(acts, grad_in, gain, w_qkv, w_out):
    dp, tm = lax.axis_size("dp"), lax.axis_size("tm")
    part = acts.shape[3]
    rows = acts.shape[2]
    few = rows // tm
    width = w_qkv.shape[0]
    cols = w_qkv.shape[2]
    heads = cols // HD
    norm = (rows * dp * tm) ** (-0.5)

    own = jnp.stack([acts.reshape(tm, few, part), grad_in.reshape(tm, few, part)], axis=1)
    own = lax.all_to_all(own, "tm", split_axis=0, concat_axis=0, tiled=True)
    far = lax.ppermute(own, "tensor", CHIP)
    near = lax.ppermute(own, "tensor", CORE)
    cross = lax.ppermute(far, "tensor", CORE)

    gain_rows = gain.reshape(4, 1, part)
    w = jnp.transpose(w_qkv, (1, 0, 2)).reshape(3, 4, part, cols)
    message = ((2, rows + SIDE, part), BF)
    dw, send, keep, stats = call(
        functools.partial(main_kernel, heads, norm),
        (gain_rows, own, near, far, cross, w, w_out),
        (
            ((4, part, 4 * cols), BF),
            message,
            message,
            ((8, rows), F32),
        ),
        (
            pltpu.VMEM((4, part, 4 * cols), BF),
            pltpu.VMEM((2, rows + SIDE, part), BF),
            pltpu.VMEM((3, rows, cols), BF),
            pltpu.VMEM((4, rows, part), F32),
            pltpu.VMEM((4, rows, part), BF),
            pltpu.VMEM((4, rows, part), BF),
            pltpu.VMEM((rows, cols), BF),
            pltpu.SemaphoreType.DMA((5,)),
        ),
        flops=7 * 10**9,
        mib=36,
        copied=2,
    )

    dw = dw.reshape(dp, width // dp, 4 * cols)
    dw = lax.all_to_all(dw, "dp", split_axis=0, concat_axis=0, tiled=True)

    got = lax.ppermute(send, "tensor", CORE)
    lines = ((2, 128), F32)
    mid, near_gain, far_gain = call(
        mid_kernel, (keep, got), (((rows + SIDE, part), BF), lines, lines), flops=1000
    )
    far_gain = lax.ppermute(far_gain, "tensor", CHIP)
    last = lax.ppermute(mid, "tensor", CHIP)
    (gain_sum,) = call(sum_kernel, (near_gain, far_gain), (lines,), flops=1000)
    gain_sums = [gain_sum] + [
        lax.ppermute(gain_sum, "dp", [(i, i ^ bit) for i in range(dp)]) for bit in (1, 3, 2)
    ]
    (grad,) = call(
        acts_kernel,
        (keep, got, last, stats, own, gain_rows),
        (((tm, 8, 2 * part), BF),),
        flops=10**6,
    )

    share = width // (dp * tm)
    total = 4 * cols + 2 * part + 128
    group = tm // 4
    pack = pl.pallas_call(
        pack_kernel,
        grid=(tm // group,),
        out_shape=jax.ShapeDtypeStruct((tm, share, total), BF),
        in_specs=[
            pl.BlockSpec((dp, group * share, 4 * cols), lambda i: (0, i, 0)),
            pl.BlockSpec((group, share, 2 * part), lambda i: (i, 0, 0)),
        ]
        + [pl.BlockSpec((2, 128), lambda i: (0, 0))] * 4,
        out_specs=pl.BlockSpec((group, share, total), lambda i: (i, 0, 0)),
        compiler_params=pltpu.CompilerParams(vmem_limit_bytes=8 * 2**20),
        cost_estimate=pl.CostEstimate(flops=10**6, bytes_accessed=10**6, transcendentals=0),
    )(dw, grad, *gain_sums)
    pack = lax.all_to_all(pack, "tm", split_axis=0, concat_axis=0, tiled=True)
    out, dw, dw_out, gain_sum = call(
        last_kernel,
        (pack,),
        (((rows, part), BF), ((3, share, cols), F32), ((share, cols), F32), ((2, 128), F32)),
        flops=10**7,
    )
    return (
        out.reshape(grad_in.shape),
        jnp.transpose(dw, (1, 0, 2)),
        dw_out,
        gain_sum.reshape(part),
    )


def solution(mesh):
    placed = (
        P("dp", "tm", None, "tensor"),
        P("dp", "tm", None, "tensor"),
        P(),
        P(None, None, "tensor"),
        P("tensor", None),
    )
    return jax.shard_map(
        per_device,
        mesh=mesh,
        in_specs=placed,
        out_specs=(
            P("dp", "tm", None, "tensor"),
            P(("dp", "tm"), None, "tensor"),
            P(("dp", "tm"), "tensor"),
            P("tensor"),
        ),
        check_vma=False,
    )
```

```python
import functools
import math

import jax
import jax.numpy as jnp
from jax import lax
from jax.experimental import pallas as pl
from jax.experimental.pallas import tpu as pltpu
from jax.sharding import PartitionSpec as P

HD = 64
EPS = 1e-05
CORE = [(0, 1), (1, 0), (2, 3), (3, 2)]
CHIP = [(0, 2), (2, 0), (1, 3), (3, 1)]
BOTH = [(0, 3), (3, 0), (1, 2), (2, 1)]
F32, BF = jnp.float32, jnp.bfloat16
SIDE = 32


def dot(a, b, contract):
    return lax.dot_general(a, b, (contract, ((), ())), preferred_element_type=F32)


def grouped(a):
    frames, few, part = a.shape
    a = a.astype(F32).reshape(frames, few // 8, 8, part)
    return jnp.concatenate([a[:, i].reshape(frames * 8, part) for i in range(few // 8)])


def attention(q, k, v, g, heads, scale):
    rows, cols = q.shape
    same = (
        lax.broadcasted_iota(jnp.int32, (rows, rows), 0) % 8
        == lax.broadcasted_iota(jnp.int32, (rows, rows), 1) % 8
    )
    lane = lax.broadcasted_iota(jnp.int32, (rows, cols), 1) // HD
    zero = jnp.zeros((rows, cols), BF)
    q_heads, k_heads, v_heads, g_heads = [
        [jnp.where(lane == h, a, zero) for h in range(heads)] for a in (q, k, v, g)
    ]
    g_scaled = (g.astype(F32) * scale).astype(BF)
    lows, dss = [], []
    for h in range(heads):
        scores = dot(q, k_heads[h], ((1,), (1,))) * (scale * math.log2(math.e))
        expd = jnp.exp2(jnp.where(same, scores, -1e30))
        prob = expd * (1.0 / jnp.sum(expd, axis=-1, keepdims=True))
        low = prob.astype(BF)
        dprob = dot(g_scaled, v_heads[h], ((1,), (1,)))
        delta = jnp.sum(low.astype(F32) * dprob, axis=-1, keepdims=True)
        lows.append(low)
        dss.append((prob * (dprob - delta)).astype(BF))

    def joined(parts, axis):
        return jnp.concatenate(parts, axis=axis)

    sums = (
        dot(joined(lows, 1), joined(v_heads, 0), ((1,), (0,))),
        dot(joined(dss, 1), joined(k_heads, 0), ((1,), (0,))),
        dot(joined(dss, 0), joined(q_heads, 0), ((0,), (0,))),
        dot(joined(lows, 0), joined(g_heads, 0), ((0,), (0,))),
    )
    return [a.astype(BF) for a in sums]


def split(a):
    high = a.astype(BF).astype(F32)
    return high, a - high


def main_kernel(
    heads, gain, own, near, far, cross, w, w_out,
    dw_at, send_at, keep, stats, far_gain, cross_gain,
    dw, send, gqkv, xhat, normed, dy, attn, left,
):
    t = lax.axis_index("tensor")
    rows, part = normed.shape[1:]
    width = 4 * part
    pieces = (own, near, far, cross)
    x = [grouped(a[:, 0]) for a in pieces]
    mean = sum(jnp.sum(a, axis=-1, keepdims=True) for a in x) / width
    x = [a - mean for a in x]
    inv = lax.rsqrt(sum(jnp.sum(a * a, axis=-1, keepdims=True) for a in x) / width + EPS)
    for i in range(4):
        xhat[i] = x[i] * inv
        normed[i] = (xhat[i] * gain[t ^ i]).astype(BF)
    qkv = [
        sum(dot(normed[i], w[s, t ^ i], ((1,), (0,))) for i in range(4)).astype(BF)
        for s in range(3)
    ]
    for i in range(4):
        dy[i] = grouped(pieces[i][:, 1]).astype(BF)
    g = sum(
        dot(dy[i], w_out[:, pl.ds(pl.multiple_of((t ^ i) * part, part), part)], ((1,), (1,)))
        for i in range(4)
    ).astype(BF)
    half, cols = rows // 2, w.shape[3]
    for i in range(2):
        span = slice(i * half, (i + 1) * half)
        parts = attention(*(a[span] for a in qkv), g[span], heads, HD ** (-0.5))
        attn[span] = parts[0]
        for s in range(3):
            gqkv[span, s * cols : (s + 1) * cols] = parts[1 + s]
    first = jnp.zeros((rows, 1), F32)
    second = jnp.zeros((rows, 1), F32)
    outs = (keep.at[0], send.at[0], keep.at[1], send.at[1])
    gains = []
    for i in range(4):
        term = sum(
            dot(gqkv[:, s * cols : (s + 1) * cols], w[s, t ^ i], ((1,), (1,))) for s in range(3)
        ).astype(BF)
        outs[i][:rows] = term
        wide = term.astype(F32)
        product = wide * xhat[i]
        gains.append(jnp.sum(product, axis=0, keepdims=True))
        first += jnp.sum(wide * gain[t ^ i], axis=-1, keepdims=True)
        second += jnp.sum(product * gain[t ^ i], axis=-1, keepdims=True)
    for ref, line in ((far_gain, gains[2]), (cross_gain, gains[3])):
        ref[0:1] = line[:, :128]
        ref[1:2] = line[:, 128:]
    lane = lax.broadcasted_iota(jnp.int32, (rows, 128), 1)
    moments = jnp.where(lane == 0, first / width, jnp.where(lane == 1, second / width, 0.0))
    moments = jnp.where(lane == 8, mean, jnp.where(lane == 9, inv, moments)).T
    stats[...] = moments[8:16]
    high, low = split(moments[:8])
    line = lax.broadcasted_iota(jnp.int32, (8, part), 0)
    for i in range(4):
        gain_high, gain_low = split(gains[i])
        top = jnp.where(line == 2, gain_high, jnp.where(line == 3, gain_low, high[:, :part]))
        side = [top, high[:, part:], low[:, :part], low[:, part:]]
        outs[i][rows:] = jnp.concatenate(side).astype(BF)
    copies = [pltpu.make_async_copy(send, send_at, left.at[4])]
    copies[0].start()
    for i in range(4):
        dw[i, :, : 3 * cols] = dot(normed[i], gqkv[...], ((0,), (0,))).astype(BF)
        dw[i, :, 3 * cols :] = dot(dy[i], attn[...], ((0,), (0,))).astype(BF)
        copies.append(pltpu.make_async_copy(dw.at[i], dw_at.at[t ^ i], left.at[i]))
        copies[-1].start()
    for copy in copies:
        copy.wait()


def acts_kernel(keep, got, last, stats, own, gain, out):
    t = lax.axis_index("tensor")
    frames, part = own.shape[0], own.shape[3]
    rows = stats.shape[1]
    total = keep[0].astype(F32) + got[0].astype(F32) + last[...].astype(F32)
    side = total[rows:]
    moments = jnp.concatenate([side[:8] + side[16:24], side[8:16] + side[24:]], axis=1)
    moments = jnp.concatenate([moments, stats[...], jnp.zeros((112, rows), F32)]).T
    first, second, mean, inv = [moments[:, i : i + 1] for i in (0, 1, 8, 9)]
    xhat = (grouped(own[:, 0]) - mean) * inv
    grad = grouped(own[:, 1]) + inv * (total[:rows] * gain[t] - first - xhat * second)
    half = frames * 8
    for i in range(2):
        block = grad[i * half : (i + 1) * half].reshape(frames, 8, part)
        out[:, :, i * part : (i + 1) * part] = block.astype(BF)


def pack_kernel(dw, grad, gain, first, second, third, out):
    group, share, cols = out.shape[0], out.shape[1], dw.shape[2]
    block = sum(dw[i].astype(F32) for i in range(dw.shape[0]))
    out[:, :, :cols] = block.reshape(group, share, cols).astype(BF)
    end = cols + grad.shape[2]
    out[:, :, cols:end] = grad[...]
    high, low = split(gain[...] + first[...] + second[...] + third[...])
    ride = jnp.concatenate([high, low, high, low])
    out[:, :, end:] = jnp.broadcast_to(ride[None], (group, share, 128)).astype(BF)


def last_kernel(norm, came, out, dw, dw_out, gain):
    frames = came.shape[0]
    part = out.shape[1]
    for s in range(3):
        dw[s] = jnp.sum(came[:, :, s * part : (s + 1) * part].astype(F32), axis=0) * norm
    dw_out[...] = jnp.sum(came[:, :, 3 * part : 4 * part].astype(F32), axis=0) * norm
    grad = [came[:, :, i * part : (i + 1) * part].astype(F32) for i in (4, 5)]
    out[...] = jnp.concatenate(grad, axis=1).reshape(out.shape).astype(BF)
    ride = jnp.sum(came[:, :, 6 * part :].astype(F32), axis=0)
    gain[...] = (ride[0:2] + ride[2:4]) * norm


def call(kernel, args, outs, scratch=(), flops=0, mib=8, copied=0):
    vmem, hbm = [pl.BlockSpec(memory_space=a) for a in (pltpu.VMEM, pltpu.HBM)]
    shapes = [
        pltpu.HBM(s, d) if i < copied else jax.ShapeDtypeStruct(s, d)
        for i, (s, d) in enumerate(outs)
    ]
    moved = sum(math.prod(a.shape) * a.dtype.itemsize for a in list(args) + shapes)
    return pl.pallas_call(
        kernel,
        out_shape=shapes,
        in_specs=[vmem] * len(args),
        out_specs=[hbm] * copied + [vmem] * (len(outs) - copied),
        scratch_shapes=list(scratch),
        compiler_params=pltpu.CompilerParams(vmem_limit_bytes=mib * 2**20),
        cost_estimate=pl.CostEstimate(flops=flops, bytes_accessed=moved, transcendentals=0),
    )(*args)


def mid_kernel(keep, got, far, cross, mid, gain):
    mid[...] = (keep[1].astype(F32) + got[1].astype(F32)).astype(BF)
    rows = keep.shape[1] - SIDE
    side = keep[0, rows:].astype(F32) + got[0, rows:].astype(F32)
    line = side[2:3] + side[3:4]
    gain[0:1] = line[:, :128] + far[0:1] + cross[0:1]
    gain[1:2] = line[:, 128:] + far[1:2] + cross[1:2]


def per_device(acts, grad_in, gain, w_qkv, w_out):
    dp, tm = lax.axis_size("dp"), lax.axis_size("tm")
    part = acts.shape[3]
    rows = acts.shape[2]
    few = rows // tm
    width = w_qkv.shape[0]
    cols = w_qkv.shape[2]
    heads = cols // HD
    norm = (rows * dp * tm) ** (-0.5)

    own = jnp.stack([acts.reshape(tm, few, part), grad_in.reshape(tm, few, part)], axis=1)
    own = lax.all_to_all(own, "tm", split_axis=0, concat_axis=0, tiled=True)
    far = lax.ppermute(own, "tensor", CHIP)
    near = lax.ppermute(own, "tensor", CORE)
    cross = lax.ppermute(far, "tensor", CORE)

    gain_rows = gain.reshape(4, 1, part)
    w = jnp.transpose(w_qkv, (1, 0, 2)).reshape(3, 4, part, cols)
    message = ((2, rows + SIDE, part), BF)
    dw, send, keep, stats, far_gain, cross_gain = call(
        functools.partial(main_kernel, heads),
        (gain_rows, own, near, far, cross, w, w_out),
        (
            ((4, part, 4 * cols), BF),
            message,
            message,
            ((8, rows), F32),
            ((2, 128), F32),
            ((2, 128), F32),
        ),
        (
            pltpu.VMEM((4, part, 4 * cols), BF),
            pltpu.VMEM((2, rows + SIDE, part), BF),
            pltpu.VMEM((rows, 3 * cols), BF),
            pltpu.VMEM((4, rows, part), F32),
            pltpu.VMEM((4, rows, part), BF),
            pltpu.VMEM((4, rows, part), BF),
            pltpu.VMEM((rows, cols), BF),
            pltpu.SemaphoreType.DMA((5,)),
        ),
        flops=7 * 10**9,
        mib=36,
        copied=2,
    )

    dw = dw.reshape(dp, width // dp, 4 * cols)
    dw = lax.all_to_all(dw, "dp", split_axis=0, concat_axis=0, tiled=True)

    far_gain = lax.ppermute(far_gain, "tensor", CHIP)
    cross_gain = lax.ppermute(cross_gain, "tensor", BOTH)
    got = lax.ppermute(send, "tensor", CORE)
    mid, gain_sum = call(
        mid_kernel,
        (keep, got, far_gain, cross_gain),
        (((rows + SIDE, part), BF), ((2, 128), F32)),
        flops=1000,
    )
    last = lax.ppermute(mid, "tensor", CHIP)
    gain_sums = [gain_sum] + [
        lax.ppermute(gain_sum, "dp", [(i, i ^ bit) for i in range(dp)]) for bit in (2, 1, 3)
    ]
    (grad,) = call(
        acts_kernel,
        (keep, got, last, stats, own, gain_rows),
        (((tm, 8, 2 * part), BF),),
        flops=10**6,
    )

    share = width // (dp * tm)
    total = 4 * cols + 2 * part + 128
    group = tm // 4
    pack = pl.pallas_call(
        pack_kernel,
        grid=(tm // group,),
        out_shape=jax.ShapeDtypeStruct((tm, share, total), BF),
        in_specs=[
            pl.BlockSpec((dp, group * share, 4 * cols), lambda i: (0, i, 0)),
            pl.BlockSpec((group, share, 2 * part), lambda i: (i, 0, 0)),
        ]
        + [pl.BlockSpec((2, 128), lambda i: (0, 0))] * 4,
        out_specs=pl.BlockSpec((group, share, total), lambda i: (i, 0, 0)),
        compiler_params=pltpu.CompilerParams(vmem_limit_bytes=8 * 2**20),
        cost_estimate=pl.CostEstimate(flops=10**6, bytes_accessed=10**6, transcendentals=0),
    )(dw, grad, *gain_sums)
    pack = lax.all_to_all(pack, "tm", split_axis=0, concat_axis=0, tiled=True)
    out, dw, dw_out, gain_sum = call(
        functools.partial(last_kernel, norm),
        (pack,),
        (((rows, part), BF), ((3, share, cols), F32), ((share, cols), F32), ((2, 128), F32)),
        flops=10**7,
    )
    return (
        out.reshape(grad_in.shape),
        jnp.transpose(dw, (1, 0, 2)),
        dw_out,
        gain_sum.reshape(part),
    )


def solution(mesh):
    placed = (
        P("dp", "tm", None, "tensor"),
        P("dp", "tm", None, "tensor"),
        P(),
        P(None, None, "tensor"),
        P("tensor", None),
    )
    return jax.shard_map(
        per_device,
        mesh=mesh,
        in_specs=placed,
        out_specs=(
            P("dp", "tm", None, "tensor"),
            P(("dp", "tm"), None, "tensor"),
            P(("dp", "tm"), "tensor"),
            P("tensor"),
        ),
        check_vma=False,
    )
```

```python
import functools
import math

import jax
import jax.numpy as jnp
from jax import lax
from jax.experimental import pallas as pl
from jax.experimental.pallas import tpu as pltpu
from jax.sharding import PartitionSpec as P

HD = 64
EPS = 1e-05
CORE = [(0, 1), (1, 0), (2, 3), (3, 2)]
CHIP = [(0, 2), (2, 0), (1, 3), (3, 1)]
BOTH = [(0, 3), (3, 0), (1, 2), (2, 1)]
F32, BF = jnp.float32, jnp.bfloat16
SIDE = 32


def dot(a, b, contract):
    return lax.dot_general(a, b, (contract, ((), ())), preferred_element_type=F32)


def grouped(a):
    frames, few, part = a.shape
    a = a.astype(F32).reshape(frames, few // 8, 8, part)
    return jnp.concatenate([a[:, i].reshape(frames * 8, part) for i in range(few // 8)])


def attention(q, k, v, g, heads, scale):
    rows, cols = q.shape
    same = (
        lax.broadcasted_iota(jnp.int32, (rows, rows), 0) % 8
        == lax.broadcasted_iota(jnp.int32, (rows, rows), 1) % 8
    )
    lane = lax.broadcasted_iota(jnp.int32, (rows, cols), 1) // HD
    zero = jnp.zeros((rows, cols), BF)
    q_heads, k_heads, v_heads, g_heads = [
        [jnp.where(lane == h, a, zero) for h in range(heads)] for a in (q, k, v, g)
    ]
    g_scaled = (g.astype(F32) * scale).astype(BF)
    lows, dss = [], []
    for h in range(heads):
        scores = dot(q, k_heads[h], ((1,), (1,))) * (scale * math.log2(math.e))
        expd = jnp.exp2(jnp.where(same, scores, -1e30))
        prob = expd * (1.0 / jnp.sum(expd, axis=-1, keepdims=True))
        low = prob.astype(BF)
        dprob = dot(g_scaled, v_heads[h], ((1,), (1,)))
        delta = jnp.sum(low.astype(F32) * dprob, axis=-1, keepdims=True)
        lows.append(low)
        dss.append((prob * (dprob - delta)).astype(BF))

    def joined(parts, axis):
        return jnp.concatenate(parts, axis=axis)

    sums = (
        dot(joined(lows, 1), joined(v_heads, 0), ((1,), (0,))),
        dot(joined(dss, 1), joined(k_heads, 0), ((1,), (0,))),
        dot(joined(dss, 0), joined(q_heads, 0), ((0,), (0,))),
        dot(joined(lows, 0), joined(g_heads, 0), ((0,), (0,))),
    )
    return [a.astype(BF) for a in sums]


def split(a):
    high = a.astype(BF).astype(F32)
    return high, a - high


def main_kernel(
    heads, gain, own, near, far, cross, w, w_out,
    dw_at, send_at, keep, stats, far_gain, cross_gain,
    dw, send, gqkv, xhat, normed, dy, attn, left,
):
    t = lax.axis_index("tensor")
    rows, part = normed.shape[1:]
    width = 4 * part
    pieces = (own, near, far, cross)
    x = [grouped(a[:, 0]) for a in pieces]
    mean = sum(jnp.sum(a, axis=-1, keepdims=True) for a in x) / width
    x = [a - mean for a in x]
    inv = lax.rsqrt(sum(jnp.sum(a * a, axis=-1, keepdims=True) for a in x) / width + EPS)
    for i in range(4):
        xhat[i] = x[i] * inv
        normed[i] = (xhat[i] * gain[t ^ i]).astype(BF)
    order = [t ^ i for i in range(4)]
    wide_normed = jnp.concatenate([normed[i] for i in range(4)], axis=1)
    qkv = [
        dot(wide_normed, jnp.concatenate([w[s, j] for j in order]), ((1,), (0,))).astype(BF)
        for s in range(3)
    ]
    for i in range(4):
        dy[i] = grouped(pieces[i][:, 1]).astype(BF)
    wide_dy = jnp.concatenate([dy[i] for i in range(4)], axis=1)
    places = [pl.ds(pl.multiple_of(j * part, part), part) for j in order]
    wide_out = jnp.concatenate([w_out[:, place] for place in places], axis=1)
    g = dot(wide_dy, wide_out, ((1,), (1,))).astype(BF)
    half, cols = rows // 2, w.shape[3]
    for i in range(2):
        span = slice(i * half, (i + 1) * half)
        parts = attention(*(a[span] for a in qkv), g[span], heads, HD ** (-0.5))
        attn[span] = parts[0]
        for s in range(3):
            gqkv[span, s * cols : (s + 1) * cols] = parts[1 + s]
    first = jnp.zeros((rows, 1), F32)
    second = jnp.zeros((rows, 1), F32)
    outs = (keep.at[0], send.at[0], keep.at[1], send.at[1])
    gains = []
    for i in range(4):
        weights = jnp.concatenate([w[s, order[i]] for s in range(3)], axis=1)
        term = dot(gqkv[...], weights, ((1,), (1,))).astype(BF)
        outs[i][:rows] = term
        wide = term.astype(F32)
        product = wide * xhat[i]
        gains.append(jnp.sum(product, axis=0, keepdims=True))
        first += jnp.sum(wide * gain[t ^ i], axis=-1, keepdims=True)
        second += jnp.sum(product * gain[t ^ i], axis=-1, keepdims=True)
    for ref, line in ((far_gain, gains[2]), (cross_gain, gains[3])):
        ref[0:1] = line[:, :128]
        ref[1:2] = line[:, 128:]
    lane = lax.broadcasted_iota(jnp.int32, (rows, 128), 1)
    moments = jnp.where(lane == 0, first / width, jnp.where(lane == 1, second / width, 0.0))
    moments = jnp.where(lane == 8, mean, jnp.where(lane == 9, inv, moments)).T
    stats[...] = moments[8:16]
    high, low = split(moments[:8])
    line = lax.broadcasted_iota(jnp.int32, (8, part), 0)
    for i in range(4):
        gain_high, gain_low = split(gains[i])
        top = jnp.where(line == 2, gain_high, jnp.where(line == 3, gain_low, high[:, :part]))
        side = [top, high[:, part:], low[:, :part], low[:, part:]]
        outs[i][rows:] = jnp.concatenate(side).astype(BF)
    copies = [pltpu.make_async_copy(send, send_at, left.at[4])]
    copies[0].start()
    for i in range(4):
        dw[i, :, : 3 * cols] = dot(normed[i], gqkv[...], ((0,), (0,))).astype(BF)
        dw[i, :, 3 * cols :] = dot(dy[i], attn[...], ((0,), (0,))).astype(BF)
        copies.append(pltpu.make_async_copy(dw.at[i], dw_at.at[t ^ i], left.at[i]))
        copies[-1].start()
    for copy in copies:
        copy.wait()


def acts_kernel(keep, got, last, stats, own, gain, out):
    t = lax.axis_index("tensor")
    frames, part = own.shape[0], own.shape[3]
    rows = stats.shape[1]
    total = keep[0].astype(F32) + got[0].astype(F32) + last[...].astype(F32)
    side = total[rows:]
    moments = jnp.concatenate([side[:8] + side[16:24], side[8:16] + side[24:]], axis=1)
    moments = jnp.concatenate([moments, stats[...], jnp.zeros((112, rows), F32)]).T
    first, second, mean, inv = [moments[:, i : i + 1] for i in (0, 1, 8, 9)]
    xhat = (grouped(own[:, 0]) - mean) * inv
    grad = grouped(own[:, 1]) + inv * (total[:rows] * gain[t] - first - xhat * second)
    half = frames * 8
    for i in range(2):
        block = grad[i * half : (i + 1) * half].reshape(frames, 8, part)
        out[:, :, i * part : (i + 1) * part] = block.astype(BF)


def pack_kernel(dw, grad, gain, first, second, third, out):
    group, share, cols = out.shape[0], out.shape[1], dw.shape[2]
    block = sum(dw[i].astype(F32) for i in range(dw.shape[0]))
    out[:, :, :cols] = block.reshape(group, share, cols).astype(BF)
    end = cols + grad.shape[2]
    out[:, :, cols:end] = grad[...]
    high, low = split(gain[...] + first[...] + second[...] + third[...])
    ride = jnp.concatenate([high, low, high, low])
    out[:, :, end:] = jnp.broadcast_to(ride[None], (group, share, 128)).astype(BF)


def last_kernel(norm, came, out, dw, dw_out, gain):
    frames = came.shape[0]
    part = out.shape[1]
    for s in range(3):
        dw[s] = jnp.sum(came[:, :, s * part : (s + 1) * part].astype(F32), axis=0) * norm
    dw_out[...] = jnp.sum(came[:, :, 3 * part : 4 * part].astype(F32), axis=0) * norm
    grad = [came[:, :, i * part : (i + 1) * part].astype(F32) for i in (4, 5)]
    out[...] = jnp.concatenate(grad, axis=1).reshape(out.shape).astype(BF)
    ride = jnp.sum(came[:, :, 6 * part :].astype(F32), axis=0)
    gain[...] = (ride[0:2] + ride[2:4]) * norm


def call(kernel, args, outs, scratch=(), flops=0, mib=8, copied=0):
    vmem, hbm = [pl.BlockSpec(memory_space=a) for a in (pltpu.VMEM, pltpu.HBM)]
    shapes = [
        pltpu.HBM(s, d) if i < copied else jax.ShapeDtypeStruct(s, d)
        for i, (s, d) in enumerate(outs)
    ]
    moved = sum(math.prod(a.shape) * a.dtype.itemsize for a in list(args) + shapes)
    return pl.pallas_call(
        kernel,
        out_shape=shapes,
        in_specs=[vmem] * len(args),
        out_specs=[hbm] * copied + [vmem] * (len(outs) - copied),
        scratch_shapes=list(scratch),
        compiler_params=pltpu.CompilerParams(vmem_limit_bytes=mib * 2**20),
        cost_estimate=pl.CostEstimate(flops=flops, bytes_accessed=moved, transcendentals=0),
    )(*args)


def mid_kernel(keep, got, far, cross, mid, gain):
    mid[...] = (keep[1].astype(F32) + got[1].astype(F32)).astype(BF)
    rows = keep.shape[1] - SIDE
    side = keep[0, rows:].astype(F32) + got[0, rows:].astype(F32)
    line = side[2:3] + side[3:4]
    gain[0:1] = line[:, :128] + far[0:1] + cross[0:1]
    gain[1:2] = line[:, 128:] + far[1:2] + cross[1:2]


def pair_kernel(first, second, out):
    out[:, 0] = first[...]
    out[:, 1] = second[...]


def paired(first, second):
    count, rows, cols = first.shape
    group = count // 2
    block = pl.BlockSpec((group, rows, cols), lambda i: (i, 0, 0))
    return pl.pallas_call(
        pair_kernel,
        grid=(count // group,),
        out_shape=jax.ShapeDtypeStruct((count, 2, rows, cols), first.dtype),
        in_specs=[block, block],
        out_specs=pl.BlockSpec((group, 2, rows, cols), lambda i: (i, 0, 0, 0)),
        compiler_params=pltpu.CompilerParams(vmem_limit_bytes=60 * 2**20),
    )(first, second)


def per_device(acts, grad_in, gain, w_qkv, w_out):
    dp, tm = lax.axis_size("dp"), lax.axis_size("tm")
    part = acts.shape[3]
    rows = acts.shape[2]
    few = rows // tm
    width = w_qkv.shape[0]
    cols = w_qkv.shape[2]
    heads = cols // HD
    norm = (rows * dp * tm) ** (-0.5)

    own = paired(acts.reshape(tm, few, part), grad_in.reshape(tm, few, part))
    own = lax.all_to_all(own, "tm", split_axis=0, concat_axis=0, tiled=True)
    far = lax.ppermute(own, "tensor", CHIP)
    near = lax.ppermute(own, "tensor", CORE)
    cross = lax.ppermute(far, "tensor", CORE)

    gain_rows = gain.reshape(4, 1, part)
    w = jnp.transpose(w_qkv, (1, 0, 2)).reshape(3, 4, part, cols)
    message = ((2, rows + SIDE, part), BF)
    dw, send, keep, stats, far_gain, cross_gain = call(
        functools.partial(main_kernel, heads),
        (gain_rows, own, near, far, cross, w, w_out),
        (
            ((4, part, 4 * cols), BF),
            message,
            message,
            ((8, rows), F32),
            ((2, 128), F32),
            ((2, 128), F32),
        ),
        (
            pltpu.VMEM((4, part, 4 * cols), BF),
            pltpu.VMEM((2, rows + SIDE, part), BF),
            pltpu.VMEM((rows, 3 * cols), BF),
            pltpu.VMEM((4, rows, part), F32),
            pltpu.VMEM((4, rows, part), BF),
            pltpu.VMEM((4, rows, part), BF),
            pltpu.VMEM((rows, cols), BF),
            pltpu.SemaphoreType.DMA((5,)),
        ),
        flops=7 * 10**9,
        mib=36,
        copied=2,
    )

    dw = dw.reshape(dp, width // dp, 4 * cols)
    dw = lax.all_to_all(dw, "dp", split_axis=0, concat_axis=0, tiled=True)

    far_gain = lax.ppermute(far_gain, "tensor", CHIP)
    cross_gain = lax.ppermute(cross_gain, "tensor", BOTH)
    got = lax.ppermute(send, "tensor", CORE)
    mid, gain_sum = call(
        mid_kernel,
        (keep, got, far_gain, cross_gain),
        (((rows + SIDE, part), BF), ((2, 128), F32)),
        flops=1000,
    )
    last = lax.ppermute(mid, "tensor", CHIP)
    gain_sums = [gain_sum] + [
        lax.ppermute(gain_sum, "dp", [(i, i ^ bit) for i in range(dp)]) for bit in (2, 1, 3)
    ]
    (grad,) = call(
        acts_kernel,
        (keep, got, last, stats, own, gain_rows),
        (((tm, 8, 2 * part), BF),),
        flops=10**6,
    )

    share = width // (dp * tm)
    total = 4 * cols + 2 * part + 128
    group = tm // 4
    pack = pl.pallas_call(
        pack_kernel,
        grid=(tm // group,),
        out_shape=jax.ShapeDtypeStruct((tm, share, total), BF),
        in_specs=[
            pl.BlockSpec((dp, group * share, 4 * cols), lambda i: (0, i, 0)),
            pl.BlockSpec((group, share, 2 * part), lambda i: (i, 0, 0)),
        ]
        + [pl.BlockSpec((2, 128), lambda i: (0, 0))] * 4,
        out_specs=pl.BlockSpec((group, share, total), lambda i: (i, 0, 0)),
        compiler_params=pltpu.CompilerParams(vmem_limit_bytes=8 * 2**20),
        cost_estimate=pl.CostEstimate(flops=10**6, bytes_accessed=10**6, transcendentals=0),
    )(dw, grad, *gain_sums)
    pack = lax.all_to_all(pack, "tm", split_axis=0, concat_axis=0, tiled=True)
    out, dw, dw_out, gain_sum = call(
        functools.partial(last_kernel, norm),
        (pack,),
        (((rows, part), BF), ((3, share, cols), F32), ((share, cols), F32), ((2, 128), F32)),
        flops=10**7,
    )
    return (
        out.reshape(grad_in.shape),
        jnp.transpose(dw, (1, 0, 2)),
        dw_out,
        gain_sum.reshape(part),
    )


def solution(mesh):
    placed = (
        P("dp", "tm", None, "tensor"),
        P("dp", "tm", None, "tensor"),
        P(),
        P(None, None, "tensor"),
        P("tensor", None),
    )
    return jax.shard_map(
        per_device,
        mesh=mesh,
        in_specs=placed,
        out_specs=(
            P("dp", "tm", None, "tensor"),
            P(("dp", "tm"), None, "tensor"),
            P(("dp", "tm"), "tensor"),
            P("tensor"),
        ),
        check_vma=False,
    )
```

```python
import functools
import math

import jax
import jax.numpy as jnp
from jax import lax
from jax.experimental import pallas as pl
from jax.experimental.pallas import tpu as pltpu
from jax.sharding import PartitionSpec as P

HD = 64
EPS = 1e-05
CORE = [(0, 1), (1, 0), (2, 3), (3, 2)]
CHIP = [(0, 2), (2, 0), (1, 3), (3, 1)]
BOTH = [(0, 3), (3, 0), (1, 2), (2, 1)]
F32, BF = jnp.float32, jnp.bfloat16
SIDE = 32


def dot(a, b, contract):
    return lax.dot_general(a, b, (contract, ((), ())), preferred_element_type=F32)


def grouped(a):
    frames, few, part = a.shape
    a = a.astype(F32).reshape(frames, few // 8, 8, part)
    return jnp.concatenate([a[:, i].reshape(frames * 8, part) for i in range(few // 8)])


def attention(q, k, v, g, heads, scale):
    rows, cols = q.shape
    same = (
        lax.broadcasted_iota(jnp.int32, (rows, rows), 0) % 8
        == lax.broadcasted_iota(jnp.int32, (rows, rows), 1) % 8
    )
    lane = lax.broadcasted_iota(jnp.int32, (rows, cols), 1) // HD
    zero = jnp.zeros((rows, cols), BF)
    q_heads, k_heads, v_heads, g_heads = [
        [jnp.where(lane == h, a, zero) for h in range(heads)] for a in (q, k, v, g)
    ]
    g_scaled = (g.astype(F32) * scale).astype(BF)
    lows, dss = [], []
    for h in range(heads):
        scores = dot(q, k_heads[h], ((1,), (1,))) * (scale * math.log2(math.e))
        expd = jnp.exp2(jnp.where(same, scores, -1e30))
        prob = expd * (1.0 / jnp.sum(expd, axis=-1, keepdims=True))
        low = prob.astype(BF)
        dprob = dot(g_scaled, v_heads[h], ((1,), (1,)))
        delta = jnp.sum(low.astype(F32) * dprob, axis=-1, keepdims=True)
        lows.append(low)
        dss.append((prob * (dprob - delta)).astype(BF))

    def joined(parts, axis):
        return jnp.concatenate(parts, axis=axis)

    sums = (
        dot(joined(lows, 1), joined(v_heads, 0), ((1,), (0,))),
        dot(joined(dss, 1), joined(k_heads, 0), ((1,), (0,))),
        dot(joined(dss, 0), joined(q_heads, 0), ((0,), (0,))),
        dot(joined(lows, 0), joined(g_heads, 0), ((0,), (0,))),
    )
    return [a.astype(BF) for a in sums]


def split(a):
    high = a.astype(BF).astype(F32)
    return high, a - high


def feature_columns(w_out, t, pieces):
    part = w_out.shape[1] // 4
    places = [pl.ds(pl.multiple_of((t ^ i) * part, part), part) for i in pieces]
    return jnp.concatenate([w_out[:, place] for place in places], axis=1)


def early_kernel(own, near, far, w_out, x, dy, g):
    t = lax.axis_index("tensor")
    for i, piece in enumerate((own, near, far)):
        x[i] = grouped(piece[:, 0])
        dy[i] = grouped(piece[:, 1]).astype(BF)
    wide_dy = jnp.concatenate([dy[i] for i in range(3)], axis=1)
    g[...] = dot(wide_dy, feature_columns(w_out, t, (0, 1, 2)), ((1,), (1,)))


def main_kernel(
    heads, gain, early_x, early_dy, early_g, cross, w, w_out,
    dw_at, send_at, keep, stats, far_gain, cross_gain,
    dw, send, gqkv, xhat, normed, dy, attn, left,
):
    t = lax.axis_index("tensor")
    rows, part = normed.shape[1:]
    width = 4 * part
    x = [early_x[i] for i in range(3)] + [grouped(cross[:, 0])]
    mean = sum(jnp.sum(a, axis=-1, keepdims=True) for a in x) / width
    x = [a - mean for a in x]
    inv = lax.rsqrt(sum(jnp.sum(a * a, axis=-1, keepdims=True) for a in x) / width + EPS)
    for i in range(4):
        xhat[i] = x[i] * inv
        normed[i] = (xhat[i] * gain[t ^ i]).astype(BF)
    order = [t ^ i for i in range(4)]
    wide_normed = jnp.concatenate([normed[i] for i in range(4)], axis=1)
    qkv = [
        dot(wide_normed, jnp.concatenate([w[s, j] for j in order]), ((1,), (0,))).astype(BF)
        for s in range(3)
    ]
    for i in range(3):
        dy[i] = early_dy[i]
    dy[3] = grouped(cross[:, 1]).astype(BF)
    g = dot(dy[3], feature_columns(w_out, t, (3,)), ((1,), (1,)))
    g = (g + early_g[...]).astype(BF)
    half, cols = rows // 2, w.shape[3]
    for i in range(2):
        span = slice(i * half, (i + 1) * half)
        parts = attention(*(a[span] for a in qkv), g[span], heads, HD ** (-0.5))
        attn[span] = parts[0]
        for s in range(3):
            gqkv[span, s * cols : (s + 1) * cols] = parts[1 + s]
    first = jnp.zeros((rows, 1), F32)
    second = jnp.zeros((rows, 1), F32)
    outs = (keep.at[0], send.at[0], keep.at[1], send.at[1])
    gains = []
    for i in range(4):
        weights = jnp.concatenate([w[s, order[i]] for s in range(3)], axis=1)
        term = dot(gqkv[...], weights, ((1,), (1,))).astype(BF)
        outs[i][:rows] = term
        wide = term.astype(F32)
        product = wide * xhat[i]
        gains.append(jnp.sum(product, axis=0, keepdims=True))
        first += jnp.sum(wide * gain[t ^ i], axis=-1, keepdims=True)
        second += jnp.sum(product * gain[t ^ i], axis=-1, keepdims=True)
    for ref, line in ((far_gain, gains[2]), (cross_gain, gains[3])):
        ref[0:1] = line[:, :128]
        ref[1:2] = line[:, 128:]
    lane = lax.broadcasted_iota(jnp.int32, (rows, 128), 1)
    moments = jnp.where(lane == 0, first / width, jnp.where(lane == 1, second / width, 0.0))
    moments = jnp.where(lane == 8, mean, jnp.where(lane == 9, inv, moments)).T
    stats[...] = moments[8:16]
    high, low = split(moments[:8])
    line = lax.broadcasted_iota(jnp.int32, (8, part), 0)
    for i in range(4):
        gain_high, gain_low = split(gains[i])
        top = jnp.where(line == 2, gain_high, jnp.where(line == 3, gain_low, high[:, :part]))
        side = [top, high[:, part:], low[:, :part], low[:, part:]]
        outs[i][rows:] = jnp.concatenate(side).astype(BF)
    copies = [pltpu.make_async_copy(send, send_at, left.at[4])]
    copies[0].start()
    for i in range(4):
        dw[i, :, : 3 * cols] = dot(normed[i], gqkv[...], ((0,), (0,))).astype(BF)
        dw[i, :, 3 * cols :] = dot(dy[i], attn[...], ((0,), (0,))).astype(BF)
        copies.append(pltpu.make_async_copy(dw.at[i], dw_at.at[t ^ i], left.at[i]))
        copies[-1].start()
    for copy in copies:
        copy.wait()


def acts_kernel(keep, got, last, stats, own, gain, out):
    t = lax.axis_index("tensor")
    frames, part = own.shape[0], own.shape[3]
    rows = stats.shape[1]
    total = keep[0].astype(F32) + got[0].astype(F32) + last[...].astype(F32)
    side = total[rows:]
    moments = jnp.concatenate([side[:8] + side[16:24], side[8:16] + side[24:]], axis=1)
    moments = jnp.concatenate([moments, stats[...], jnp.zeros((112, rows), F32)]).T
    first, second, mean, inv = [moments[:, i : i + 1] for i in (0, 1, 8, 9)]
    xhat = (grouped(own[:, 0]) - mean) * inv
    grad = grouped(own[:, 1]) + inv * (total[:rows] * gain[t] - first - xhat * second)
    half = frames * 8
    for i in range(2):
        block = grad[i * half : (i + 1) * half].reshape(frames, 8, part)
        out[:, :, i * part : (i + 1) * part] = block.astype(BF)


def pack_kernel(dw, grad, gain, first, second, third, out):
    group, share, cols = out.shape[0], out.shape[1], dw.shape[2]
    block = sum(dw[i].astype(F32) for i in range(dw.shape[0]))
    out[:, :, :cols] = block.reshape(group, share, cols).astype(BF)
    end = cols + grad.shape[2]
    out[:, :, cols:end] = grad[...]
    high, low = split(gain[...] + first[...] + second[...] + third[...])
    ride = jnp.concatenate([high, low, high, low])
    out[:, :, end:] = jnp.broadcast_to(ride[None], (group, share, 128)).astype(BF)


def last_kernel(norm, came, out, dw, dw_out, gain):
    frames = came.shape[0]
    part = out.shape[1]
    for s in range(3):
        dw[s] = jnp.sum(came[:, :, s * part : (s + 1) * part].astype(F32), axis=0) * norm
    dw_out[...] = jnp.sum(came[:, :, 3 * part : 4 * part].astype(F32), axis=0) * norm
    grad = [came[:, :, i * part : (i + 1) * part].astype(F32) for i in (4, 5)]
    out[...] = jnp.concatenate(grad, axis=1).reshape(out.shape).astype(BF)
    ride = jnp.sum(came[:, :, 6 * part :].astype(F32), axis=0)
    gain[...] = (ride[0:2] + ride[2:4]) * norm


def call(kernel, args, outs, scratch=(), flops=0, mib=8, copied=0):
    vmem, hbm = [pl.BlockSpec(memory_space=a) for a in (pltpu.VMEM, pltpu.HBM)]
    shapes = [
        pltpu.HBM(s, d) if i < copied else jax.ShapeDtypeStruct(s, d)
        for i, (s, d) in enumerate(outs)
    ]
    moved = sum(math.prod(a.shape) * a.dtype.itemsize for a in list(args) + shapes)
    return pl.pallas_call(
        kernel,
        out_shape=shapes,
        in_specs=[vmem] * len(args),
        out_specs=[hbm] * copied + [vmem] * (len(outs) - copied),
        scratch_shapes=list(scratch),
        compiler_params=pltpu.CompilerParams(vmem_limit_bytes=mib * 2**20),
        cost_estimate=pl.CostEstimate(flops=flops, bytes_accessed=moved, transcendentals=0),
    )(*args)


def mid_kernel(keep, got, far, cross, mid, gain):
    mid[...] = (keep[1].astype(F32) + got[1].astype(F32)).astype(BF)
    rows = keep.shape[1] - SIDE
    side = keep[0, rows:].astype(F32) + got[0, rows:].astype(F32)
    line = side[2:3] + side[3:4]
    gain[0:1] = line[:, :128] + far[0:1] + cross[0:1]
    gain[1:2] = line[:, 128:] + far[1:2] + cross[1:2]


def per_device(acts, grad_in, gain, w_qkv, w_out):
    dp, tm = lax.axis_size("dp"), lax.axis_size("tm")
    part = acts.shape[3]
    rows = acts.shape[2]
    few = rows // tm
    width = w_qkv.shape[0]
    cols = w_qkv.shape[2]
    heads = cols // HD
    norm = (rows * dp * tm) ** (-0.5)

    own = jnp.stack([acts.reshape(tm, few, part), grad_in.reshape(tm, few, part)], axis=1)
    own = lax.all_to_all(own, "tm", split_axis=0, concat_axis=0, tiled=True)
    far = lax.ppermute(own, "tensor", CHIP)
    near = lax.ppermute(own, "tensor", CORE)
    cross = lax.ppermute(far, "tensor", CORE)

    gain_rows = gain.reshape(4, 1, part)
    w = jnp.transpose(w_qkv, (1, 0, 2)).reshape(3, 4, part, cols)
    message = ((2, rows + SIDE, part), BF)
    early = call(
        early_kernel,
        (own, near, far, w_out),
        (((3, rows, part), F32), ((3, rows, part), BF), ((rows, cols), F32)),
        flops=3 * 10**8,
        mib=16,
    )
    dw, send, keep, stats, far_gain, cross_gain = call(
        functools.partial(main_kernel, heads),
        (gain_rows, *early, cross, w, w_out),
        (
            ((4, part, 4 * cols), BF),
            message,
            message,
            ((8, rows), F32),
            ((2, 128), F32),
            ((2, 128), F32),
        ),
        (
            pltpu.VMEM((4, part, 4 * cols), BF),
            pltpu.VMEM((2, rows + SIDE, part), BF),
            pltpu.VMEM((rows, 3 * cols), BF),
            pltpu.VMEM((4, rows, part), F32),
            pltpu.VMEM((4, rows, part), BF),
            pltpu.VMEM((4, rows, part), BF),
            pltpu.VMEM((rows, cols), BF),
            pltpu.SemaphoreType.DMA((5,)),
        ),
        flops=7 * 10**9,
        mib=36,
        copied=2,
    )

    dw = dw.reshape(dp, width // dp, 4 * cols)
    dw = lax.all_to_all(dw, "dp", split_axis=0, concat_axis=0, tiled=True)

    far_gain = lax.ppermute(far_gain, "tensor", CHIP)
    cross_gain = lax.ppermute(cross_gain, "tensor", BOTH)
    got = lax.ppermute(send, "tensor", CORE)
    mid, gain_sum = call(
        mid_kernel,
        (keep, got, far_gain, cross_gain),
        (((rows + SIDE, part), BF), ((2, 128), F32)),
        flops=1000,
    )
    last = lax.ppermute(mid, "tensor", CHIP)
    gain_sums = [gain_sum] + [
        lax.ppermute(gain_sum, "dp", [(i, i ^ bit) for i in range(dp)]) for bit in (2, 1, 3)
    ]
    (grad,) = call(
        acts_kernel,
        (keep, got, last, stats, own, gain_rows),
        (((tm, 8, 2 * part), BF),),
        flops=10**6,
    )

    share = width // (dp * tm)
    total = 4 * cols + 2 * part + 128
    group = tm // 4
    pack = pl.pallas_call(
        pack_kernel,
        grid=(tm // group,),
        out_shape=jax.ShapeDtypeStruct((tm, share, total), BF),
        in_specs=[
            pl.BlockSpec((dp, group * share, 4 * cols), lambda i: (0, i, 0)),
            pl.BlockSpec((group, share, 2 * part), lambda i: (i, 0, 0)),
        ]
        + [pl.BlockSpec((2, 128), lambda i: (0, 0))] * 4,
        out_specs=pl.BlockSpec((group, share, total), lambda i: (i, 0, 0)),
        compiler_params=pltpu.CompilerParams(vmem_limit_bytes=8 * 2**20),
        cost_estimate=pl.CostEstimate(flops=10**6, bytes_accessed=10**6, transcendentals=0),
    )(dw, grad, *gain_sums)
    pack = lax.all_to_all(pack, "tm", split_axis=0, concat_axis=0, tiled=True)
    out, dw, dw_out, gain_sum = call(
        functools.partial(last_kernel, norm),
        (pack,),
        (((rows, part), BF), ((3, share, cols), F32), ((share, cols), F32), ((2, 128), F32)),
        flops=10**7,
    )
    return (
        out.reshape(grad_in.shape),
        jnp.transpose(dw, (1, 0, 2)),
        dw_out,
        gain_sum.reshape(part),
    )


def solution(mesh):
    placed = (
        P("dp", "tm", None, "tensor"),
        P("dp", "tm", None, "tensor"),
        P(),
        P(None, None, "tensor"),
        P("tensor", None),
    )
    return jax.shard_map(
        per_device,
        mesh=mesh,
        in_specs=placed,
        out_specs=(
            P("dp", "tm", None, "tensor"),
            P(("dp", "tm"), None, "tensor"),
            P(("dp", "tm"), "tensor"),
            P("tensor"),
        ),
        check_vma=False,
    )
```

```python
import functools
import math

import jax
import jax.numpy as jnp
from jax import lax
from jax.experimental import pallas as pl
from jax.experimental.pallas import tpu as pltpu
from jax.sharding import PartitionSpec as P

HD = 64
EPS = 1e-05
CORE = [(0, 1), (1, 0), (2, 3), (3, 2)]
CHIP = [(0, 2), (2, 0), (1, 3), (3, 1)]
F32, BF = jnp.float32, jnp.bfloat16
SIDE = 32


def dot(a, b, contract):
    return lax.dot_general(a, b, (contract, ((), ())), preferred_element_type=F32)


def grouped(a):
    frames, few, part = a.shape
    a = a.astype(F32).reshape(frames, few // 8, 8, part)
    return jnp.concatenate([a[:, i].reshape(frames * 8, part) for i in range(few // 8)])


def attention(q, k, v, g, heads, scale):
    rows, cols = q.shape
    same = (
        lax.broadcasted_iota(jnp.int32, (rows, rows), 0) % 8
        == lax.broadcasted_iota(jnp.int32, (rows, rows), 1) % 8
    )
    lane = lax.broadcasted_iota(jnp.int32, (rows, cols), 1) // HD
    zero = jnp.zeros((rows, cols), BF)
    q_heads, k_heads, v_heads, g_heads = [
        [jnp.where(lane == h, a, zero) for h in range(heads)] for a in (q, k, v, g)
    ]
    g_scaled = (g.astype(F32) * scale).astype(BF)
    lows, dss = [], []
    for h in range(heads):
        scores = dot(q, k_heads[h], ((1,), (1,))) * (scale * math.log2(math.e))
        expd = jnp.exp2(jnp.where(same, scores, -1e30))
        prob = expd * (1.0 / jnp.sum(expd, axis=-1, keepdims=True))
        low = prob.astype(BF)
        dprob = dot(g_scaled, v_heads[h], ((1,), (1,)))
        delta = jnp.sum(low.astype(F32) * dprob, axis=-1, keepdims=True)
        lows.append(low)
        dss.append((prob * (dprob - delta)).astype(BF))

    def joined(parts, axis):
        return jnp.concatenate(parts, axis=axis)

    sums = (
        dot(joined(lows, 1), joined(v_heads, 0), ((1,), (0,))),
        dot(joined(dss, 1), joined(k_heads, 0), ((1,), (0,))),
        dot(joined(dss, 0), joined(q_heads, 0), ((0,), (0,))),
        dot(joined(lows, 0), joined(g_heads, 0), ((0,), (0,))),
    )
    return [a.astype(BF) for a in sums]


def split(a):
    high = a.astype(BF).astype(F32)
    return high, a - high


def main_kernel(
    heads, gain, own, near, far, cross, w, w_out,
    dw_at, send_at, keep, stats,
    dw, send, gqkv, xhat, normed, dy, attn, left,
):
    t = lax.axis_index("tensor")
    rows, part = normed.shape[1:]
    width = 4 * part
    pieces = (own, near, far, cross)
    x = [grouped(a[:, 0]) for a in pieces]
    mean = sum(jnp.sum(a, axis=-1, keepdims=True) for a in x) / width
    x = [a - mean for a in x]
    inv = lax.rsqrt(sum(jnp.sum(a * a, axis=-1, keepdims=True) for a in x) / width + EPS)
    for i in range(4):
        xhat[i] = x[i] * inv
        normed[i] = (xhat[i] * gain[t ^ i]).astype(BF)
    qkv = [
        sum(dot(normed[i], w[s, t ^ i], ((1,), (0,))) for i in range(4)).astype(BF)
        for s in range(3)
    ]
    for i in range(4):
        dy[i] = grouped(pieces[i][:, 1]).astype(BF)
    g = sum(
        dot(dy[i], w_out[:, pl.ds(pl.multiple_of((t ^ i) * part, part), part)], ((1,), (1,)))
        for i in range(4)
    ).astype(BF)
    half, cols = rows // 2, w.shape[3]
    for i in range(2):
        span = slice(i * half, (i + 1) * half)
        parts = attention(*(a[span] for a in qkv), g[span], heads, HD ** (-0.5))
        attn[span] = parts[0]
        for s in range(3):
            gqkv[span, s * cols : (s + 1) * cols] = parts[1 + s]
    first = jnp.zeros((rows, 1), F32)
    second = jnp.zeros((rows, 1), F32)
    outs = (keep.at[0], send.at[0], keep.at[1], send.at[1])
    gains = []
    for i in range(4):
        term = sum(
            dot(gqkv[:, s * cols : (s + 1) * cols], w[s, t ^ i], ((1,), (1,))) for s in range(3)
        ).astype(BF)
        outs[i][:rows] = term
        wide = term.astype(F32)
        product = wide * xhat[i]
        gains.append(jnp.sum(product, axis=0, keepdims=True))
        first += jnp.sum(wide * gain[t ^ i], axis=-1, keepdims=True)
        second += jnp.sum(product * gain[t ^ i], axis=-1, keepdims=True)
    lane = lax.broadcasted_iota(jnp.int32, (rows, 128), 1)
    moments = jnp.where(lane == 0, first / width, jnp.where(lane == 1, second / width, 0.0))
    moments = jnp.where(lane == 8, mean, jnp.where(lane == 9, inv, moments)).T
    stats[...] = moments[8:16]
    high, low = split(moments[:8])
    line = lax.broadcasted_iota(jnp.int32, (8, part), 0)
    for i in range(4):
        gain_high, gain_low = split(gains[i])
        top = jnp.where(line == 2, gain_high, jnp.where(line == 3, gain_low, high[:, :part]))
        side = [top, high[:, part:], low[:, :part], low[:, part:]]
        outs[i][rows:] = jnp.concatenate(side).astype(BF)
    copies = [pltpu.make_async_copy(send, send_at, left.at[4])]
    copies[0].start()
    for i in range(4):
        dw[i, :, : 3 * cols] = dot(normed[i], gqkv[...], ((0,), (0,))).astype(BF)
        dw[i, :, 3 * cols :] = dot(dy[i], attn[...], ((0,), (0,))).astype(BF)
        copies.append(pltpu.make_async_copy(dw.at[i], dw_at.at[t ^ i], left.at[i]))
        copies[-1].start()
    for copy in copies:
        copy.wait()


def acts_kernel(keep, got, last, stats, own, gain, out, gain_sum):
    t = lax.axis_index("tensor")
    frames, part = own.shape[0], own.shape[3]
    rows = stats.shape[1]
    total = keep[0].astype(F32) + got[0].astype(F32) + last[...].astype(F32)
    side = total[rows:]
    line = side[2:3] + side[3:4]
    gain_sum[0:1] = line[:, :128]
    gain_sum[1:2] = line[:, 128:]
    moments = jnp.concatenate([side[:8] + side[16:24], side[8:16] + side[24:]], axis=1)
    moments = jnp.concatenate([moments, stats[...], jnp.zeros((112, rows), F32)]).T
    first, second, mean, inv = [moments[:, i : i + 1] for i in (0, 1, 8, 9)]
    xhat = (grouped(own[:, 0]) - mean) * inv
    grad = grouped(own[:, 1]) + inv * (total[:rows] * gain[t] - first - xhat * second)
    half = frames * 8
    for i in range(2):
        block = grad[i * half : (i + 1) * half].reshape(frames, 8, part)
        out[:, :, i * part : (i + 1) * part] = block.astype(BF)


def pack_kernel(dw, grad, gain, first, second, third, out):
    group, share, cols = out.shape[0], out.shape[1], dw.shape[2]
    block = sum(dw[i].astype(F32) for i in range(dw.shape[0]))
    out[:, :, :cols] = block.reshape(group, share, cols).astype(BF)
    end = cols + grad.shape[2]
    out[:, :, cols:end] = grad[...]
    high, low = split(gain[...] + first[...] + second[...] + third[...])
    ride = jnp.concatenate([high, low, high, low])
    out[:, :, end:] = jnp.broadcast_to(ride[None], (group, share, 128)).astype(BF)


def last_kernel(norm, came, out, dw, dw_out, gain):
    frames = came.shape[0]
    part = out.shape[1]
    for s in range(3):
        dw[s] = jnp.sum(came[:, :, s * part : (s + 1) * part].astype(F32), axis=0) * norm
    dw_out[...] = jnp.sum(came[:, :, 3 * part : 4 * part].astype(F32), axis=0) * norm
    grad = [came[:, :, i * part : (i + 1) * part].astype(F32) for i in (4, 5)]
    out[...] = jnp.concatenate(grad, axis=1).reshape(out.shape).astype(BF)
    ride = jnp.sum(came[:, :, 6 * part :].astype(F32), axis=0)
    gain[...] = (ride[0:2] + ride[2:4]) * norm


def call(kernel, args, outs, scratch=(), flops=0, mib=8, copied=0):
    vmem, hbm = [pl.BlockSpec(memory_space=a) for a in (pltpu.VMEM, pltpu.HBM)]
    shapes = [
        pltpu.HBM(s, d) if i < copied else jax.ShapeDtypeStruct(s, d)
        for i, (s, d) in enumerate(outs)
    ]
    moved = sum(math.prod(a.shape) * a.dtype.itemsize for a in list(args) + shapes)
    return pl.pallas_call(
        kernel,
        out_shape=shapes,
        in_specs=[vmem] * len(args),
        out_specs=[hbm] * copied + [vmem] * (len(outs) - copied),
        scratch_shapes=list(scratch),
        compiler_params=pltpu.CompilerParams(vmem_limit_bytes=mib * 2**20),
        cost_estimate=pl.CostEstimate(flops=flops, bytes_accessed=moved, transcendentals=0),
    )(*args)


def mid_kernel(keep, got, mid):
    mid[...] = (keep[1].astype(F32) + got[1].astype(F32)).astype(BF)


def per_device(acts, grad_in, gain, w_qkv, w_out):
    dp, tm = lax.axis_size("dp"), lax.axis_size("tm")
    part = acts.shape[3]
    rows = acts.shape[2]
    few = rows // tm
    width = w_qkv.shape[0]
    cols = w_qkv.shape[2]
    heads = cols // HD
    norm = (rows * dp * tm) ** (-0.5)

    own = jnp.stack([acts.reshape(tm, few, part), grad_in.reshape(tm, few, part)], axis=1)
    own = lax.all_to_all(own, "tm", split_axis=0, concat_axis=0, tiled=True)
    far = lax.ppermute(own, "tensor", CHIP)
    near = lax.ppermute(own, "tensor", CORE)
    cross = lax.ppermute(far, "tensor", CORE)

    gain_rows = gain.reshape(4, 1, part)
    w = jnp.transpose(w_qkv, (1, 0, 2)).reshape(3, 4, part, cols)
    message = ((2, rows + SIDE, part), BF)
    dw, send, keep, stats = call(
        functools.partial(main_kernel, heads),
        (gain_rows, own, near, far, cross, w, w_out),
        (
            ((4, part, 4 * cols), BF),
            message,
            message,
            ((8, rows), F32),
        ),
        (
            pltpu.VMEM((4, part, 4 * cols), BF),
            pltpu.VMEM((2, rows + SIDE, part), BF),
            pltpu.VMEM((rows, 3 * cols), BF),
            pltpu.VMEM((4, rows, part), F32),
            pltpu.VMEM((4, rows, part), BF),
            pltpu.VMEM((4, rows, part), BF),
            pltpu.VMEM((rows, cols), BF),
            pltpu.SemaphoreType.DMA((5,)),
        ),
        flops=7 * 10**9,
        mib=36,
        copied=2,
    )

    dw = dw.reshape(dp, width // dp, 4 * cols)
    dw = lax.all_to_all(dw, "dp", split_axis=0, concat_axis=0, tiled=True)

    got = lax.ppermute(send, "tensor", CORE)
    (mid,) = call(mid_kernel, (keep, got), (((rows + SIDE, part), BF),), flops=1000)
    last = lax.ppermute(mid, "tensor", CHIP)
    grad, gain_sum = call(
        acts_kernel,
        (keep, got, last, stats, own, gain_rows),
        (((tm, 8, 2 * part), BF), ((2, 128), F32)),
        flops=10**6,
    )
    gain_sums = [gain_sum] + [
        lax.ppermute(gain_sum, "dp", [(i, i ^ bit) for i in range(dp)]) for bit in (2, 1, 3)
    ]

    share = width // (dp * tm)
    total = 4 * cols + 2 * part + 128
    group = tm // 4
    pack = pl.pallas_call(
        pack_kernel,
        grid=(tm // group,),
        out_shape=jax.ShapeDtypeStruct((tm, share, total), BF),
        in_specs=[
            pl.BlockSpec((dp, group * share, 4 * cols), lambda i: (0, i, 0)),
            pl.BlockSpec((group, share, 2 * part), lambda i: (i, 0, 0)),
        ]
        + [pl.BlockSpec((2, 128), lambda i: (0, 0))] * 4,
        out_specs=pl.BlockSpec((group, share, total), lambda i: (i, 0, 0)),
        compiler_params=pltpu.CompilerParams(vmem_limit_bytes=8 * 2**20),
        cost_estimate=pl.CostEstimate(flops=10**6, bytes_accessed=10**6, transcendentals=0),
    )(dw, grad, *gain_sums)
    pack = lax.all_to_all(pack, "tm", split_axis=0, concat_axis=0, tiled=True)
    out, dw, dw_out, gain_sum = call(
        functools.partial(last_kernel, norm),
        (pack,),
        (((rows, part), BF), ((3, share, cols), F32), ((share, cols), F32), ((2, 128), F32)),
        flops=10**7,
    )
    return (
        out.reshape(grad_in.shape),
        jnp.transpose(dw, (1, 0, 2)),
        dw_out,
        gain_sum.reshape(part),
    )


def solution(mesh):
    placed = (
        P("dp", "tm", None, "tensor"),
        P("dp", "tm", None, "tensor"),
        P(),
        P(None, None, "tensor"),
        P("tensor", None),
    )
    return jax.shard_map(
        per_device,
        mesh=mesh,
        in_specs=placed,
        out_specs=(
            P("dp", "tm", None, "tensor"),
            P(("dp", "tm"), None, "tensor"),
            P(("dp", "tm"), "tensor"),
            P("tensor"),
        ),
        check_vma=False,
    )
```

```python
import functools
import math

import jax
import jax.numpy as jnp
from jax import lax
from jax.experimental import pallas as pl
from jax.experimental.pallas import tpu as pltpu
from jax.sharding import PartitionSpec as P

HD = 64
EPS = 1e-05
CORE = [(0, 1), (1, 0), (2, 3), (3, 2)]
CHIP = [(0, 2), (2, 0), (1, 3), (3, 1)]
BOTH = [(0, 3), (3, 0), (1, 2), (2, 1)]
F32, BF = jnp.float32, jnp.bfloat16
SIDE = 32


def dot(a, b, contract):
    return lax.dot_general(a, b, (contract, ((), ())), preferred_element_type=F32)


def grouped(a):
    frames, few, part = a.shape
    a = a.astype(F32).reshape(frames, few // 8, 8, part)
    return jnp.concatenate([a[:, i].reshape(frames * 8, part) for i in range(few // 8)])


def attention(q, k, v, g, heads, scale):
    rows, cols = q.shape
    same = (
        lax.broadcasted_iota(jnp.int32, (rows, rows), 0) % 8
        == lax.broadcasted_iota(jnp.int32, (rows, rows), 1) % 8
    )
    lane = lax.broadcasted_iota(jnp.int32, (rows, cols), 1) // HD
    zero = jnp.zeros((rows, cols), BF)
    q_heads, k_heads, v_heads, g_heads = [
        [jnp.where(lane == h, a, zero) for h in range(heads)] for a in (q, k, v, g)
    ]
    g_scaled = (g.astype(F32) * scale).astype(BF)
    lows, dss = [], []
    for h in range(heads):
        scores = dot(q, k_heads[h], ((1,), (1,))) * (scale * math.log2(math.e))
        expd = jnp.exp2(jnp.where(same, scores, -1e30))
        prob = expd * (1.0 / jnp.sum(expd, axis=-1, keepdims=True))
        low = prob.astype(BF)
        dprob = dot(g_scaled, v_heads[h], ((1,), (1,)))
        delta = jnp.sum(low.astype(F32) * dprob, axis=-1, keepdims=True)
        lows.append(low)
        dss.append((prob * (dprob - delta)).astype(BF))

    def joined(parts, axis):
        return jnp.concatenate(parts, axis=axis)

    sums = (
        dot(joined(lows, 1), joined(v_heads, 0), ((1,), (0,))),
        dot(joined(dss, 1), joined(k_heads, 0), ((1,), (0,))),
        dot(joined(dss, 0), joined(q_heads, 0), ((0,), (0,))),
        dot(joined(lows, 0), joined(g_heads, 0), ((0,), (0,))),
    )
    return [a.astype(BF) for a in sums]


def split(a):
    high = a.astype(BF).astype(F32)
    return high, a - high


def main_kernel(
    heads, gain, own, near, far, cross, w, w_out,
    dw_at, send_at, keep, stats, far_gain, cross_gain,
    dw, send, gqkv, xhat, normed, dy, attn, left,
):
    t = lax.axis_index("tensor")
    rows, part = normed.shape[1:]
    width = 4 * part
    pieces = (own, near, far, cross)
    x = [grouped(a[:, 0]) for a in pieces]
    mean = sum(jnp.sum(a, axis=-1, keepdims=True) for a in x) / width
    x = [a - mean for a in x]
    inv = lax.rsqrt(sum(jnp.sum(a * a, axis=-1, keepdims=True) for a in x) / width + EPS)
    for i in range(4):
        xhat[i] = x[i] * inv
        normed[i] = (xhat[i] * gain[t ^ i]).astype(BF)
    order = [t ^ i for i in range(4)]
    wide_normed = jnp.concatenate([normed[i] for i in range(4)], axis=1)
    qkv = [
        dot(wide_normed, jnp.concatenate([w[s, j] for j in order]), ((1,), (0,))).astype(BF)
        for s in range(3)
    ]
    for i in range(4):
        dy[i] = grouped(pieces[i][:, 1]).astype(BF)
    wide_dy = jnp.concatenate([dy[i] for i in range(4)], axis=1)
    places = [pl.ds(pl.multiple_of(j * part, part), part) for j in order]
    wide_out = jnp.concatenate([w_out[:, place] for place in places], axis=1)
    g = dot(wide_dy, wide_out, ((1,), (1,))).astype(BF)
    half, cols = rows // 2, w.shape[3]
    for i in range(2):
        span = slice(i * half, (i + 1) * half)
        parts = attention(*(a[span] for a in qkv), g[span], heads, HD ** (-0.5))
        attn[span] = parts[0]
        for s in range(3):
            gqkv[span, s * cols : (s + 1) * cols] = parts[1 + s]
    first = jnp.zeros((rows, 1), F32)
    second = jnp.zeros((rows, 1), F32)
    outs = (keep.at[0], send.at[0], keep.at[1], send.at[1])
    gains = []
    for i in range(4):
        weights = jnp.concatenate([w[s, order[i]] for s in range(3)], axis=1)
        term = dot(gqkv[...], weights, ((1,), (1,))).astype(BF)
        outs[i][:rows] = term
        wide = term.astype(F32)
        product = wide * xhat[i]
        gains.append(jnp.sum(product, axis=0, keepdims=True))
        first += jnp.sum(wide * gain[t ^ i], axis=-1, keepdims=True)
        second += jnp.sum(product * gain[t ^ i], axis=-1, keepdims=True)
    for ref, line in ((far_gain, gains[2]), (cross_gain, gains[3])):
        ref[0:1] = line[:, :128]
        ref[1:2] = line[:, 128:]
    lane = lax.broadcasted_iota(jnp.int32, (rows, 128), 1)
    moments = jnp.where(lane == 0, first / width, jnp.where(lane == 1, second / width, 0.0))
    moments = jnp.where(lane == 8, mean, jnp.where(lane == 9, inv, moments)).T
    stats[...] = moments[8:16]
    high, low = split(moments[:8])
    line = lax.broadcasted_iota(jnp.int32, (8, part), 0)
    for i in range(4):
        gain_high, gain_low = split(gains[i])
        top = jnp.where(line == 2, gain_high, jnp.where(line == 3, gain_low, high[:, :part]))
        side = [top, high[:, part:], low[:, :part], low[:, part:]]
        outs[i][rows:] = jnp.concatenate(side).astype(BF)
    copies = [pltpu.make_async_copy(send, send_at, left.at[4])]
    copies[0].start()
    for i in range(4):
        dw[i, :, : 3 * cols] = dot(normed[i], gqkv[...], ((0,), (0,))).astype(BF)
        dw[i, :, 3 * cols :] = dot(dy[i], attn[...], ((0,), (0,))).astype(BF)
        copies.append(pltpu.make_async_copy(dw.at[i], dw_at.at[t ^ i], left.at[i]))
        copies[-1].start()
    for copy in copies:
        copy.wait()


def acts_kernel(keep, got, last, stats, own, gain, out):
    t = lax.axis_index("tensor")
    frames, part = own.shape[0], own.shape[3]
    rows = stats.shape[1]
    total = keep[0].astype(F32) + got[0].astype(F32) + last[...].astype(F32)
    side = total[rows:]
    moments = jnp.concatenate([side[:8] + side[16:24], side[8:16] + side[24:]], axis=1)
    moments = jnp.concatenate([moments, stats[...], jnp.zeros((112, rows), F32)]).T
    first, second, mean, inv = [moments[:, i : i + 1] for i in (0, 1, 8, 9)]
    xhat = (grouped(own[:, 0]) - mean) * inv
    grad = grouped(own[:, 1]) + inv * (total[:rows] * gain[t] - first - xhat * second)
    half = frames * 8
    for i in range(2):
        block = grad[i * half : (i + 1) * half].reshape(frames, 8, part)
        out[:, :, i * part : (i + 1) * part] = block.astype(BF)


def pack_kernel(dw, grad, gain, first, second, third, out):
    group, share, cols = out.shape[0], out.shape[1], dw.shape[2]
    block = sum(dw[i].astype(F32) for i in range(dw.shape[0]))
    out[:, :, :cols] = block.reshape(group, share, cols).astype(BF)
    end = cols + grad.shape[2]
    out[:, :, cols:end] = grad[...]
    high, low = split(gain[...] + first[...] + second[...] + third[...])
    ride = jnp.concatenate([high, low, high, low])
    out[:, :, end:] = jnp.broadcast_to(ride[None], (group, share, 128)).astype(BF)


def last_kernel(norm, came, out, dw, dw_out, gain):
    frames = came.shape[0]
    part = out.shape[1]
    for s in range(3):
        dw[s] = jnp.sum(came[:, :, s * part : (s + 1) * part].astype(F32), axis=0) * norm
    dw_out[...] = jnp.sum(came[:, :, 3 * part : 4 * part].astype(F32), axis=0) * norm
    grad = [came[:, :, i * part : (i + 1) * part].astype(F32) for i in (4, 5)]
    out[...] = jnp.concatenate(grad, axis=1).reshape(out.shape).astype(BF)
    ride = jnp.sum(came[:, :, 6 * part :].astype(F32), axis=0)
    gain[...] = (ride[0:2] + ride[2:4]) * norm


def call(kernel, args, outs, scratch=(), flops=0, mib=8, copied=0):
    vmem, hbm = [pl.BlockSpec(memory_space=a) for a in (pltpu.VMEM, pltpu.HBM)]
    shapes = [
        pltpu.HBM(s, d) if i < copied else jax.ShapeDtypeStruct(s, d)
        for i, (s, d) in enumerate(outs)
    ]
    moved = sum(math.prod(a.shape) * a.dtype.itemsize for a in list(args) + shapes)
    return pl.pallas_call(
        kernel,
        out_shape=shapes,
        in_specs=[vmem] * len(args),
        out_specs=[hbm] * copied + [vmem] * (len(outs) - copied),
        scratch_shapes=list(scratch),
        compiler_params=pltpu.CompilerParams(vmem_limit_bytes=mib * 2**20),
        cost_estimate=pl.CostEstimate(flops=flops, bytes_accessed=moved, transcendentals=0),
    )(*args)


def mid_kernel(keep, got, far, cross, mid, gain):
    mid[...] = (keep[1].astype(F32) + got[1].astype(F32)).astype(BF)
    rows = keep.shape[1] - SIDE
    side = keep[0, rows:].astype(F32) + got[0, rows:].astype(F32)
    line = side[2:3] + side[3:4]
    gain[0:1] = line[:, :128] + far[0:1] + cross[0:1]
    gain[1:2] = line[:, 128:] + far[1:2] + cross[1:2]


def per_device(acts, grad_in, gain, w_qkv, w_out):
    dp, tm = lax.axis_size("dp"), lax.axis_size("tm")
    part = acts.shape[3]
    rows = acts.shape[2]
    few = rows // tm
    width = w_qkv.shape[0]
    cols = w_qkv.shape[2]
    heads = cols // HD
    norm = (rows * dp * tm) ** (-0.5)

    own = jnp.stack([acts.reshape(tm, few, part), grad_in.reshape(tm, few, part)], axis=1)
    own = lax.all_to_all(own, "tm", split_axis=0, concat_axis=0, tiled=True)
    far = lax.ppermute(own, "tensor", CHIP)
    near = lax.ppermute(own, "tensor", CORE)
    cross = lax.ppermute(far, "tensor", CORE)

    gain_rows = gain.reshape(4, 1, part)
    w = jnp.transpose(w_qkv, (1, 0, 2)).reshape(3, 4, part, cols)
    message = ((2, rows + SIDE, part), BF)
    dw, send, keep, stats, far_gain, cross_gain = call(
        functools.partial(main_kernel, heads),
        (gain_rows, own, near, far, cross, w, w_out),
        (
            ((4, part, 4 * cols), BF),
            message,
            message,
            ((8, rows), F32),
            ((2, 128), F32),
            ((2, 128), F32),
        ),
        (
            pltpu.VMEM((4, part, 4 * cols), BF),
            pltpu.VMEM((2, rows + SIDE, part), BF),
            pltpu.VMEM((rows, 3 * cols), BF),
            pltpu.VMEM((4, rows, part), F32),
            pltpu.VMEM((4, rows, part), BF),
            pltpu.VMEM((4, rows, part), BF),
            pltpu.VMEM((rows, cols), BF),
            pltpu.SemaphoreType.DMA((5,)),
        ),
        flops=7 * 10**9,
        mib=36,
        copied=2,
    )

    dw = dw.reshape(dp, width // dp, 4 * cols)
    dw = lax.all_to_all(dw, "dp", split_axis=0, concat_axis=0, tiled=True)

    far_gain = lax.ppermute(far_gain, "tensor", CHIP)
    cross_gain = lax.ppermute(cross_gain, "tensor", BOTH)
    got = lax.ppermute(send, "tensor", CORE)
    mid, gain_sum = call(
        mid_kernel,
        (keep, got, far_gain, cross_gain),
        (((rows + SIDE, part), BF), ((2, 128), F32)),
        flops=1000,
    )
    last = lax.ppermute(mid, "tensor", CHIP)
    gain_sums = [gain_sum] + [
        lax.ppermute(gain_sum, "dp", [(i, i ^ bit) for i in range(dp)]) for bit in (2, 1, 3)
    ]
    (grad,) = call(
        acts_kernel,
        (keep, got, last, stats, own, gain_rows),
        (((tm, 8, 2 * part), BF),),
        flops=10**6,
    )

    share = width // (dp * tm)
    total = 4 * cols + 2 * part + 128
    group = tm // 4
    pack = pl.pallas_call(
        pack_kernel,
        grid=(tm // group,),
        out_shape=jax.ShapeDtypeStruct((tm, share, total), BF),
        in_specs=[
            pl.BlockSpec((dp, group * share, 4 * cols), lambda i: (0, i, 0)),
            pl.BlockSpec((group, share, 2 * part), lambda i: (i, 0, 0)),
        ]
        + [pl.BlockSpec((2, 128), lambda i: (0, 0))] * 4,
        out_specs=pl.BlockSpec((group, share, total), lambda i: (i, 0, 0)),
        compiler_params=pltpu.CompilerParams(vmem_limit_bytes=8 * 2**20),
        cost_estimate=pl.CostEstimate(flops=10**6, bytes_accessed=10**6, transcendentals=0),
    )(dw, grad, *gain_sums)
    pack = lax.all_to_all(pack, "tm", split_axis=0, concat_axis=0, tiled=True)
    out, dw, dw_out, gain_sum = call(
        functools.partial(last_kernel, norm),
        (pack,),
        (((rows, part), BF), ((3, share, cols), F32), ((share, cols), F32), ((2, 128), F32)),
        flops=10**7,
    )
    return (
        out.reshape(grad_in.shape),
        jnp.transpose(dw, (1, 0, 2)),
        dw_out,
        gain_sum.reshape(part),
    )


def solution(mesh):
    placed = (
        P("dp", "tm", None, "tensor"),
        P("dp", "tm", None, "tensor"),
        P(),
        P(None, None, "tensor"),
        P("tensor", None),
    )
    return jax.shard_map(
        per_device,
        mesh=mesh,
        in_specs=placed,
        out_specs=(
            P("dp", "tm", None, "tensor"),
            P(("dp", "tm"), None, "tensor"),
            P(("dp", "tm"), "tensor"),
            P("tensor"),
        ),
        check_vma=False,
    )
```
